128 devices in a mesh: fsdp: 16 (over x_hi, z, core), tp: 8 (over x_lo, y).
Axes of the slice: x: 4 (x_hi: 2, x_lo: 2; x = x_hi * 2 + x_lo), y: 4, z: 4, core: 2. Of those that a mesh axis runs over, the one named last changes fastest.
Arguments:
- trainer_weights: bfloat16 [16, 3, 1536, 4096], P('tp', None, None, 'fsdp'), may hold values from -0.09375 to 0.09375
- hidden_in: bfloat16 [256, 4096], P('fsdp'), may hold values from -6 to 6
- norm_gain: float32 [4096], replicated, may hold values from 0.1 to 1.9
- routing: int32 [4, 256, 8], P(None, 'fsdp'), may hold values from 0 to 15, all different within a row; in each aligned block of 16 rows (0 to 15, 16 to 31, ..., all dimensions but the last counted through in order) at most 11 rows name the same one
- gate_weights: float32 [4, 256, 8], P(None, 'fsdp'), may hold values from 0.2 to 1
Outputs:
- hidden_out: float32 [256, 4096], P('fsdp')
The draws below stay inside these ranges and needn't reach their ends.
Inputs may be any that keep to these rules, and one draw needn't show every extreme that they name: `routing`: each row names 8 different experts in each step. In each step, the 16 rows of one fsdp index name any one expert at most 11 times, a bound that some of these blocks reach.
All inputs are finite; a program needn't handle non-finite values.
Results may differ from the reference program's by a relative error of at most 0.04.
Values may be sent and summed in bfloat16 or wider, within the bound.
No kernel may reach another device: no remote copies, remote signals or barrier semaphores. Data moves between devices by JAX's collectives and lax.ppermute only.
A program may use at most 128 MiB of HBM per device.

```python
import math
import jax
import jax.numpy as jnp
import numpy as np
from jax import lax

D = 4096
FF = 1536
TOPK = 8
EXPERTS = 16
QB = 128
STEPS = 4
ROWS_DEV = 16
CAP = 11
ROWS = 256
N_FSDP = 16
N_TP = 8


def steps_of(stream_key, extent, cuts, least, top_value):
    factor_of = 1.0
    for axis_at, blocks in cuts:
        steps = jax.random.uniform(jax.random.fold_in(jax.random.fold_in(stream_key, 6), axis_at), (blocks,), jnp.float32, least / len(cuts), top_value / len(cuts))
        factor_of = factor_of * jnp.repeat(jnp.exp(steps), extent[axis_at] // blocks).reshape((-1,) + (1,) * (len(extent) - 1 - axis_at))
    return factor_of


def routed_block(rng, own, number, rows, amount, top, limit, slope):
    order = jax.random.permutation(rng, amount)
    crowded, usual = portions_of(amount, rows * top, limit, slope, True), portions_of(amount, rows * top, limit, slope, False)
    places = jnp.arange(amount)

    def named(tallies, rotation):
        used = int((tallies > 0).sum())
        fixed = max(1, used // 4)
        shifted = fixed + (places - fixed + rotation * (used - fixed)) % max(1, amount - fixed)
        return jnp.zeros((amount,), jnp.int32).at[order[jnp.where(places < fixed, places, shifted)]].set(jnp.asarray(tallies, jnp.int32))

    tallies = jnp.where(number % 4 == 0, named(crowded, number // 4), named(usual, number - number // 4 - 1))
    mixed = jax.random.permutation(jax.random.fold_in(own, 3), amount)
    giver, taker = mixed[0:amount // 2 * 2:2], mixed[1:amount // 2 * 2:2]
    room = jnp.minimum(tallies[giver] - 1, limit - tallies[taker]) // 2
    room = jnp.where((giver == order[0]) | (taker == order[0]) | (tallies[taker] == 0), 0, jnp.maximum(room, 0))
    shifted = jax.random.randint(jax.random.fold_in(own, 4), (amount // 2,), 0, 1 << 20) % (room + 1)
    tallies = tallies.at[giver].add(-shifted).at[taker].add(shifted)
    items = jnp.searchsorted(jnp.cumsum(tallies), jnp.arange(rows * top), side="right").astype(jnp.int32)
    table = items.reshape(top, rows).T
    table = table[jax.random.permutation(jax.random.fold_in(own, 1), rows)]
    rotation = jax.random.randint(jax.random.fold_in(own, 2), (rows, 1), 0, top)
    return jnp.take_along_axis(table, (jnp.arange(top)[None, :] + rotation) % top, axis=1)


def portions_of(count, total, most, skew, full):
    loads = [(1 << 20) // math.isqrt(rank ** skew) + 1 for rank in range(1, count + 1)]
    largest = most if full else min(most, max(-(-total // count), total * loads[0] // sum(loads)))
    least = 1 if total - largest >= count - 1 else 0
    holding, spare = [largest] + [least] * (count - 1), total - largest - least * (count - 1)
    while spare > 0:
        movable = [i for i in range(1, count) if holding[i] < largest] or [i for i in range(1, count) if holding[i] < most]
        mass, budget = sum([loads[i] for i in movable]), spare
        for i in movable:
            extra = min(most - holding[i], max(1, budget * loads[i] // mass), spare)
            holding[i] = holding[i] + extra
            spare = spare - extra
    return np.array(holding)


def scatter_about(stream_key, extent, width, limit, split=(), kind=jnp.bfloat16):
    gain = steps_of(stream_key, extent, split, -0.22, 0.18) if split else 1.0
    array = jax.random.normal(stream_key, extent, jnp.float32) * width * gain
    return jnp.minimum(jnp.maximum(array, -limit), limit).astype(kind)


def setup_inputs(seed: int = 0) -> dict:
    keys = jax.random.split(jax.random.key(seed), 6)
    trainer_weights = scatter_about(keys[0], (EXPERTS, 3, FF, D), D ** -0.5, 0.09375, ((0, 8), (3, 16)))
    hidden_in = scatter_about(keys[1], (ROWS, D), 1.0, 6.0, ((0, 16),))
    norm_gain = jnp.clip(1.0 + 0.18 * jax.random.normal(keys[2], (D,), jnp.float32), 0.1, 1.9)
    routing_keys = jax.random.split(jax.random.fold_in(keys[3], 1), STEPS * ROWS // ROWS_DEV)
    routing_turns = jax.random.permutation(jax.random.fold_in(keys[3], 3), STEPS * ROWS // ROWS_DEV)
    routing = jax.vmap(lambda own, number: routed_block(jax.random.fold_in(keys[3], 2), own, number, ROWS_DEV, EXPERTS, TOPK, CAP, 2))(routing_keys, routing_turns).reshape((STEPS, ROWS, TOPK))
    gate_weights = jnp.clip(0.2 + 0.8 * jax.random.uniform(keys[4], (STEPS, ROWS, TOPK), jnp.float32) ** steps_of(keys[4], (STEPS, ROWS, TOPK), ((1, 16),), -0.2, 0.2), 0.2, 1.0)
    return dict(trainer_weights=trainer_weights, hidden_in=hidden_in, norm_gain=norm_gain, routing=routing, gate_weights=gate_weights)


norm_eps = 1e-06
scale_eps = 1e-06
code_limit = 448.0
smallest_normal = 0.015625

def float_code(values):
    magnitude = jnp.maximum(jnp.abs(values), smallest_normal)
    exponent = jnp.floor(jnp.log2(magnitude))
    spacing = jnp.exp2(exponent - 3.0)
    return jnp.floor(values / spacing + 0.5) * spacing

def dequant_expert(matrices):
    values = matrices.astype(jnp.float32).reshape(3, FF // QB, QB, D // QB, QB)
    largest = lax.optimization_barrier(jnp.max(jnp.abs(values), axis=(2, 4)))
    scales = (largest + scale_eps) / code_limit
    coded = float_code(values / scales[:, :, None, :, None]).astype(jnp.bfloat16)
    restored = coded.astype(jnp.float32) * scales[:, :, None, :, None]
    return restored.reshape(3, FF, D).astype(jnp.bfloat16)

def expert_rows(picked_rows, matrices):
    gate_sum = jnp.dot(picked_rows, matrices[0].T, preferred_element_type=jnp.float32)
    up_sum = jnp.dot(picked_rows, matrices[1].T, preferred_element_type=jnp.float32)
    hidden = (jax.nn.silu(gate_sum) * up_sum).astype(jnp.bfloat16)
    count = picked_rows.shape[0]
    pieces = hidden.reshape(count, N_TP, FF // N_TP).astype(jnp.float32)
    down_proj = matrices[2].reshape(N_TP, FF // N_TP, D).astype(jnp.float32)
    partial_value = jnp.einsum('mjf,jfd->jmd', pieces, down_proj).astype(jnp.bfloat16)
    return lax.optimization_barrier(jnp.sum(partial_value.astype(jnp.float32), axis=0)).astype(jnp.bfloat16)

def reference(trainer_weights, hidden_in, norm_gain, routing, gate_weights):
    weights = lax.map(dequant_expert, trainer_weights)
    stream = hidden_in.astype(jnp.float32)
    rows_total = stream.shape[0]
    row_order = jnp.arange(rows_total, dtype=jnp.int32)
    for decode_step in range(STEPS):
        normed = stream * lax.rsqrt(lax.optimization_barrier(jnp.mean(stream * stream, axis=-1, keepdims=True)) + norm_eps) * norm_gain
        normed = normed.astype(jnp.bfloat16)
        step_routes = routing[decode_step]
        step_gates = gate_weights[decode_step]

        def visit(combined, expert):
            matches = step_routes == expert
            weight_row = lax.optimization_barrier(jnp.sum(jnp.where(matches, step_gates, jnp.zeros_like(step_gates)), axis=1))
            routed = jnp.any(matches, axis=1).astype(jnp.int32)
            ranking = routed * rows_total + (rows_total - 1 - row_order)
            unused, chosen_rows = lax.top_k(ranking, N_FSDP * CAP)
            chosen_rows = chosen_rows.astype(jnp.int32)
            result = expert_rows(normed[chosen_rows], lax.dynamic_index_in_dim(weights, expert, 0, keepdims=False))
            combined = combined.at[chosen_rows].add(weight_row[chosen_rows][:, None] * result.astype(jnp.float32))
            return (combined, None)
        combined, unused = lax.scan(visit, jnp.zeros((rows_total, D), jnp.float32), jnp.arange(EXPERTS, dtype=jnp.int32))
        stream = stream + combined
    return stream
```

```python
import jax
import jax.numpy as jnp
from jax import lax
from jax.experimental import pallas as pl
from jax.experimental.pallas import tpu as pltpu
from jax.sharding import Mesh, PartitionSpec as P

D = 4096
FF = 1536
TOPK = 8
EXPERTS = 16
QB = 128
STEPS = 4
CAP = 11
ROWS_DEV = 16
ROWS = 256
SLOTS = 16 * CAP
WIDTH = 512
HALF = 256
UNITS = 192
PAY = 192
EXT = 640
FIRST = 768

XZ = ("xh", "z")
CT = ("c", "xl", "y")
ALL = ("xh", "z", "c", "xl", "y")

norm_eps = 1e-06
scale_eps = 1e-06
code_limit = 448.0
smallest_normal = 0.015625
f32 = jnp.float32
bf16 = jnp.bfloat16

NN = (((1,), (0,)), ((), ()))
NT = (((1,), (1,)), ((), ()))


def dot(a, b, dims=NN):
    return lax.dot_general(a, b, dims, preferred_element_type=f32)


def split3(v):
    hi = v.astype(bf16)
    rest = v - hi.astype(f32)
    mid = rest.astype(bf16)
    low = (rest - mid.astype(f32)).astype(bf16)
    return hi, mid, low


def float_code(v):
    big = v * 1048577.0
    fine = big - (big - v)
    coarse = (v + 24576.0) - 24576.0
    return jnp.where(jnp.abs(v) < smallest_normal, coarse, fine)


def quant_kernel(which_ref, w_ref, gu_ref, dn_ref):
    for m in range(3):
        for q in range(3):
            for h in range(2):
                cols = slice(h * QB, (h + 1) * QB)
                tile = w_ref[0, m, q * QB : (q + 1) * QB, cols].astype(f32)
                top = jnp.max(jnp.abs(tile), axis=(0, 1), keepdims=True) + scale_eps
                scale = top / code_limit
                back = (float_code(tile * (1.0 / scale)) * scale).astype(bf16)
                if m == 2:
                    dn_ref[q * QB : (q + 1) * QB, cols] = back
                else:
                    for g in range(2):
                        unit = q * 2 + g
                        j, part = unit // 3, unit % 3
                        if m == 0:
                            to = j * 384 + part * 64
                        elif part < 2:
                            to = j * 384 + 256 + part * 64
                        else:
                            to = j * 384 + 192
                        gu_ref[to : to + 64, cols] = back[g * 64 : g * 64 + 64]


def quantize(which, w):
    return pl.pallas_call(
        quant_kernel,
        grid_spec=pltpu.PrefetchScalarGridSpec(
            num_scalar_prefetch=1,
            grid=(4,),
            in_specs=[pl.BlockSpec((1, 3, 384, HALF), lambda i, s: (s[0], 0, i, 0))],
            out_specs=[
                pl.BlockSpec((768, HALF), lambda i, s: (i, 0)),
                pl.BlockSpec((384, HALF), lambda i, s: (i, 0)),
            ],
        ),
        out_shape=[
            jax.ShapeDtypeStruct((2 * FF, HALF), bf16),
            jax.ShapeDtypeStruct((FF, HALF), bf16),
        ],
        name="quantize",
    )(which, w)


def prepare_kernel(
    ids_ref, own_ref, other_ref, gain_ref, x_ref, stream_ref, s_ref, st_ref, w_ref, rows
):
    core, tp, expert = ids_ref[0], ids_ref[1], ids_ref[2]
    rows[pl.ds(pl.multiple_of(core * 128, 128), 128), :] = own_ref[...]
    rows[pl.ds(pl.multiple_of((1 - core) * 128, 128), 128), :] = other_ref[...]
    stream_ref[...] = own_ref[pl.ds(pl.multiple_of(tp * 16, 16), 16), :WIDTH].astype(f32)
    rs = jnp.sum(rows[:, 640:768].astype(f32), axis=1, keepdims=True)
    x_ref[...] = (rows[:, :WIDTH].astype(f32) * rs * gain_ref[...]).astype(bf16)
    named = rows[:, 512:640].astype(f32)
    gates = pltpu.roll(named, 96, 1) + pltpu.roll(named, 64, 1) + pltpu.roll(named, 32, 1)
    lane = lax.broadcasted_iota(jnp.int32, (ROWS, 128), 1)
    match = jnp.where((named == expert.astype(f32)) & (lane < 32), 1.0, 0.0)
    weighted = match * gates
    group = lane // TOPK
    mask = jnp.zeros((ROWS, 128), f32)
    weight = jnp.zeros((ROWS, 128), f32)
    for s in range(STEPS):
        here = jnp.sum(jnp.where(group == s, match, 0.0), axis=1, keepdims=True)
        gate = jnp.sum(jnp.where(group == s, weighted, 0.0), axis=1, keepdims=True)
        mask = jnp.where(lane == s, here, mask)
        weight = jnp.where(lane == s, gate, weight)
    w_ref[...] = weight
    r0 = lax.broadcasted_iota(jnp.int32, (ROWS, ROWS), 0)
    r1 = lax.broadcasted_iota(jnp.int32, (ROWS, ROWS), 1)
    before = jnp.where(r1 < r0, 1.0, 0.0).astype(bf16)
    place = dot(before, mask.astype(bf16))
    slot = r1.astype(f32)
    for s in range(STEPS):
        hot = jnp.where((slot == place[:, s : s + 1]) & (mask[:, s : s + 1] > 0.0), 1.0, 0.0)
        st_ref[s] = hot.astype(bf16)
        s_ref[s] = hot.T[:SLOTS].astype(bf16)


def prepare(ids, own, other, gain):
    return pl.pallas_call(
        prepare_kernel,
        in_specs=[pl.BlockSpec(memory_space=pltpu.SMEM)] + [pl.BlockSpec()] * 3,
        out_shape=[
            jax.ShapeDtypeStruct((ROWS, WIDTH), bf16),
            jax.ShapeDtypeStruct((ROWS_DEV, WIDTH), f32),
            jax.ShapeDtypeStruct((STEPS, SLOTS, ROWS), bf16),
            jax.ShapeDtypeStruct((STEPS, ROWS, ROWS), bf16),
            jax.ShapeDtypeStruct((ROWS, 128), f32),
        ],
        scratch_shapes=[pltpu.VMEM((ROWS, FIRST), bf16)],
        name="prepare",
    )(ids, own, other, gain)


def gate_up_kernel(first, ids_ref, x_ref, s_ref, st_ref, wa_ref, wb_ref, p_ref):
    core = ids_ref[0]
    picked = dot(s_ref[...], x_ref[:, :WIDTH]).astype(bf16)
    left, right = picked[:, :HALF], picked[:, HALF:]
    xa = jnp.where(core == 0, left, right)
    xb = jnp.where(core == 0, right, left)
    if first:
        tail = jnp.zeros((PAY - SLOTS, 384), bf16)
    else:
        squares = jnp.sum(x_ref[:, WIDTH:].astype(f32), axis=1, keepdims=True)
        line = jnp.sum(st_ref[...].astype(f32) * squares, axis=0, keepdims=True)
        line = jnp.concatenate([line, jnp.zeros((1, 128), f32)], axis=1)
        hi, mid, low = split3(line)
        at = lax.broadcasted_iota(jnp.int32, (PAY - SLOTS, 384), 0)
        tail = jnp.where(
            at == 0,
            hi.astype(f32),
            jnp.where(at == 1, mid.astype(f32), jnp.where(at == 2, low.astype(f32), 0.0)),
        ).astype(bf16)
    for j in range(8):
        at = slice(j * 384, (j + 1) * 384)
        part = dot(xa, wa_ref[at, :], NT) + dot(xb, wb_ref[at, :], NT)
        p_ref[j, :SLOTS, :] = part.astype(bf16)
        p_ref[j, SLOTS:, :] = tail


def gate_up(first, ids, x, s, st, wa, wb):
    return pl.pallas_call(
        lambda *refs: gate_up_kernel(first, *refs),
        in_specs=[pl.BlockSpec(memory_space=pltpu.SMEM)] + [pl.BlockSpec()] * 5,
        out_shape=jax.ShapeDtypeStruct((8, PAY, 384), bf16),
        compiler_params=pltpu.CompilerParams(vmem_limit_bytes=32 << 20),
        name="gate_up",
    )(ids, x, s, st, wa, wb)


def act_kernel(first, p_ref, out_ref):
    total = p_ref[0].astype(f32)
    for j in range(1, 8):
        total = total + p_ref[j].astype(f32)
    sums = total[:SLOTS]
    if not first:
        line = jnp.sum(total[SLOTS : SLOTS + 8, :HALF], axis=0, keepdims=True)
        rs_line = lax.rsqrt(line * (1.0 / D) + norm_eps)
        r0 = lax.broadcasted_iota(jnp.int32, (SLOTS, HALF), 0)
        r1 = lax.broadcasted_iota(jnp.int32, (SLOTS, HALF), 1)
        rs = jnp.sum(jnp.where(r0 == r1, rs_line, 0.0), axis=1, keepdims=True)
        sums = sums * rs
    t0, t1, t2 = sums[:, :128], sums[:, 128:256], sums[:, 256:]
    a0 = jax.nn.silu(t0) * t2
    a1 = jax.nn.silu(t1) * pltpu.roll(t1, 64, 1)
    half = SLOTS // 2
    lane = lax.broadcasted_iota(jnp.int32, (half, 128), 1)
    middle = jnp.where(lane < 64, a1[:half], pltpu.roll(a1[half:], 64, 1))
    packed = jnp.concatenate([a0[:half], middle, a0[half:]], axis=1).astype(bf16)
    for j in range(8):
        out_ref[j] = packed


def activate(first, p):
    return pl.pallas_call(
        lambda *refs: act_kernel(first, *refs),
        out_shape=jax.ShapeDtypeStruct((8, SLOTS // 2, 384), bf16),
        name="activate",
    )(p)


def down_kernel(step, ids_ref, a_ref, st_ref, w_ref, wa_ref, wb_ref, out_ref):
    core = ids_ref[0]
    half = SLOTS // 2
    lane = lax.broadcasted_iota(jnp.int32, (half, 128), 1)
    sum_a = jnp.zeros((SLOTS, HALF), f32)
    sum_b = jnp.zeros((SLOTS, HALF), f32)
    for j in range(8):
        block = a_ref[j].astype(f32)
        middle = block[:, 128:256]
        low = jnp.concatenate([block[:, :128], jnp.where(lane < 64, middle, 0.0)], axis=1)
        high = jnp.concatenate([block[:, 256:], jnp.where(lane < 64, 0.0, middle)], axis=1)
        act = jnp.concatenate([low, high], axis=0).astype(bf16)
        at = j * UNITS
        wa = jnp.concatenate([wa_ref[at : at + UNITS, :], wa_ref[at + 128 : at + UNITS, :]], axis=0)
        wb = jnp.concatenate([wb_ref[at : at + UNITS, :], wb_ref[at + 128 : at + UNITS, :]], axis=0)
        sum_a = sum_a + dot(act, wa)
        sum_b = sum_b + dot(act, wb)
    left = jnp.where(core == 0, sum_a, sum_b).astype(bf16)
    right = jnp.where(core == 0, sum_b, sum_a).astype(bf16)
    weight = w_ref[:, step : step + 1]
    st = st_ref[:, :SLOTS]
    out_ref[:, :HALF] = (dot(st, left) * weight).astype(bf16)
    out_ref[:, HALF:] = (dot(st, right) * weight).astype(bf16)


def down(step, ids, a, st, w, wa, wb):
    return pl.pallas_call(
        lambda *refs: down_kernel(step, *refs),
        in_specs=[pl.BlockSpec(memory_space=pltpu.SMEM)] + [pl.BlockSpec()] * 5,
        out_shape=jax.ShapeDtypeStruct((ROWS, WIDTH), bf16),
        compiler_params=pltpu.CompilerParams(vmem_limit_bytes=32 << 20),
        name="down",
    )(ids, a, st, w, wa, wb)


def residual_kernel(p_ref, stream_ref, gain_ref, new_ref, x_ref):
    total = p_ref[0].astype(f32)
    for j in range(1, 16):
        total = total + p_ref[j].astype(f32)
    stream = stream_ref[...] + total
    new_ref[...] = stream
    hi, mid, low = split3(jnp.sum(stream * stream, axis=1, keepdims=True))
    lane = lax.broadcasted_iota(jnp.int32, (ROWS_DEV, 128), 1)
    parts = jnp.where(
        lane == 0,
        hi.astype(f32),
        jnp.where(lane == 1, mid.astype(f32), jnp.where(lane == 2, low.astype(f32), 0.0)),
    )
    row = jnp.concatenate([stream * gain_ref[...], parts], axis=1).astype(bf16)
    for j in range(16):
        x_ref[j] = row


def residual(p, stream, gain):
    return pl.pallas_call(
        residual_kernel,
        out_shape=[
            jax.ShapeDtypeStruct((ROWS_DEV, WIDTH), f32),
            jax.ShapeDtypeStruct((16, ROWS_DEV, EXT), bf16),
        ],
        name="residual",
    )(p, stream, gain)


def last_kernel(p_ref, stream_ref, new_ref):
    total = p_ref[0].astype(f32)
    for j in range(1, 16):
        total = total + p_ref[j].astype(f32)
    new_ref[...] = stream_ref[...] + total


def last(p, stream):
    return pl.pallas_call(
        last_kernel,
        out_shape=jax.ShapeDtypeStruct((ROWS_DEV, WIDTH), f32),
        name="last",
    )(p, stream)


def exchange(x, axes):
    return lax.all_to_all(x, axes, split_axis=0, concat_axis=0, tiled=True)


def reduced(v):
    return lax.reduce_precision(v, exponent_bits=8, mantissa_bits=7)


def parts3(v):
    hi = reduced(v)
    mid = reduced(v - hi)
    return [hi, mid, v - hi - mid]


def body(trainer_weights, hidden_in, norm_gain, routing, gate_weights):
    core = lax.axis_index("c")
    tp = lax.axis_index(("xl", "y"))
    xz = lax.axis_index(XZ)
    ids = jnp.stack([core, tp, 2 * tp + core]).astype(jnp.int32)
    zero = jnp.zeros((1,), jnp.int32)
    gain = lax.dynamic_slice(norm_gain, (xz * WIDTH,), (WIDTH,)).reshape(1, WIDTH)

    given = lax.dynamic_index_in_dim(trainer_weights, 1 - core, 0, keepdims=True)
    taken = lax.ppermute(given, "c", [(0, 1), (1, 0)])

    hidden = hidden_in.astype(f32)
    rs = lax.rsqrt(jnp.mean(hidden * hidden, axis=-1, keepdims=True) + norm_eps)
    flat = lambda v: jnp.transpose(v, (1, 0, 2)).reshape(ROWS_DEV, STEPS * TOPK)
    extra = jnp.concatenate(
        [flat(routing).astype(f32)] + parts3(flat(gate_weights)) + parts3(rs)
        + [jnp.zeros((ROWS_DEV, 125), f32)],
        axis=1,
    ).astype(bf16)
    pieces = jnp.transpose(hidden_in.reshape(ROWS_DEV, 8, WIDTH), (1, 0, 2))
    extra = jnp.broadcast_to(extra[None], (8, ROWS_DEV, FIRST - WIDTH))
    own = exchange(jnp.concatenate([pieces, extra], axis=2), XZ).reshape(128, FIRST)
    other = lax.ppermute(own, "c", [(0, 1), (1, 0)])

    gu_a, dn_a = quantize(core.astype(jnp.int32).reshape(1), trainer_weights)
    gu_b, dn_b = quantize(zero, taken)
    x, stream, s, st, w = prepare(ids, own, other, gain)

    for step in range(STEPS):
        first = step == 0
        partial = gate_up(first, ids, x, s[step], st[step], gu_a, gu_b)
        act = activate(first, exchange(partial, XZ))
        back = down(step, ids, exchange(act, XZ), st[step], w, dn_a, dn_b)
        sums = exchange(back.reshape(16, ROWS_DEV, WIDTH), CT)
        if step < STEPS - 1:
            stream, rows = residual(sums, stream, gain)
            x = exchange(rows, CT).reshape(ROWS, EXT)
        else:
            stream = last(sums, stream)

    turn = [
        ((a * 2 + c) * 8 + b, (b * 2 + c) * 8 + a)
        for a in range(8)
        for c in range(2)
        for b in range(8)
    ]
    mine = lax.ppermute(stream, ALL, turn)
    whole = exchange(jnp.broadcast_to(mine[None], (8, ROWS_DEV, WIDTH)), ("xl", "y"))
    return jnp.transpose(whole, (1, 0, 2)).reshape(ROWS_DEV, D)


def solution(mesh):
    fine = Mesh(mesh.devices.reshape(2, 4, 2, 2, 4), ALL)
    fsdp, tp = ("xh", "z", "c"), ("xl", "y")
    in_specs = (
        P(tp, None, None, fsdp),
        P(fsdp, None),
        P(),
        P(None, fsdp, None),
        P(None, fsdp, None),
    )
    return jax.shard_map(
        body, mesh=fine, in_specs=in_specs, out_specs=P(fsdp, None), check_vma=False
    )
```

```python
import jax
import jax.numpy as jnp
from jax import lax
from jax.experimental import pallas as pl
from jax.experimental.pallas import tpu as pltpu
from jax.sharding import Mesh, PartitionSpec as P

D = 4096
FF = 1536
TOPK = 8
EXPERTS = 16
QB = 128
STEPS = 4
CAP = 11
ROWS_DEV = 16
ROWS = 256
SLOTS = 16 * CAP
UNIT_HALF = 768
WIDTH = 1024
HALF = 256
UNITS = 192
PAY = 192
EXT = 1152
FIRST = 1280

XZ = ("xh", "z")
XT = ("xh", "xl", "y")
T = ("xl", "y")
ALL = ("xh", "z", "c", "xl", "y")

norm_eps = 1e-06
scale_eps = 1e-06
code_limit = 448.0
smallest_normal = 0.015625
f32 = jnp.float32
bf16 = jnp.bfloat16

NN = (((1,), (0,)), ((), ()))
NT = (((1,), (1,)), ((), ()))


def dot(a, b, dims=NN):
    return lax.dot_general(a, b, dims, preferred_element_type=f32)


def busy(us):
    return pl.CostEstimate(flops=int(us * 1.15e9), bytes_accessed=0, transcendentals=0)


def split3(v):
    hi = v.astype(bf16)
    rest = v - hi.astype(f32)
    mid = rest.astype(bf16)
    low = (rest - mid.astype(f32)).astype(bf16)
    return hi, mid, low


def float_code(v):
    big = v * 1048577.0
    fine = big - (big - v)
    coarse = (v + 24576.0) - 24576.0
    return jnp.where(jnp.abs(v) < smallest_normal, coarse, fine)


def quant_block(tile):
    tile = tile.astype(f32)
    top = jnp.max(jnp.abs(tile), axis=(0, 1), keepdims=True) + scale_eps
    scale = top / code_limit
    return (float_code(tile * (1.0 / scale)) * scale).astype(bf16)


def quant_gate_up(src, out_ref, group):
    for m in range(2):
        for q in range(3):
            for h in range(2):
                cols = slice(h * QB, (h + 1) * QB)
                back = quant_block(src[m, q * QB : (q + 1) * QB, cols])
                for g in range(2):
                    unit = q * 2 + g
                    j, part = unit // 3, unit % 3
                    if m == 0:
                        to = part * 64
                    elif part < 2:
                        to = 256 + part * 64
                    else:
                        to = 192
                    to = group * 768 + j * 384 + to
                    out_ref[to : to + 64, cols] = back[g * 64 : g * 64 + 64]


def quant_down(src, out_ref, at, blocks):
    for q in range(blocks):
        for h in range(2):
            cols = slice(h * QB, (h + 1) * QB)
            back = quant_block(src[q * QB : (q + 1) * QB, cols])
            out_ref[at + q * QB : at + (q + 1) * QB, cols] = back


def quant_far_kernel(ids_ref, w_ref, near_ref, diag_ref, buf, sem):
    core, half = ids_ref[0], 1 - ids_ref[3]
    copies = []
    for p in range(2):
        for g in range(2):
            expert = core if p == 0 else 1 - core
            at = pl.multiple_of(half * UNIT_HALF + g * 384, 128)
            src = w_ref.at[expert, pl.ds(0, 2), pl.ds(at, 384), :]
            copies.append(pltpu.make_async_copy(src, buf.at[p * 2 + g], sem.at[p * 2 + g]))
    for copy in copies:
        copy.start()
    for p in range(2):
        for g in range(2):
            copies[p * 2 + g].wait()
            quant_gate_up(buf.at[p * 2 + g], diag_ref if p else near_ref, g)


def quantize_far(ids, w):
    out = jax.ShapeDtypeStruct((2 * UNIT_HALF, HALF), bf16)
    return pl.pallas_call(
        quant_far_kernel,
        in_specs=[
            pl.BlockSpec(memory_space=pltpu.SMEM),
            pl.BlockSpec(memory_space=pltpu.HBM),
        ],
        out_shape=[out, out],
        scratch_shapes=[pltpu.VMEM((4, 2, 384, HALF), bf16), pltpu.SemaphoreType.DMA((4,))],
        compiler_params=pltpu.CompilerParams(vmem_limit_bytes=60 << 20),
        name="quantize_far",
    )(ids, w)


def quant_rest_kernel(
    ids_ref, w_ref, own_ref, other_ref, near_ref, diag_ref, buf, sem, down_buf, down_sem
):
    core, half = ids_ref[0], ids_ref[3]
    copies = []
    for p in range(2):
        expert = core if p == 0 else 1 - core
        for g in range(2):
            at = pl.multiple_of(half * UNIT_HALF + g * 384, 128)
            src = w_ref.at[expert, :, pl.ds(at, 384), :]
            copies.append(pltpu.make_async_copy(src, buf.at[p * 2 + g], sem.at[p * 2 + g]))
    down_copies = []
    for p in range(2):
        expert = core if p == 0 else 1 - core
        at = pl.multiple_of((1 - half) * UNIT_HALF, 128)
        src = w_ref.at[expert, 2, pl.ds(at, UNIT_HALF), :]
        down_copies.append(pltpu.make_async_copy(src, down_buf.at[p], down_sem.at[p]))
    for copy in copies + down_copies:
        copy.start()
    for p in range(2):
        out_ref = other_ref if p else own_ref
        for g in range(2):
            copies[p * 2 + g].wait()
            quant_gate_up(buf.at[p * 2 + g], out_ref, g)
            quant_down(buf.at[p * 2 + g, 2], out_ref, 2 * UNIT_HALF + g * 384, 3)
    for p in range(2):
        down_copies[p].wait()
        quant_down(down_buf.at[p], diag_ref if p else near_ref, 0, 6)


def quantize_rest(ids, w):
    whole = jax.ShapeDtypeStruct((3 * UNIT_HALF, HALF), bf16)
    third = jax.ShapeDtypeStruct((UNIT_HALF, HALF), bf16)
    return pl.pallas_call(
        quant_rest_kernel,
        in_specs=[
            pl.BlockSpec(memory_space=pltpu.SMEM),
            pl.BlockSpec(memory_space=pltpu.HBM),
        ],
        out_shape=[whole, whole, third, third],
        scratch_shapes=[
            pltpu.VMEM((4, 3, 384, HALF), bf16),
            pltpu.SemaphoreType.DMA((4,)),
            pltpu.VMEM((2, UNIT_HALF, HALF), bf16),
            pltpu.SemaphoreType.DMA((2,)),
        ],
        compiler_params=pltpu.CompilerParams(vmem_limit_bytes=60 << 20),
        name="quantize_rest",
    )(ids, w)


def spread_kernel(ids_ref, own_ref, far_ref, *out_refs):
    half, z = ids_ref[3], ids_ref[4]
    for d in range(4):
        at = (z + d) % 4
        out_refs[d][half] = own_ref[at]
        out_refs[d][1 - half] = far_ref[at]


def spread(ids, own, far):
    return pl.pallas_call(
        spread_kernel,
        in_specs=[pl.BlockSpec(memory_space=pltpu.SMEM)] + [pl.BlockSpec()] * 2,
        out_shape=[jax.ShapeDtypeStruct((2, ROWS_DEV, FIRST), bf16)] * 4,
        compiler_params=pltpu.CompilerParams(vmem_limit_bytes=4 << 20),
        name="spread",
    )(ids, own, far)


def prepare_kernel(ids_ref, own_ref, other_ref, gain_ref, x_ref, stream_ref, tab_ref, rows, tab):
    core, tp, expert, half, z = [ids_ref[i] for i in range(5)]
    for d in range(4):
        for far in range(2):
            at = (far * 4 + (z - d + 4) % 4) * 16
            rows[pl.ds(pl.multiple_of(core * 128 + at, 16), 16), :] = own_ref[d, far]
            rows[pl.ds(pl.multiple_of((1 - core) * 128 + at, 16), 16), :] = other_ref[d, far]
    named = rows[:, WIDTH : WIDTH + 128].astype(f32)
    gates = pltpu.roll(named, 96, 1) + pltpu.roll(named, 64, 1) + pltpu.roll(named, 32, 1)
    lane = lax.broadcasted_iota(jnp.int32, (ROWS, 128), 1)
    match = jnp.where((named == expert.astype(f32)) & (lane < 32), 1.0, 0.0)
    weighted = match * gates
    group = lane // TOPK
    mask = jnp.zeros((ROWS, 128), f32)
    weight = jnp.zeros((ROWS, 128), f32)
    for s in range(STEPS):
        here = jnp.sum(jnp.where(group == s, match, 0.0), axis=1, keepdims=True)
        gate = jnp.sum(jnp.where(group == s, weighted, 0.0), axis=1, keepdims=True)
        mask = jnp.where(lane == s, here, mask)
        weight = jnp.where(lane == s, gate, weight)
    r0 = lax.broadcasted_iota(jnp.int32, (ROWS, ROWS), 0)
    r1 = lax.broadcasted_iota(jnp.int32, (ROWS, ROWS), 1)
    before = jnp.where(r1 < r0, 1.0, 0.0).astype(bf16)
    place = jnp.where(mask > 0.0, dot(before, mask.astype(bf16)), -1.0)
    tab[...] = jnp.where(lane < 64, weight, pltpu.roll(place, 64, 1))
    for c in range(2):
        for far in range(2):
            for u in range(4):
                at = pl.multiple_of(c * 128 + far * 64 + ((u - z + 4) % 4) * 16, 16)
                to = slice(c * 128 + far * 64 + u * 16, c * 128 + far * 64 + u * 16 + 16)
                block = rows[pl.ds(at, 16), :].astype(f32)
                rs = jnp.sum(block[:, WIDTH + 128 :], axis=1, keepdims=True)
                x_ref[to, :] = (block[:, :WIDTH] * rs * gain_ref[...]).astype(bf16)
                tab_ref[to, :] = tab[pl.ds(at, 16), :]
    at = core * 128 + half * 64 + ((tp // 2 - z + 4) % 4) * 16
    mine = rows[pl.ds(pl.multiple_of(at, 16), 16), :WIDTH].astype(f32)
    stream_ref[...] = jnp.where(tp % 2 == 0, mine[:8], mine[8:])


def prepare(ids, own, other, gain):
    return pl.pallas_call(
        prepare_kernel,
        in_specs=[pl.BlockSpec(memory_space=pltpu.SMEM)] + [pl.BlockSpec()] * 3,
        out_shape=[
            jax.ShapeDtypeStruct((ROWS, WIDTH), bf16),
            jax.ShapeDtypeStruct((8, WIDTH), f32),
            jax.ShapeDtypeStruct((ROWS, 128), f32),
        ],
        scratch_shapes=[pltpu.VMEM((ROWS, FIRST), bf16), pltpu.VMEM((ROWS, 128), f32)],
        compiler_params=pltpu.CompilerParams(vmem_limit_bytes=8 << 20),
        name="prepare",
    )(ids, own, other, gain)


def one_hot(tab_ref, step):
    slot = lax.broadcasted_iota(jnp.int32, (ROWS, ROWS), 1).astype(f32)
    return jnp.where(slot == tab_ref[:, 64 + step : 65 + step], 1.0, 0.0)


def block_at(ids_ref):
    core, half = ids_ref[0], ids_ref[3]
    far = 1 - half
    return [half * 2 + core, half * 2 + 1 - core, far * 2 + core, far * 2 + 1 - core]


def gate_up_kernel(step, ids_ref, *refs):
    core, z = ids_ref[0], ids_ref[4]
    first = step == 0
    if first:
        x_ref, *refs = refs
    else:
        own_ref, other_ref, *refs = refs
    tab_ref, *refs = refs
    w_refs, p_refs, xs = refs[:4], refs[4:8], refs[8]
    if not first:
        x_ref = refs[9]
        x_ref[pl.ds(pl.multiple_of(core * 128, 128), 128), :] = own_ref[...]
        x_ref[pl.ds(pl.multiple_of((1 - core) * 128, 128), 128), :] = other_ref[...]
    hot = one_hot(tab_ref, step)
    picked = dot(hot.T[:SLOTS].astype(bf16), x_ref[:, :WIDTH]).astype(bf16)
    for b in range(4):
        xs[b] = picked[:, b * HALF : (b + 1) * HALF]
    if first:
        tail = jnp.zeros((PAY - SLOTS, 384), bf16)
    else:
        squares = jnp.sum(x_ref[:, WIDTH:].astype(f32), axis=1, keepdims=True)
        line = jnp.sum(hot * squares, axis=0, keepdims=True)
        line = jnp.concatenate([line, jnp.zeros((1, 128), f32)], axis=1)
        hi, mid, low = split3(line)
        at = lax.broadcasted_iota(jnp.int32, (PAY - SLOTS, 384), 0)
        tail = jnp.where(
            at == 0,
            hi.astype(f32),
            jnp.where(at == 1, mid.astype(f32), jnp.where(at == 2, low.astype(f32), 0.0)),
        ).astype(bf16)
    ours = [xs[at] for at in block_at(ids_ref)]
    for d in range(4):
        at = pl.multiple_of(((z + d) % 4) * 384, 128)
        part = dot(ours[0], w_refs[0][pl.ds(at, 384), :], NT)
        for b in range(1, 4):
            part = part + dot(ours[b], w_refs[b][pl.ds(at, 384), :], NT)
        p_refs[d][:SLOTS, :] = part.astype(bf16)
        p_refs[d][SLOTS:, :] = tail


def gate_up(step, ids, x, tab, weights):
    scratch = [pltpu.VMEM((4, SLOTS, HALF), bf16)]
    if step > 0:
        scratch.append(pltpu.VMEM((ROWS, EXT), bf16))
    return pl.pallas_call(
        lambda *refs: gate_up_kernel(step, *refs),
        in_specs=[pl.BlockSpec(memory_space=pltpu.SMEM)] + [pl.BlockSpec()] * (len(x) + 5),
        out_shape=[jax.ShapeDtypeStruct((PAY, 384), bf16)] * 4,
        scratch_shapes=scratch,
        compiler_params=pltpu.CompilerParams(vmem_limit_bytes=16 << 20),
        cost_estimate=busy(2.2),
        name="gate_up",
    )(ids, *x, tab, *weights)


def act_kernel(first, *refs):
    out_ref = refs[4]
    total = refs[0][...].astype(f32)
    for j in range(1, 4):
        total = total + refs[j][...].astype(f32)
    sums = total[:SLOTS]
    if not first:
        line = jnp.sum(total[SLOTS : SLOTS + 8, :HALF], axis=0, keepdims=True)
        rs_line = lax.rsqrt(line * (1.0 / D) + norm_eps)
        r0 = lax.broadcasted_iota(jnp.int32, (SLOTS, HALF), 0)
        r1 = lax.broadcasted_iota(jnp.int32, (SLOTS, HALF), 1)
        rs = jnp.sum(jnp.where(r0 == r1, rs_line, 0.0), axis=1, keepdims=True)
        sums = sums * rs
    t0, t1, t2 = sums[:, :128], sums[:, 128:256], sums[:, 256:]
    a0 = jax.nn.silu(t0) * t2
    a1 = jax.nn.silu(t1) * pltpu.roll(t1, 64, 1)
    half = SLOTS // 2
    lane = lax.broadcasted_iota(jnp.int32, (half, 128), 1)
    middle = jnp.where(lane < 64, a1[:half], pltpu.roll(a1[half:], 64, 1))
    out_ref[...] = jnp.concatenate([a0[:half], middle, a0[half:]], axis=1).astype(bf16)


def activate(first, p):
    return pl.pallas_call(
        lambda *refs: act_kernel(first, *refs),
        out_shape=jax.ShapeDtypeStruct((SLOTS // 2, 384), bf16),
        compiler_params=pltpu.CompilerParams(vmem_limit_bytes=8 << 20),
        cost_estimate=busy(0.3),
        name="activate",
    )(*p)


def down_kernel(step, ids_ref, *refs):
    core, z = ids_ref[0], ids_ref[4]
    a_refs, tab_ref, w_refs = refs[:4], refs[4], refs[5:9]
    send_ref, keep_ref, ys = refs[9:]
    half = SLOTS // 2
    lane = lax.broadcasted_iota(jnp.int32, (half, 128), 1)
    sums = [jnp.zeros((SLOTS, HALF), f32)] * 4
    for d in range(4):
        block = a_refs[d][...].astype(f32)
        middle = block[:, 128:256]
        low = jnp.concatenate([block[:, :128], jnp.where(lane < 64, middle, 0.0)], axis=1)
        high = jnp.concatenate([block[:, 256:], jnp.where(lane < 64, 0.0, middle)], axis=1)
        act = jnp.concatenate([low, high], axis=0).astype(bf16)
        for b in range(4):
            start = 2 * UNIT_HALF if b < 2 else 0
            at = pl.multiple_of(((z - d + 4) % 4) * UNITS + start, 64)
            after = pl.multiple_of(((z - d + 4) % 4) * UNITS + start + 128, 64)
            w = jnp.concatenate([w_refs[b][pl.ds(at, UNITS), :], w_refs[b][pl.ds(after, 64), :]], axis=0)
            sums[b] = sums[b] + dot(act, w)
    for b, at in enumerate(block_at(ids_ref)):
        ys[at] = sums[b].astype(bf16)
    slot = lax.broadcasted_iota(jnp.int32, (128, HALF), 1).astype(f32)
    for ref, part in ((send_ref, 1 - core), (keep_ref, core)):
        tab = tab_ref[pl.ds(pl.multiple_of(part * 128, 128), 128), :]
        hot = jnp.where(slot == tab[:, 64 + step : 65 + step], 1.0, 0.0)[:, :SLOTS].astype(bf16)
        for b in range(4):
            rows = dot(hot, ys[b]) * tab[:, step : step + 1]
            ref[:, b * HALF : (b + 1) * HALF] = rows.astype(ref.dtype)


def down(step, ids, acts, tab, weights):
    return pl.pallas_call(
        lambda *refs: down_kernel(step, *refs),
        in_specs=[pl.BlockSpec(memory_space=pltpu.SMEM)] + [pl.BlockSpec()] * 9,
        out_shape=[
            jax.ShapeDtypeStruct((128, WIDTH), bf16),
            jax.ShapeDtypeStruct((128, WIDTH), f32),
        ],
        scratch_shapes=[pltpu.VMEM((4, SLOTS, HALF), bf16)],
        compiler_params=pltpu.CompilerParams(vmem_limit_bytes=16 << 20),
        cost_estimate=busy(1.9),
        name="down",
    )(ids, *acts, tab, *weights)


def pair_kernel(keep_ref, other_ref, out_ref):
    out_ref[...] = (keep_ref[...] + other_ref[...].astype(f32)).astype(bf16)


def pair(keep, other):
    return pl.pallas_call(
        pair_kernel,
        out_shape=jax.ShapeDtypeStruct((128, WIDTH), bf16),
        compiler_params=pltpu.CompilerParams(vmem_limit_bytes=4 << 20),
        name="pair",
    )(keep, other)


def residual_kernel(p_ref, stream_ref, gain_ref, new_ref, x_ref):
    total = p_ref[0].astype(f32)
    for j in range(1, 16):
        total = total + p_ref[j].astype(f32)
    stream = stream_ref[...] + total
    new_ref[...] = stream
    hi, mid, low = split3(jnp.sum(stream * stream, axis=1, keepdims=True))
    lane = lax.broadcasted_iota(jnp.int32, (8, 128), 1)
    parts = jnp.where(
        lane == 0,
        hi.astype(f32),
        jnp.where(lane == 1, mid.astype(f32), jnp.where(lane == 2, low.astype(f32), 0.0)),
    )
    row = jnp.concatenate([stream * gain_ref[...], parts], axis=1).astype(bf16)
    for j in range(16):
        x_ref[j] = row


def residual(p, stream, gain):
    return pl.pallas_call(
        residual_kernel,
        out_shape=[
            jax.ShapeDtypeStruct((8, WIDTH), f32),
            jax.ShapeDtypeStruct((16, 8, EXT), bf16),
        ],
        compiler_params=pltpu.CompilerParams(vmem_limit_bytes=4 << 20),
        name="residual",
    )(p, stream, gain)


def last_kernel(p_ref, stream_ref, new_ref):
    total = p_ref[0].astype(f32)
    for j in range(1, 16):
        total = total + p_ref[j].astype(f32)
    new_ref[...] = stream_ref[...] + total


def last(p, stream):
    return pl.pallas_call(
        last_kernel,
        out_shape=jax.ShapeDtypeStruct((8, WIDTH), f32),
        compiler_params=pltpu.CompilerParams(vmem_limit_bytes=4 << 20),
        name="last",
    )(p, stream)


def place_kernel(ids_ref, whole_ref, out_ref):
    z = ids_ref[4]
    for a in range(4):
        for h in range(2):
            block = whole_ref[((a + z) % 4) * 2 + h]
            for far in range(2):
                to = far * 2048 + a * 512
                out_ref[h * 8 : h * 8 + 8, to : to + 512] = block[:, far * 512 : far * 512 + 512]


def place_rows(ids, whole):
    return pl.pallas_call(
        place_kernel,
        in_specs=[pl.BlockSpec(memory_space=pltpu.SMEM), pl.BlockSpec()],
        out_shape=jax.ShapeDtypeStruct((ROWS_DEV, D), f32),
        compiler_params=pltpu.CompilerParams(vmem_limit_bytes=4 << 20),
        name="place_rows",
    )(ids, whole)


def exchange(x, axes):
    return lax.all_to_all(x, axes, split_axis=0, concat_axis=0, tiled=True)


def reduced(v):
    return lax.reduce_precision(v, exponent_bits=8, mantissa_bits=7)


def parts3(v):
    hi = reduced(v)
    mid = reduced(v - hi)
    return [hi, mid, v - hi - mid]


def swap(x):
    return lax.ppermute(x, "c", [(0, 1), (1, 0)])


def around(x, d):
    return lax.ppermute(x, "z", [(i, (i + d) % 4) for i in range(4)])


def body(trainer_weights, hidden_in, norm_gain, routing, gate_weights):
    core, far, z = lax.axis_index("c"), lax.axis_index("xh"), lax.axis_index("z")
    tp = lax.axis_index(T)
    ids = jnp.stack([core, tp, 2 * tp + core, far, z, far * 8 + tp]).astype(jnp.int32)
    gain = lax.dynamic_index_in_dim(norm_gain.reshape(2, 4, 512), z, 1, keepdims=False)
    gain = gain.reshape(1, WIDTH)

    hidden = hidden_in.astype(f32)
    rs = lax.rsqrt(jnp.mean(hidden * hidden, axis=-1, keepdims=True) + norm_eps)
    flat = lambda v: jnp.transpose(v, (1, 0, 2)).reshape(ROWS_DEV, STEPS * TOPK)
    extra = jnp.concatenate(
        [flat(routing).astype(f32)] + parts3(flat(gate_weights)) + parts3(rs)
        + [jnp.zeros((ROWS_DEV, 125), f32)],
        axis=1,
    ).astype(bf16)
    pieces = jnp.transpose(hidden_in.reshape(ROWS_DEV, 2, 4, 512), (2, 0, 1, 3))
    pieces = pieces.reshape(4, ROWS_DEV, WIDTH)
    extra = jnp.broadcast_to(extra[None], (4, ROWS_DEV, FIRST - WIDTH))
    pieces = jnp.concatenate([pieces, extra], axis=2)
    pieces_far = lax.ppermute(pieces, "xh", [(0, 1), (1, 0)])

    near_out, diag_out = quantize_far(ids, trainer_weights)
    near_out, diag_out, pieces_far = lax.optimization_barrier((near_out, diag_out, pieces_far))
    gu_near = lax.ppermute(near_out, "xh", [(0, 1), (1, 0)])
    gu_diag = lax.ppermute(diag_out, ("xh", "c"), [(0, 3), (3, 0), (1, 2), (2, 1)])
    rows = spread(ids, pieces, pieces_far)
    rows = jnp.stack([rows[0]] + [around(rows[d], d) for d in (1, 2, 3)])
    x, stream, tab = prepare(ids, rows, swap(rows), gain)
    own, other_out, near_out, diag_out = quantize_rest(ids, trainer_weights)
    near_out, diag_out, gu_near, gu_diag, x, stream, tab, other_out = lax.optimization_barrier(
        (near_out, diag_out, gu_near, gu_diag, x, stream, tab, other_out)
    )
    other = swap(other_out)
    down_near = lax.ppermute(near_out, "xh", [(0, 1), (1, 0)])
    down_diag = lax.ppermute(diag_out, ("xh", "c"), [(0, 3), (3, 0), (1, 2), (2, 1)])

    x = [x]
    for step in range(STEPS):
        part = gate_up(step, ids, x, tab, [own, other, gu_near, gu_diag])
        part = [part[0]] + [around(part[d], d) for d in (1, 2, 3)]
        act = activate(step == 0, part)
        acts = [act] + [around(act, d) for d in (1, 2, 3)]
        send, keep = down(step, ids, acts, tab, [own, other, down_near, down_diag])
        sums = exchange(pair(keep, swap(send)).reshape(16, 8, WIDTH), XT)
        if step < STEPS - 1:
            stream, rows = residual(sums, stream, gain)
            rows = exchange(rows, XT).reshape(128, EXT)
            x = [rows, swap(rows)]
        else:
            stream = last(sums, stream)

    turn = [(a * 8 + t, ((t // 2 - a) % 4) * 8 + t) for a in range(4) for t in range(8)]
    mine = lax.ppermute(stream, ("z", "xl", "y"), turn)
    whole = exchange(jnp.broadcast_to(mine[None], (8, 8, WIDTH)), T)
    return place_rows(ids, whole)


def solution(mesh):
    fine = Mesh(mesh.devices.reshape(2, 4, 2, 2, 4), ALL)
    fsdp, tp = ("xh", "z", "c"), ("xl", "y")
    in_specs = (
        P(tp, None, None, fsdp),
        P(fsdp, None),
        P(),
        P(None, fsdp, None),
        P(None, fsdp, None),
    )
    return jax.shard_map(
        body, mesh=fine, in_specs=in_specs, out_specs=P(fsdp, None), check_vma=False
    )
```

```python
import jax
import jax.numpy as jnp
from jax import lax
from jax.experimental import pallas as pl
from jax.experimental.pallas import tpu as pltpu
from jax.sharding import Mesh, PartitionSpec as P

D = 4096
FF = 1536
TOPK = 8
EXPERTS = 16
QB = 128
STEPS = 4
CAP = 11
ROWS_DEV = 16
ROWS = 256
SLOTS = 16 * CAP
UNIT_HALF = 768
WIDTH = 1024
HALF = 256
UNITS = 192
PAY = 184
EXT = 1152
FIRST = 1280

XZ = ("xh", "z")
XT = ("xh", "xl", "y")
T = ("xl", "y")
ALL = ("xh", "z", "c", "xl", "y")

norm_eps = 1e-06
scale_eps = 1e-06
code_limit = 448.0
smallest_normal = 0.015625
f32 = jnp.float32
bf16 = jnp.bfloat16

NN = (((1,), (0,)), ((), ()))
NT = (((1,), (1,)), ((), ()))


def dot(a, b, dims=NN):
    return lax.dot_general(a, b, dims, preferred_element_type=f32)


def busy(us):
    return pl.CostEstimate(flops=int(us * 1.15e9), bytes_accessed=0, transcendentals=0)


def split3(v):
    hi = v.astype(bf16)
    rest = v - hi.astype(f32)
    mid = rest.astype(bf16)
    low = (rest - mid.astype(f32)).astype(bf16)
    return hi, mid, low


def float_code(v):
    big = v * 1048577.0
    fine = big - (big - v)
    coarse = (v + 24576.0) - 24576.0
    return jnp.where(jnp.abs(v) < smallest_normal, coarse, fine)


def quant_block(tile):
    top = jnp.max(jnp.abs(tile), axis=0, keepdims=True).astype(f32)
    top = jnp.max(top, axis=1, keepdims=True) + scale_eps
    tile = tile.astype(f32)
    scale = top / code_limit
    return (float_code(tile * (1.0 / scale)) * scale).astype(bf16)


def quant_gate_up(src, out_ref, group):
    for m in range(2):
        for q in range(3):
            for h in range(2):
                cols = slice(h * QB, (h + 1) * QB)
                back = quant_block(src[m, q * QB : (q + 1) * QB, cols])
                for g in range(2):
                    unit = q * 2 + g
                    j, part = unit // 3, unit % 3
                    if m == 0:
                        to = part * 64
                    elif part < 2:
                        to = 256 + part * 64
                    else:
                        to = 192
                    to = group * 768 + j * 384 + to
                    out_ref[to : to + 64, cols] = back[g * 64 : g * 64 + 64]


def quant_down(src, out_ref, at, blocks):
    for q in range(blocks):
        for h in range(2):
            cols = slice(h * QB, (h + 1) * QB)
            back = quant_block(src[q * QB : (q + 1) * QB, cols])
            out_ref[at + q * QB : at + (q + 1) * QB, cols] = back


def quant_far_kernel(ids_ref, w_ref, near_ref, diag_ref, buf, sem):
    core, half = ids_ref[0], 1 - ids_ref[3]
    copies = []
    for p in range(2):
        for g in range(2):
            expert = core if p == 0 else 1 - core
            at = pl.multiple_of(half * UNIT_HALF + g * 384, 128)
            src = w_ref.at[expert, pl.ds(0, 2), pl.ds(at, 384), :]
            copies.append(pltpu.make_async_copy(src, buf.at[p * 2 + g], sem.at[p * 2 + g]))
    for copy in copies:
        copy.start()
    for p in range(2):
        for g in range(2):
            copies[p * 2 + g].wait()
            quant_gate_up(buf.at[p * 2 + g], diag_ref if p else near_ref, g)


def quantize_far(ids, w):
    out = jax.ShapeDtypeStruct((2 * UNIT_HALF, HALF), bf16)
    return pl.pallas_call(
        quant_far_kernel,
        in_specs=[
            pl.BlockSpec(memory_space=pltpu.SMEM),
            pl.BlockSpec(memory_space=pltpu.HBM),
        ],
        out_shape=[out, out],
        scratch_shapes=[pltpu.VMEM((4, 2, 384, HALF), bf16), pltpu.SemaphoreType.DMA((4,))],
        compiler_params=pltpu.CompilerParams(vmem_limit_bytes=60 << 20),
        name="quantize_far",
    )(ids, w)


def quant_rest_kernel(
    ids_ref, w_ref, own_ref, other_ref, near_ref, diag_ref, buf, sem, down_buf, down_sem
):
    core, half = ids_ref[0], ids_ref[3]
    copies = []
    for p in range(2):
        expert = core if p == 0 else 1 - core
        for g in range(2):
            at = pl.multiple_of(half * UNIT_HALF + g * 384, 128)
            src = w_ref.at[expert, :, pl.ds(at, 384), :]
            copies.append(pltpu.make_async_copy(src, buf.at[p * 2 + g], sem.at[p * 2 + g]))
    down_copies = []
    for p in range(2):
        expert = core if p == 0 else 1 - core
        at = pl.multiple_of((1 - half) * UNIT_HALF, 128)
        src = w_ref.at[expert, 2, pl.ds(at, UNIT_HALF), :]
        down_copies.append(pltpu.make_async_copy(src, down_buf.at[p], down_sem.at[p]))
    for copy in copies + down_copies:
        copy.start()
    for p in range(2):
        out_ref = other_ref if p else own_ref
        for g in range(2):
            copies[p * 2 + g].wait()
            quant_gate_up(buf.at[p * 2 + g], out_ref, g)
            quant_down(buf.at[p * 2 + g, 2], out_ref, 2 * UNIT_HALF + g * 384, 3)
    for p in range(2):
        down_copies[p].wait()
        quant_down(down_buf.at[p], diag_ref if p else near_ref, 0, 6)


def quantize_rest(ids, w):
    whole = jax.ShapeDtypeStruct((3 * UNIT_HALF, HALF), bf16)
    third = jax.ShapeDtypeStruct((UNIT_HALF, HALF), bf16)
    return pl.pallas_call(
        quant_rest_kernel,
        in_specs=[
            pl.BlockSpec(memory_space=pltpu.SMEM),
            pl.BlockSpec(memory_space=pltpu.HBM),
        ],
        out_shape=[whole, whole, third, third],
        scratch_shapes=[
            pltpu.VMEM((4, 3, 384, HALF), bf16),
            pltpu.SemaphoreType.DMA((4,)),
            pltpu.VMEM((2, UNIT_HALF, HALF), bf16),
            pltpu.SemaphoreType.DMA((2,)),
        ],
        compiler_params=pltpu.CompilerParams(vmem_limit_bytes=60 << 20),
        name="quantize_rest",
    )(ids, w)


def first_kernel(*refs):
    sources, (out_ref, table), held, sem = refs[:3], refs[3:5], refs[5:8], refs[8]
    copies = [pltpu.make_async_copy(a, b, sem.at[i]) for i, (a, b) in enumerate(zip(sources, held))]
    for copy in copies:
        copy.start()
    for copy in copies:
        copy.wait()
    hidden_ref, routing_ref, gates_ref = held
    hidden = hidden_ref[...].astype(f32)
    mean = jnp.sum(hidden * hidden, axis=1, keepdims=True) * (1.0 / D)
    hi, mid, low = split3(lax.rsqrt(mean + norm_eps))
    lane = lax.broadcasted_iota(jnp.int32, (ROWS_DEV, 128), 1)
    rs = jnp.where(
        lane == 0,
        hi.astype(f32),
        jnp.where(lane == 1, mid.astype(f32), jnp.where(lane == 2, low.astype(f32), 0.0)),
    ).astype(bf16)
    table[...] = jnp.zeros((128, 128), f32)
    table[0:32, :ROWS_DEV] = routing_ref[...].astype(f32)
    for i, part in enumerate(split3(gates_ref[...])):
        table[32 + 32 * i : 64 + 32 * i, :ROWS_DEV] = part.astype(f32)
    named = table[...].T[:ROWS_DEV].astype(bf16)
    for z in range(4):
        for half in range(2):
            at = half * 2048 + z * 512
            out_ref[z, :, half * 512 : half * 512 + 512] = hidden_ref[:, at : at + 512]
        out_ref[z, :, WIDTH : WIDTH + 128] = named
        out_ref[z, :, WIDTH + 128 :] = rs


def first_rows(hidden, routing, gates):
    return pl.pallas_call(
        first_kernel,
        in_specs=[pl.BlockSpec(memory_space=pltpu.HBM)] * 3,
        out_shape=jax.ShapeDtypeStruct((4, ROWS_DEV, FIRST), bf16),
        scratch_shapes=[
            pltpu.VMEM((128, 128), f32),
            pltpu.VMEM((ROWS_DEV, D), bf16),
            pltpu.VMEM((STEPS * TOPK, ROWS_DEV), jnp.int32),
            pltpu.VMEM((STEPS * TOPK, ROWS_DEV), f32),
            pltpu.SemaphoreType.DMA((3,)),
        ],
        compiler_params=pltpu.CompilerParams(vmem_limit_bytes=60 << 20),
        name="first_rows",
    )(hidden, routing, gates)


def spread_kernel(ids_ref, own_ref, far_ref, *out_refs):
    half, z = ids_ref[3], ids_ref[4]
    for d in range(4):
        at = (z + d) % 4
        out_refs[d][half] = own_ref[at]
        out_refs[d][1 - half] = far_ref[at]


def spread(ids, own, far):
    return pl.pallas_call(
        spread_kernel,
        in_specs=[pl.BlockSpec(memory_space=pltpu.SMEM)] + [pl.BlockSpec()] * 2,
        out_shape=[jax.ShapeDtypeStruct((2, ROWS_DEV, FIRST), bf16)] * 4,
        compiler_params=pltpu.CompilerParams(vmem_limit_bytes=4 << 20),
        name="spread",
    )(ids, own, far)


def prepare_kernel(ids_ref, own_ref, other_ref, gain_ref, x_ref, stream_ref, tab_ref, rows, tab):
    core, tp, expert, half, z = [ids_ref[i] for i in range(5)]
    for d in range(4):
        for far in range(2):
            at = (far * 4 + (z - d + 4) % 4) * 16
            rows[pl.ds(pl.multiple_of(core * 128 + at, 16), 16), :] = own_ref[d, far]
            rows[pl.ds(pl.multiple_of((1 - core) * 128 + at, 16), 16), :] = other_ref[d, far]
    named = rows[:, WIDTH : WIDTH + 128].astype(f32)
    gates = pltpu.roll(named, 96, 1) + pltpu.roll(named, 64, 1) + pltpu.roll(named, 32, 1)
    lane = lax.broadcasted_iota(jnp.int32, (ROWS, 128), 1)
    match = jnp.where((named == expert.astype(f32)) & (lane < 32), 1.0, 0.0)
    weighted = match * gates
    group = lane // TOPK
    mask = jnp.zeros((ROWS, 128), f32)
    weight = jnp.zeros((ROWS, 128), f32)
    for s in range(STEPS):
        here = jnp.sum(jnp.where(group == s, match, 0.0), axis=1, keepdims=True)
        gate = jnp.sum(jnp.where(group == s, weighted, 0.0), axis=1, keepdims=True)
        mask = jnp.where(lane == s, here, mask)
        weight = jnp.where(lane == s, gate, weight)
    r0 = lax.broadcasted_iota(jnp.int32, (ROWS, ROWS), 0)
    r1 = lax.broadcasted_iota(jnp.int32, (ROWS, ROWS), 1)
    before = jnp.where(r1 < r0, 1.0, 0.0).astype(bf16)
    place = jnp.where(mask > 0.0, dot(before, mask.astype(bf16)), -1.0)
    tab[...] = jnp.where(lane < 64, weight, pltpu.roll(place, 64, 1))
    for c in range(2):
        for far in range(2):
            for u in range(4):
                at = pl.multiple_of(c * 128 + far * 64 + ((u - z + 4) % 4) * 16, 16)
                to = slice(c * 128 + far * 64 + u * 16, c * 128 + far * 64 + u * 16 + 16)
                block = rows[pl.ds(at, 16), :].astype(f32)
                rs = jnp.sum(block[:, WIDTH + 128 :], axis=1, keepdims=True)
                x_ref[to, :] = (block[:, :WIDTH] * rs * gain_ref[...]).astype(bf16)
                tab_ref[to, :] = tab[pl.ds(at, 16), :]
    at = core * 128 + half * 64 + ((tp // 2 - z + 4) % 4) * 16
    mine = rows[pl.ds(pl.multiple_of(at, 16), 16), :WIDTH].astype(f32)
    stream_ref[...] = jnp.where(tp % 2 == 0, mine[:8], mine[8:])


def prepare(ids, own, other, gain):
    return pl.pallas_call(
        prepare_kernel,
        in_specs=[pl.BlockSpec(memory_space=pltpu.SMEM)] + [pl.BlockSpec()] * 3,
        out_shape=[
            jax.ShapeDtypeStruct((ROWS, WIDTH), bf16),
            jax.ShapeDtypeStruct((8, WIDTH), f32),
            jax.ShapeDtypeStruct((ROWS, 128), f32),
        ],
        scratch_shapes=[pltpu.VMEM((ROWS, FIRST), bf16), pltpu.VMEM((ROWS, 128), f32)],
        compiler_params=pltpu.CompilerParams(vmem_limit_bytes=8 << 20),
        name="prepare",
    )(ids, own, other, gain)


def one_hot(tab_ref, step):
    slot = lax.broadcasted_iota(jnp.int32, (ROWS, ROWS), 1).astype(f32)
    return jnp.where(slot == tab_ref[:, 64 + step : 65 + step], 1.0, 0.0)


def block_at(ids_ref):
    core, half = ids_ref[0], ids_ref[3]
    far = 1 - half
    return [half * 2 + core, half * 2 + 1 - core, far * 2 + core, far * 2 + 1 - core]


def gate_up_kernel(step, ids_ref, *refs):
    core, z = ids_ref[0], ids_ref[4]
    first = step == 0
    if first:
        x_ref, *refs = refs
    else:
        own_ref, other_ref, *refs = refs
    tab_ref, *refs = refs
    w_refs, p_refs, xs = refs[:4], refs[4:8], refs[8]
    if not first:
        x_ref = refs[9]
        x_ref[pl.ds(pl.multiple_of(core * 128, 128), 128), :] = own_ref[...]
        x_ref[pl.ds(pl.multiple_of((1 - core) * 128, 128), 128), :] = other_ref[...]
    hot = one_hot(tab_ref, step)
    picked = dot(hot.T[:SLOTS].astype(bf16), x_ref[:, :WIDTH]).astype(bf16)
    for b in range(4):
        xs[b] = picked[:, b * HALF : (b + 1) * HALF]
    if first:
        tail = jnp.zeros((PAY - SLOTS, 384), bf16)
    else:
        squares = jnp.sum(x_ref[:, WIDTH:].astype(f32), axis=1, keepdims=True)
        line = jnp.sum(hot * squares, axis=0, keepdims=True)
        line = jnp.concatenate([line, jnp.zeros((1, 128), f32)], axis=1)
        hi, mid, low = split3(line)
        at = lax.broadcasted_iota(jnp.int32, (PAY - SLOTS, 384), 0)
        tail = jnp.where(
            at == 0,
            hi.astype(f32),
            jnp.where(at == 1, mid.astype(f32), jnp.where(at == 2, low.astype(f32), 0.0)),
        ).astype(bf16)
    ours = [xs[at] for at in block_at(ids_ref)]
    for d in range(4):
        at = pl.multiple_of(((z + d) % 4) * 384, 128)
        part = dot(ours[0], w_refs[0][pl.ds(at, 384), :], NT)
        for b in range(1, 4):
            part = part + dot(ours[b], w_refs[b][pl.ds(at, 384), :], NT)
        p_refs[d][:SLOTS, :] = part.astype(bf16)
        p_refs[d][SLOTS:, :] = tail


def gate_up(step, ids, x, tab, weights):
    scratch = [pltpu.VMEM((4, SLOTS, HALF), bf16)]
    if step > 0:
        scratch.append(pltpu.VMEM((ROWS, EXT), bf16))
    return pl.pallas_call(
        lambda *refs: gate_up_kernel(step, *refs),
        in_specs=[pl.BlockSpec(memory_space=pltpu.SMEM)] + [pl.BlockSpec()] * (len(x) + 5),
        out_shape=[jax.ShapeDtypeStruct((PAY, 384), bf16)] * 4,
        scratch_shapes=scratch,
        compiler_params=pltpu.CompilerParams(vmem_limit_bytes=16 << 20),
        cost_estimate=busy(2.2),
        name="gate_up",
    )(ids, *x, tab, *weights)


def act_kernel(first, *refs):
    out_ref = refs[4]
    total = refs[0][...].astype(f32)
    for j in range(1, 4):
        total = total + refs[j][...].astype(f32)
    sums = total[:SLOTS]
    if not first:
        line = jnp.sum(total[SLOTS : SLOTS + 8, :HALF], axis=0, keepdims=True)
        rs_line = lax.rsqrt(line * (1.0 / D) + norm_eps)
        r0 = lax.broadcasted_iota(jnp.int32, (SLOTS, HALF), 0)
        r1 = lax.broadcasted_iota(jnp.int32, (SLOTS, HALF), 1)
        rs = jnp.sum(jnp.where(r0 == r1, rs_line, 0.0), axis=1, keepdims=True)
        sums = sums * rs
    t0, t1, t2 = sums[:, :128], sums[:, 128:256], sums[:, 256:]
    a0 = jax.nn.silu(t0) * t2
    a1 = jax.nn.silu(t1) * pltpu.roll(t1, 64, 1)
    half = SLOTS // 2
    lane = lax.broadcasted_iota(jnp.int32, (half, 128), 1)
    middle = jnp.where(lane < 64, a1[:half], pltpu.roll(a1[half:], 64, 1))
    out_ref[...] = jnp.concatenate([a0[:half], middle, a0[half:]], axis=1).astype(bf16)


def activate(first, p):
    return pl.pallas_call(
        lambda *refs: act_kernel(first, *refs),
        out_shape=jax.ShapeDtypeStruct((SLOTS // 2, 384), bf16),
        compiler_params=pltpu.CompilerParams(vmem_limit_bytes=8 << 20),
        cost_estimate=busy(0.3),
        name="activate",
    )(*p)


def down_kernel(step, ids_ref, *refs):
    core, z = ids_ref[0], ids_ref[4]
    a_refs, tab_ref, w_refs = refs[:4], refs[4], refs[5:9]
    send_ref, keep_ref, ys = refs[9:]
    half = SLOTS // 2
    lane = lax.broadcasted_iota(jnp.int32, (half, 128), 1)
    sums = [jnp.zeros((SLOTS, HALF), f32)] * 4
    for d in range(4):
        block = a_refs[d][...].astype(f32)
        middle = block[:, 128:256]
        low = jnp.concatenate([block[:, :128], jnp.where(lane < 64, middle, 0.0)], axis=1)
        high = jnp.concatenate([block[:, 256:], jnp.where(lane < 64, 0.0, middle)], axis=1)
        act = jnp.concatenate([low, high], axis=0).astype(bf16)
        for b in range(4):
            start = 2 * UNIT_HALF if b < 2 else 0
            at = pl.multiple_of(((z - d + 4) % 4) * UNITS + start, 64)
            after = pl.multiple_of(((z - d + 4) % 4) * UNITS + start + 128, 64)
            w = jnp.concatenate([w_refs[b][pl.ds(at, UNITS), :], w_refs[b][pl.ds(after, 64), :]], axis=0)
            sums[b] = sums[b] + dot(act, w)
    for b, at in enumerate(block_at(ids_ref)):
        ys[at] = sums[b].astype(bf16)
    slot = lax.broadcasted_iota(jnp.int32, (128, HALF), 1).astype(f32)
    for ref, part in ((send_ref, 1 - core), (keep_ref, core)):
        tab = tab_ref[pl.ds(pl.multiple_of(part * 128, 128), 128), :]
        hot = jnp.where(slot == tab[:, 64 + step : 65 + step], 1.0, 0.0)[:, :SLOTS].astype(bf16)
        for b in range(4):
            rows = dot(hot, ys[b]) * tab[:, step : step + 1]
            ref[:, b * HALF : (b + 1) * HALF] = rows.astype(ref.dtype)


def down(step, ids, acts, tab, weights):
    return pl.pallas_call(
        lambda *refs: down_kernel(step, *refs),
        in_specs=[pl.BlockSpec(memory_space=pltpu.SMEM)] + [pl.BlockSpec()] * 9,
        out_shape=[
            jax.ShapeDtypeStruct((128, WIDTH), bf16),
            jax.ShapeDtypeStruct((128, WIDTH), f32),
        ],
        scratch_shapes=[pltpu.VMEM((4, SLOTS, HALF), bf16)],
        compiler_params=pltpu.CompilerParams(vmem_limit_bytes=16 << 20),
        cost_estimate=busy(1.9),
        name="down",
    )(ids, *acts, tab, *weights)


def pair_kernel(keep_ref, other_ref, out_ref):
    out_ref[...] = (keep_ref[...] + other_ref[...].astype(f32)).astype(bf16)


def pair(keep, other):
    return pl.pallas_call(
        pair_kernel,
        out_shape=jax.ShapeDtypeStruct((128, WIDTH), bf16),
        compiler_params=pltpu.CompilerParams(vmem_limit_bytes=4 << 20),
        name="pair",
    )(keep, other)


def residual_kernel(p_ref, stream_ref, gain_ref, new_ref, x_ref):
    total = p_ref[0].astype(f32)
    for j in range(1, 16):
        total = total + p_ref[j].astype(f32)
    stream = stream_ref[...] + total
    new_ref[...] = stream
    hi, mid, low = split3(jnp.sum(stream * stream, axis=1, keepdims=True))
    lane = lax.broadcasted_iota(jnp.int32, (8, 128), 1)
    parts = jnp.where(
        lane == 0,
        hi.astype(f32),
        jnp.where(lane == 1, mid.astype(f32), jnp.where(lane == 2, low.astype(f32), 0.0)),
    )
    row = jnp.concatenate([stream * gain_ref[...], parts], axis=1).astype(bf16)
    for j in range(16):
        x_ref[j] = row


def residual(p, stream, gain):
    return pl.pallas_call(
        residual_kernel,
        out_shape=[
            jax.ShapeDtypeStruct((8, WIDTH), f32),
            jax.ShapeDtypeStruct((16, 8, EXT), bf16),
        ],
        compiler_params=pltpu.CompilerParams(vmem_limit_bytes=4 << 20),
        name="residual",
    )(p, stream, gain)


def last_kernel(p_ref, stream_ref, before_ref, change_ref):
    total = p_ref[0].astype(f32)
    for j in range(1, 16):
        total = total + p_ref[j].astype(f32)
    change_ref[...] = (stream_ref[...] - before_ref[...] + total).astype(bf16)


def last(p, stream, before):
    return pl.pallas_call(
        last_kernel,
        out_shape=jax.ShapeDtypeStruct((8, WIDTH), bf16),
        compiler_params=pltpu.CompilerParams(vmem_limit_bytes=4 << 20),
        name="last",
    )(p, stream, before)


def place_kernel(ids_ref, whole_ref, hidden_ref, out_ref):
    z = ids_ref[4]
    for a in range(4):
        for h in range(2):
            block = whole_ref[((a + z) % 4) * 2 + h].astype(f32)
            for far in range(2):
                to = far * 2048 + a * 512
                rows = hidden_ref[:, to : to + 512].astype(f32)[h * 8 : h * 8 + 8]
                out_ref[h * 8 : h * 8 + 8, to : to + 512] = (
                    rows + block[:, far * 512 : far * 512 + 512]
                )


def place_rows(ids, whole, hidden):
    return pl.pallas_call(
        place_kernel,
        in_specs=[pl.BlockSpec(memory_space=pltpu.SMEM), pl.BlockSpec(), pl.BlockSpec()],
        out_shape=jax.ShapeDtypeStruct((ROWS_DEV, D), f32),
        compiler_params=pltpu.CompilerParams(vmem_limit_bytes=4 << 20),
        name="place_rows",
    )(ids, whole, hidden)


def exchange(x, axes):
    return lax.all_to_all(x, axes, split_axis=0, concat_axis=0, tiled=True)


def swap(x):
    return lax.ppermute(x, "c", [(0, 1), (1, 0)])


def around(x, d):
    return lax.ppermute(x, "z", [(i, (i + d) % 4) for i in range(4)])


def body(trainer_weights, hidden_in, norm_gain, routing, gate_weights):
    core, far, z = lax.axis_index("c"), lax.axis_index("xh"), lax.axis_index("z")
    tp = lax.axis_index(T)
    ids = jnp.stack([core, tp, 2 * tp + core, far, z, far * 8 + tp]).astype(jnp.int32)
    gain = lax.dynamic_index_in_dim(norm_gain.reshape(2, 4, 512), z, 1, keepdims=False)
    gain = gain.reshape(1, WIDTH)

    lines = lambda v: jnp.transpose(v, (0, 2, 1)).reshape(STEPS * TOPK, ROWS_DEV)
    pieces = first_rows(hidden_in, lines(routing), lines(gate_weights))
    pieces_far = lax.ppermute(pieces, "xh", [(0, 1), (1, 0)])

    near_out, diag_out = quantize_far(ids, trainer_weights)
    near_out, diag_out, pieces_far = lax.optimization_barrier((near_out, diag_out, pieces_far))
    gu_near = lax.ppermute(near_out, "xh", [(0, 1), (1, 0)])
    gu_diag = lax.ppermute(diag_out, ("xh", "c"), [(0, 3), (3, 0), (1, 2), (2, 1)])
    rows = spread(ids, pieces, pieces_far)
    rows = jnp.stack([rows[0]] + [around(rows[d], d) for d in (1, 2, 3)])
    x, stream, tab = prepare(ids, rows, swap(rows), gain)
    own, other_out, near_out, diag_out = quantize_rest(ids, trainer_weights)
    near_out, diag_out, gu_near, gu_diag, x, stream, tab, other_out = lax.optimization_barrier(
        (near_out, diag_out, gu_near, gu_diag, x, stream, tab, other_out)
    )
    other = swap(other_out)
    down_near = lax.ppermute(near_out, "xh", [(0, 1), (1, 0)])
    down_diag = lax.ppermute(diag_out, ("xh", "c"), [(0, 3), (3, 0), (1, 2), (2, 1)])

    x, before = [x], stream
    for step in range(STEPS):
        part = gate_up(step, ids, x, tab, [own, other, gu_near, gu_diag])
        part = [part[0]] + [around(part[d], d) for d in (1, 2, 3)]
        act = activate(step == 0, part)
        acts = [act] + [around(act, d) for d in (1, 2, 3)]
        send, keep = down(step, ids, acts, tab, [own, other, down_near, down_diag])
        sums = exchange(pair(keep, swap(send)).reshape(16, 8, WIDTH), XT)
        if step < STEPS - 1:
            stream, rows = residual(sums, stream, gain)
            rows = exchange(rows, XT).reshape(128, EXT)
            x = [rows, swap(rows)]
        else:
            change = last(sums, stream, before)

    turn = [(a * 8 + t, ((t // 2 - a) % 4) * 8 + t) for a in range(4) for t in range(8)]
    mine = lax.ppermute(change, ("z", "xl", "y"), turn)
    whole = exchange(jnp.broadcast_to(mine[None], (8, 8, WIDTH)), T)
    return place_rows(ids, whole, hidden_in)


def solution(mesh):
    fine = Mesh(mesh.devices.reshape(2, 4, 2, 2, 4), ALL)
    fsdp, tp = ("xh", "z", "c"), ("xl", "y")
    in_specs = (
        P(tp, None, None, fsdp),
        P(fsdp, None),
        P(),
        P(None, fsdp, None),
        P(None, fsdp, None),
    )
    return jax.shard_map(
        body, mesh=fine, in_specs=in_specs, out_specs=P(fsdp, None), check_vma=False
    )
```

```python
import jax
import jax.numpy as jnp
from jax import lax
from jax.experimental import pallas as pl
from jax.experimental.pallas import tpu as pltpu
from jax.sharding import Mesh, PartitionSpec as P

D = 4096
FF = 1536
TOPK = 8
EXPERTS = 16
QB = 128
STEPS = 4
CAP = 11
ROWS_DEV = 16
ROWS = 256
SLOTS = 16 * CAP
UNIT_HALF = 768
WIDTH = 1024
HALF = 256
UNITS = 192
PAY = 184
EXT = 1152
FIRST = 1280

XZ = ("xh", "z")
XT = ("xh", "xl", "y")
T = ("xl", "y")
ALL = ("xh", "z", "c", "xl", "y")

norm_eps = 1e-06
scale_eps = 1e-06
code_limit = 448.0
smallest_normal = 0.015625
f32 = jnp.float32
bf16 = jnp.bfloat16

NN = (((1,), (0,)), ((), ()))
NT = (((1,), (1,)), ((), ()))


def dot(a, b, dims=NN):
    return lax.dot_general(a, b, dims, preferred_element_type=f32)


def busy(us, moved=0):
    return pl.CostEstimate(flops=int(us * 1.15e9), bytes_accessed=moved, transcendentals=0)


def split3(v):
    hi = v.astype(bf16)
    rest = v - hi.astype(f32)
    mid = rest.astype(bf16)
    low = (rest - mid.astype(f32)).astype(bf16)
    return hi, mid, low


def float_code(v):
    big = v * 1048577.0
    fine = big - (big - v)
    coarse = (v + 24576.0) - 24576.0
    return jnp.where(jnp.abs(v) < smallest_normal, coarse, fine)


def quant_block(tile):
    top = jnp.max(jnp.abs(tile), axis=0, keepdims=True).astype(f32)
    top = jnp.max(top, axis=1, keepdims=True) + scale_eps
    tile = tile.astype(f32)
    scale = top / code_limit
    return (float_code(tile * (1.0 / scale)) * scale).astype(bf16)


def quant_gate_up(src, out_ref, group):
    for m in range(2):
        for q in range(3):
            for h in range(2):
                cols = slice(h * QB, (h + 1) * QB)
                back = quant_block(src[m, q * QB : (q + 1) * QB, cols])
                for g in range(2):
                    unit = q * 2 + g
                    j, part = unit // 3, unit % 3
                    if m == 0:
                        to = part * 64
                    elif part < 2:
                        to = 256 + part * 64
                    else:
                        to = 192
                    to = group * 768 + j * 384 + to
                    out_ref[to : to + 64, cols] = back[g * 64 : g * 64 + 64]


def quant_down(src, out_ref, at, blocks):
    for q in range(blocks):
        for h in range(2):
            cols = slice(h * QB, (h + 1) * QB)
            back = quant_block(src[q * QB : (q + 1) * QB, cols])
            out_ref[at + q * QB : at + (q + 1) * QB, cols] = back


def quant_far_kernel(ids_ref, w_ref, near_ref, diag_ref, buf, sem):
    core, half = ids_ref[0], 1 - ids_ref[3]
    copies = []
    for p in range(2):
        for g in range(2):
            expert = core if p == 0 else 1 - core
            at = pl.multiple_of(half * UNIT_HALF + g * 384, 128)
            src = w_ref.at[expert, pl.ds(0, 2), pl.ds(at, 384), :]
            copies.append(pltpu.make_async_copy(src, buf.at[p * 2 + g], sem.at[p * 2 + g]))
    for copy in copies:
        copy.start()
    for p in range(2):
        for g in range(2):
            copies[p * 2 + g].wait()
            quant_gate_up(buf.at[p * 2 + g], diag_ref if p else near_ref, g)


def quantize_far(ids, w):
    out = jax.ShapeDtypeStruct((2 * UNIT_HALF, HALF), bf16)
    return pl.pallas_call(
        quant_far_kernel,
        in_specs=[
            pl.BlockSpec(memory_space=pltpu.SMEM),
            pl.BlockSpec(memory_space=pltpu.HBM),
        ],
        out_shape=[out, out],
        scratch_shapes=[pltpu.VMEM((4, 2, 384, HALF), bf16), pltpu.SemaphoreType.DMA((4,))],
        compiler_params=pltpu.CompilerParams(vmem_limit_bytes=60 << 20),
        name="quantize_far",
    )(ids, w)


def quant_rest_kernel(
    ids_ref, w_ref, pair_ref, near_ref, diag_ref, buf, sem, down_buf, down_sem
):
    core, half = ids_ref[0], ids_ref[3]
    copies = []
    for p in range(2):
        expert = core if p == 0 else 1 - core
        for g in range(2):
            at = pl.multiple_of(half * UNIT_HALF + g * 384, 128)
            src = w_ref.at[expert, :, pl.ds(at, 384), :]
            copies.append(pltpu.make_async_copy(src, buf.at[p * 2 + g], sem.at[p * 2 + g]))
    down_copies = []
    for p in range(2):
        expert = core if p == 0 else 1 - core
        at = pl.multiple_of((1 - half) * UNIT_HALF, 128)
        src = w_ref.at[expert, 2, pl.ds(at, UNIT_HALF), :]
        down_copies.append(pltpu.make_async_copy(src, down_buf.at[p], down_sem.at[p]))
    for copy in copies + down_copies:
        copy.start()
    for p in range(2):
        out_ref = pair_ref.at[1 - core if p else core]
        for g in range(2):
            copies[p * 2 + g].wait()
            quant_gate_up(buf.at[p * 2 + g], out_ref, g)
            quant_down(buf.at[p * 2 + g, 2], out_ref, 2 * UNIT_HALF + g * 384, 3)
    for p in range(2):
        down_copies[p].wait()
        quant_down(down_buf.at[p], diag_ref if p else near_ref, 0, 6)


def keep_kernel(mixed_ref, out_ref):
    out_ref[...] = mixed_ref[...]


def hold(mixed):
    return pl.pallas_call(
        keep_kernel,
        out_shape=jax.ShapeDtypeStruct(mixed.shape, bf16),
        compiler_params=pltpu.CompilerParams(vmem_limit_bytes=12 << 20),
        name="hold",
    )(mixed)


def quantize_rest(ids, w):
    whole = jax.ShapeDtypeStruct((2, 3 * UNIT_HALF, HALF), bf16)
    third = jax.ShapeDtypeStruct((UNIT_HALF, HALF), bf16)
    return pl.pallas_call(
        quant_rest_kernel,
        in_specs=[
            pl.BlockSpec(memory_space=pltpu.SMEM),
            pl.BlockSpec(memory_space=pltpu.HBM),
        ],
        out_shape=[whole, third, third],
        scratch_shapes=[
            pltpu.VMEM((4, 3, 384, HALF), bf16),
            pltpu.SemaphoreType.DMA((4,)),
            pltpu.VMEM((2, UNIT_HALF, HALF), bf16),
            pltpu.SemaphoreType.DMA((2,)),
        ],
        compiler_params=pltpu.CompilerParams(vmem_limit_bytes=16 << 20),
        name="quantize_rest",
    )(ids, w)


def first_kernel(*refs):
    sources, (out_ref, table), held, sem = refs[:3], refs[3:5], refs[5:8], refs[8]
    copies = [pltpu.make_async_copy(a, b, sem.at[i]) for i, (a, b) in enumerate(zip(sources, held))]
    for copy in copies:
        copy.start()
    for copy in copies:
        copy.wait()
    hidden_ref, routing_ref, gates_ref = held
    hidden = hidden_ref[...].astype(f32)
    mean = jnp.sum(hidden * hidden, axis=1, keepdims=True) * (1.0 / D)
    hi, mid, low = split3(lax.rsqrt(mean + norm_eps))
    lane = lax.broadcasted_iota(jnp.int32, (ROWS_DEV, 128), 1)
    rs = jnp.where(
        lane == 0,
        hi.astype(f32),
        jnp.where(lane == 1, mid.astype(f32), jnp.where(lane == 2, low.astype(f32), 0.0)),
    ).astype(bf16)
    table[...] = jnp.zeros((128, 128), f32)
    table[0:32, :ROWS_DEV] = routing_ref[...].astype(f32)
    for i, part in enumerate(split3(gates_ref[...])):
        table[32 + 32 * i : 64 + 32 * i, :ROWS_DEV] = part.astype(f32)
    named = table[...].T[:ROWS_DEV].astype(bf16)
    for z in range(4):
        for half in range(2):
            at = half * 2048 + z * 512
            out_ref[z, :, half * 512 : half * 512 + 512] = hidden_ref[:, at : at + 512]
        out_ref[z, :, WIDTH : WIDTH + 128] = named
        out_ref[z, :, WIDTH + 128 :] = rs


def first_rows(hidden, routing, gates):
    return pl.pallas_call(
        first_kernel,
        in_specs=[pl.BlockSpec(memory_space=pltpu.HBM)] * 3,
        out_shape=jax.ShapeDtypeStruct((4, ROWS_DEV, FIRST), bf16),
        scratch_shapes=[
            pltpu.VMEM((128, 128), f32),
            pltpu.VMEM((ROWS_DEV, D), bf16),
            pltpu.VMEM((STEPS * TOPK, ROWS_DEV), jnp.int32),
            pltpu.VMEM((STEPS * TOPK, ROWS_DEV), f32),
            pltpu.SemaphoreType.DMA((3,)),
        ],
        compiler_params=pltpu.CompilerParams(vmem_limit_bytes=60 << 20),
        name="first_rows",
    )(hidden, routing, gates)


def spread_kernel(ids_ref, own_ref, far_ref, *out_refs):
    half, z = ids_ref[3], ids_ref[4]
    for d in range(4):
        at = (z + d) % 4
        out_refs[d][half] = own_ref[at]
        out_refs[d][1 - half] = far_ref[at]


def spread(ids, own, far):
    return pl.pallas_call(
        spread_kernel,
        in_specs=[pl.BlockSpec(memory_space=pltpu.SMEM)] + [pl.BlockSpec()] * 2,
        out_shape=[jax.ShapeDtypeStruct((2, ROWS_DEV, FIRST), bf16)] * 4,
        compiler_params=pltpu.CompilerParams(vmem_limit_bytes=4 << 20),
        name="spread",
    )(ids, own, far)


def prepare_kernel(ids_ref, own_ref, other_ref, gain_ref, x_ref, stream_ref, tab_ref, rows, tab):
    core, tp, expert, half, z = [ids_ref[i] for i in range(5)]
    for d in range(4):
        for far in range(2):
            at = (far * 4 + (z - d + 4) % 4) * 16
            rows[pl.ds(pl.multiple_of(core * 128 + at, 16), 16), :] = own_ref[d, far]
            rows[pl.ds(pl.multiple_of((1 - core) * 128 + at, 16), 16), :] = other_ref[d, far]
    named = rows[:, WIDTH : WIDTH + 128].astype(f32)
    gates = pltpu.roll(named, 96, 1) + pltpu.roll(named, 64, 1) + pltpu.roll(named, 32, 1)
    lane = lax.broadcasted_iota(jnp.int32, (ROWS, 128), 1)
    match = jnp.where((named == expert.astype(f32)) & (lane < 32), 1.0, 0.0)
    weighted = match * gates
    group = lane // TOPK
    mask = jnp.zeros((ROWS, 128), f32)
    weight = jnp.zeros((ROWS, 128), f32)
    for s in range(STEPS):
        here = jnp.sum(jnp.where(group == s, match, 0.0), axis=1, keepdims=True)
        gate = jnp.sum(jnp.where(group == s, weighted, 0.0), axis=1, keepdims=True)
        mask = jnp.where(lane == s, here, mask)
        weight = jnp.where(lane == s, gate, weight)
    r0 = lax.broadcasted_iota(jnp.int32, (ROWS, ROWS), 0)
    r1 = lax.broadcasted_iota(jnp.int32, (ROWS, ROWS), 1)
    before = jnp.where(r1 < r0, 1.0, 0.0).astype(bf16)
    place = jnp.where(mask > 0.0, dot(before, mask.astype(bf16)), -1.0)
    tab[...] = jnp.where(lane < 64, weight, pltpu.roll(place, 64, 1))
    for c in range(2):
        for far in range(2):
            for u in range(4):
                at = pl.multiple_of(c * 128 + far * 64 + ((u - z + 4) % 4) * 16, 16)
                to = slice(c * 128 + far * 64 + u * 16, c * 128 + far * 64 + u * 16 + 16)
                block = rows[pl.ds(at, 16), :].astype(f32)
                rs = jnp.sum(block[:, WIDTH + 128 :], axis=1, keepdims=True)
                x_ref[to, :] = (block[:, :WIDTH] * rs * gain_ref[...]).astype(bf16)
                tab_ref[to, :] = tab[pl.ds(at, 16), :]
    at = core * 128 + half * 64 + ((tp // 2 - z + 4) % 4) * 16
    mine = rows[pl.ds(pl.multiple_of(at, 16), 16), :WIDTH].astype(f32)
    stream_ref[...] = jnp.where(tp % 2 == 0, mine[:8], mine[8:])


def prepare(ids, own, other, gain):
    return pl.pallas_call(
        prepare_kernel,
        in_specs=[pl.BlockSpec(memory_space=pltpu.SMEM)] + [pl.BlockSpec()] * 3,
        out_shape=[
            jax.ShapeDtypeStruct((ROWS, WIDTH), bf16),
            jax.ShapeDtypeStruct((8, WIDTH), f32),
            jax.ShapeDtypeStruct((ROWS, 128), f32),
        ],
        scratch_shapes=[pltpu.VMEM((ROWS, FIRST), bf16), pltpu.VMEM((ROWS, 128), f32)],
        compiler_params=pltpu.CompilerParams(vmem_limit_bytes=8 << 20),
        name="prepare",
    )(ids, own, other, gain)


def one_hot(tab_ref, step):
    slot = lax.broadcasted_iota(jnp.int32, (ROWS, ROWS), 1).astype(f32)
    return jnp.where(slot == tab_ref[:, 64 + step : 65 + step], 1.0, 0.0)


def block_at(ids_ref):
    core, half = ids_ref[0], ids_ref[3]
    far = 1 - half
    return [half * 2 + core, half * 2 + 1 - core, far * 2 + core, far * 2 + 1 - core]


def gate_up_kernel(step, ids_ref, *refs):
    core, z = ids_ref[0], ids_ref[4]
    first = step == 0
    if first:
        x_ref, *refs = refs
    else:
        own_ref, other_ref, *refs = refs
    tab_ref, *refs = refs
    w_refs, p_refs, xs = refs[:3], refs[3:7], refs[7]
    w_refs = [w_refs[0].at[core], w_refs[0].at[1 - core], *w_refs[1:]]
    if not first:
        x_ref = refs[8]
        x_ref[pl.ds(pl.multiple_of(core * 128, 128), 128), :] = own_ref[...]
        x_ref[pl.ds(pl.multiple_of((1 - core) * 128, 128), 128), :] = other_ref[...]
    hot = one_hot(tab_ref, step)
    picked = dot(hot.T[:SLOTS].astype(bf16), x_ref[:, :WIDTH]).astype(bf16)
    for b in range(4):
        xs[b] = picked[:, b * HALF : (b + 1) * HALF]
    if first:
        tail = jnp.zeros((PAY - SLOTS, 384), bf16)
    else:
        squares = jnp.sum(x_ref[:, WIDTH:].astype(f32), axis=1, keepdims=True)
        line = jnp.sum(hot * squares, axis=0, keepdims=True)
        line = jnp.concatenate([line, jnp.zeros((1, 128), f32)], axis=1)
        hi, mid, low = split3(line)
        at = lax.broadcasted_iota(jnp.int32, (PAY - SLOTS, 384), 0)
        tail = jnp.where(
            at == 0,
            hi.astype(f32),
            jnp.where(at == 1, mid.astype(f32), jnp.where(at == 2, low.astype(f32), 0.0)),
        ).astype(bf16)
    ours = [xs[at] for at in block_at(ids_ref)]
    for d in range(4):
        at = pl.multiple_of(((z + d) % 4) * 384, 128)
        part = dot(ours[0], w_refs[0][pl.ds(at, 384), :], NT)
        for b in range(1, 4):
            part = part + dot(ours[b], w_refs[b][pl.ds(at, 384), :], NT)
        p_refs[d][:SLOTS, :] = part.astype(bf16)
        p_refs[d][SLOTS:, :] = tail


def gate_up(step, ids, x, tab, weights):
    scratch = [pltpu.VMEM((4, SLOTS, HALF), bf16)]
    if step > 0:
        scratch.append(pltpu.VMEM((ROWS, EXT), bf16))
    return pl.pallas_call(
        lambda *refs: gate_up_kernel(step, *refs),
        in_specs=[pl.BlockSpec(memory_space=pltpu.SMEM)] + [pl.BlockSpec()] * (len(x) + 4),
        out_shape=[jax.ShapeDtypeStruct((PAY, 384), bf16)] * 4,
        scratch_shapes=scratch,
        compiler_params=pltpu.CompilerParams(vmem_limit_bytes=10 << 20),
        cost_estimate=busy(2.2, 4600000),
        name="gate_up",
    )(ids, *x, tab, *weights)


def act_kernel(first, *refs):
    out_ref = refs[4]
    total = refs[0][...].astype(f32)
    for j in range(1, 4):
        total = total + refs[j][...].astype(f32)
    sums = total[:SLOTS]
    if not first:
        line = jnp.sum(total[SLOTS : SLOTS + 8, :HALF], axis=0, keepdims=True)
        rs_line = lax.rsqrt(line * (1.0 / D) + norm_eps)
        r0 = lax.broadcasted_iota(jnp.int32, (SLOTS, HALF), 0)
        r1 = lax.broadcasted_iota(jnp.int32, (SLOTS, HALF), 1)
        rs = jnp.sum(jnp.where(r0 == r1, rs_line, 0.0), axis=1, keepdims=True)
        sums = sums * rs
    t0, t1, t2 = sums[:, :128], sums[:, 128:256], sums[:, 256:]
    a0 = jax.nn.silu(t0) * t2
    a1 = jax.nn.silu(t1) * pltpu.roll(t1, 64, 1)
    half = SLOTS // 2
    lane = lax.broadcasted_iota(jnp.int32, (half, 128), 1)
    middle = jnp.where(lane < 64, a1[:half], pltpu.roll(a1[half:], 64, 1))
    out_ref[...] = jnp.concatenate([a0[:half], middle, a0[half:]], axis=1).astype(bf16)


def activate(first, p):
    return pl.pallas_call(
        lambda *refs: act_kernel(first, *refs),
        out_shape=jax.ShapeDtypeStruct((SLOTS // 2, 384), bf16),
        compiler_params=pltpu.CompilerParams(vmem_limit_bytes=8 << 20),
        cost_estimate=busy(0.3),
        name="activate",
    )(*p)


def down_kernel(step, ids_ref, *refs):
    core, z = ids_ref[0], ids_ref[4]
    a_refs, tab_ref, w_refs = refs[:4], refs[4], refs[5:8]
    w_refs = [w_refs[0].at[core], w_refs[0].at[1 - core], *w_refs[1:]]
    send_ref, keep_ref, ys = refs[8:]
    half = SLOTS // 2
    lane = lax.broadcasted_iota(jnp.int32, (half, 128), 1)
    sums = [jnp.zeros((SLOTS, HALF), f32)] * 4
    for d in range(4):
        block = a_refs[d][...].astype(f32)
        middle = block[:, 128:256]
        low = jnp.concatenate([block[:, :128], jnp.where(lane < 64, middle, 0.0)], axis=1)
        high = jnp.concatenate([block[:, 256:], jnp.where(lane < 64, 0.0, middle)], axis=1)
        act = jnp.concatenate([low, high], axis=0).astype(bf16)
        for b in range(4):
            start = 2 * UNIT_HALF if b < 2 else 0
            at = pl.multiple_of(((z - d + 4) % 4) * UNITS + start, 64)
            after = pl.multiple_of(((z - d + 4) % 4) * UNITS + start + 128, 64)
            w = jnp.concatenate([w_refs[b][pl.ds(at, UNITS), :], w_refs[b][pl.ds(after, 64), :]], axis=0)
            sums[b] = sums[b] + dot(act, w)
    for b, at in enumerate(block_at(ids_ref)):
        ys[at] = sums[b].astype(bf16)
    slot = lax.broadcasted_iota(jnp.int32, (128, HALF), 1).astype(f32)
    for ref, part in ((send_ref, 1 - core), (keep_ref, core)):
        tab = tab_ref[pl.ds(pl.multiple_of(part * 128, 128), 128), :]
        hot = jnp.where(slot == tab[:, 64 + step : 65 + step], 1.0, 0.0)[:, :SLOTS].astype(bf16)
        for b in range(4):
            rows = dot(hot, ys[b]) * tab[:, step : step + 1]
            ref[:, b * HALF : (b + 1) * HALF] = rows.astype(ref.dtype)


def down(step, ids, acts, tab, weights):
    return pl.pallas_call(
        lambda *refs: down_kernel(step, *refs),
        in_specs=[pl.BlockSpec(memory_space=pltpu.SMEM)] + [pl.BlockSpec()] * 8,
        out_shape=[
            jax.ShapeDtypeStruct((128, WIDTH), bf16),
            jax.ShapeDtypeStruct((128, WIDTH), f32),
        ],
        scratch_shapes=[pltpu.VMEM((4, SLOTS, HALF), bf16)],
        compiler_params=pltpu.CompilerParams(vmem_limit_bytes=10 << 20),
        cost_estimate=busy(1.9, 3000000),
        name="down",
    )(ids, *acts, tab, *weights)


def pair_kernel(keep_ref, other_ref, out_ref):
    out_ref[...] = (keep_ref[...] + other_ref[...].astype(f32)).astype(bf16)


def pair(keep, other):
    return pl.pallas_call(
        pair_kernel,
        out_shape=jax.ShapeDtypeStruct((128, WIDTH), bf16),
        compiler_params=pltpu.CompilerParams(vmem_limit_bytes=4 << 20),
        name="pair",
    )(keep, other)


def residual_kernel(p_ref, stream_ref, gain_ref, new_ref, x_ref):
    total = p_ref[0].astype(f32)
    for j in range(1, 16):
        total = total + p_ref[j].astype(f32)
    stream = stream_ref[...] + total
    new_ref[...] = stream
    hi, mid, low = split3(jnp.sum(stream * stream, axis=1, keepdims=True))
    lane = lax.broadcasted_iota(jnp.int32, (8, 128), 1)
    parts = jnp.where(
        lane == 0,
        hi.astype(f32),
        jnp.where(lane == 1, mid.astype(f32), jnp.where(lane == 2, low.astype(f32), 0.0)),
    )
    row = jnp.concatenate([stream * gain_ref[...], parts], axis=1).astype(bf16)
    for j in range(16):
        x_ref[j] = row


def residual(p, stream, gain):
    return pl.pallas_call(
        residual_kernel,
        out_shape=[
            jax.ShapeDtypeStruct((8, WIDTH), f32),
            jax.ShapeDtypeStruct((16, 8, EXT), bf16),
        ],
        compiler_params=pltpu.CompilerParams(vmem_limit_bytes=4 << 20),
        name="residual",
    )(p, stream, gain)


def last_kernel(p_ref, stream_ref, before_ref, change_ref):
    total = p_ref[0].astype(f32)
    for j in range(1, 16):
        total = total + p_ref[j].astype(f32)
    change_ref[...] = (stream_ref[...] - before_ref[...] + total).astype(bf16)


def last(p, stream, before):
    return pl.pallas_call(
        last_kernel,
        out_shape=jax.ShapeDtypeStruct((8, WIDTH), bf16),
        compiler_params=pltpu.CompilerParams(vmem_limit_bytes=4 << 20),
        name="last",
    )(p, stream, before)


def place_kernel(ids_ref, whole_ref, hidden_ref, out_ref):
    z = ids_ref[4]
    for a in range(4):
        for h in range(2):
            block = whole_ref[((a + z) % 4) * 2 + h].astype(f32)
            for far in range(2):
                to = far * 2048 + a * 512
                rows = hidden_ref[:, to : to + 512].astype(f32)[h * 8 : h * 8 + 8]
                out_ref[h * 8 : h * 8 + 8, to : to + 512] = (
                    rows + block[:, far * 512 : far * 512 + 512]
                )


def place_rows(ids, whole, hidden):
    return pl.pallas_call(
        place_kernel,
        in_specs=[pl.BlockSpec(memory_space=pltpu.SMEM), pl.BlockSpec(), pl.BlockSpec()],
        out_shape=jax.ShapeDtypeStruct((ROWS_DEV, D), f32),
        compiler_params=pltpu.CompilerParams(vmem_limit_bytes=4 << 20),
        name="place_rows",
    )(ids, whole, hidden)


def exchange(x, axes):
    return lax.all_to_all(x, axes, split_axis=0, concat_axis=0, tiled=True)


def swap(x):
    return lax.ppermute(x, "c", [(0, 1), (1, 0)])


def around(x, d):
    return lax.ppermute(x, "z", [(i, (i + d) % 4) for i in range(4)])


def body(trainer_weights, hidden_in, norm_gain, routing, gate_weights):
    core, far, z = lax.axis_index("c"), lax.axis_index("xh"), lax.axis_index("z")
    tp = lax.axis_index(T)
    ids = jnp.stack([core, tp, 2 * tp + core, far, z, far * 8 + tp]).astype(jnp.int32)
    gain = lax.dynamic_index_in_dim(norm_gain.reshape(2, 4, 512), z, 1, keepdims=False)
    gain = gain.reshape(1, WIDTH)

    lines = lambda v: jnp.transpose(v, (0, 2, 1)).reshape(STEPS * TOPK, ROWS_DEV)
    pieces = first_rows(hidden_in, lines(routing), lines(gate_weights))
    pieces_far = lax.ppermute(pieces, "xh", [(0, 1), (1, 0)])

    near_out, diag_out = quantize_far(ids, trainer_weights)
    near_out, diag_out, pieces_far = lax.optimization_barrier((near_out, diag_out, pieces_far))
    gu_near = lax.ppermute(near_out, "xh", [(0, 1), (1, 0)])
    gu_diag = lax.ppermute(diag_out, ("xh", "c"), [(0, 3), (3, 0), (1, 2), (2, 1)])
    rows = spread(ids, pieces, pieces_far)
    rows = jnp.stack([rows[0]] + [around(rows[d], d) for d in (1, 2, 3)])
    mixed, near_out, diag_out = quantize_rest(ids, trainer_weights)
    here, rows_other = lax.optimization_barrier((hold(exchange(mixed, "c")), swap(rows)))
    x, stream, tab = prepare(ids, rows, rows_other, gain)

    near_out, diag_out, gu_near, gu_diag, x, stream, tab = lax.optimization_barrier(
        (near_out, diag_out, gu_near, gu_diag, x, stream, tab)
    )
    down_near = lax.ppermute(near_out, "xh", [(0, 1), (1, 0)])
    down_diag = lax.ppermute(diag_out, ("xh", "c"), [(0, 3), (3, 0), (1, 2), (2, 1)])

    x, before = [x], stream
    for step in range(STEPS):
        part = gate_up(step, ids, x, tab, [here, gu_near, gu_diag])
        if step == 0:
            gu_near, gu_diag, *part = lax.optimization_barrier((gu_near, gu_diag, *part))
            gu_near, gu_diag = hold(gu_near), hold(gu_diag)
        part = [part[0]] + [around(part[d], d) for d in (1, 2, 3)]
        act = activate(step == 0, part)
        acts = [act] + [around(act, d) for d in (1, 2, 3)]
        send, keep = down(step, ids, acts, tab, [here, down_near, down_diag])
        sums = exchange(pair(keep, swap(send)).reshape(16, 8, WIDTH), XT)
        if step < STEPS - 1:
            stream, rows = residual(sums, stream, gain)
            rows = exchange(rows, XT).reshape(128, EXT)
            x = [rows, swap(rows)]
        else:
            change = last(sums, stream, before)

    turn = [(a * 8 + t, ((t // 2 - a) % 4) * 8 + t) for a in range(4) for t in range(8)]
    mine = lax.ppermute(change, ("z", "xl", "y"), turn)
    whole = exchange(jnp.broadcast_to(mine[None], (8, 8, WIDTH)), T)
    return place_rows(ids, whole, hidden_in)


def solution(mesh):
    fine = Mesh(mesh.devices.reshape(2, 4, 2, 2, 4), ALL)
    fsdp, tp = ("xh", "z", "c"), ("xl", "y")
    in_specs = (
        P(tp, None, None, fsdp),
        P(fsdp, None),
        P(),
        P(None, fsdp, None),
        P(None, fsdp, None),
    )
    return jax.shard_map(
        body, mesh=fine, in_specs=in_specs, out_specs=P(fsdp, None), check_vma=False
    )
```

```python
import jax
import jax.numpy as jnp
from jax import lax
from jax.experimental import pallas as pl
from jax.experimental.pallas import tpu as pltpu
from jax.sharding import Mesh, PartitionSpec as P

D = 4096
FF = 1536
TOPK = 8
EXPERTS = 16
QB = 128
STEPS = 4
CAP = 11
ROWS_DEV = 16
ROWS = 256
SLOTS = 16 * CAP
UNIT_HALF = 768
WIDTH = 1024
HALF = 256
UNITS = 192
PAY = 184
EXT = 1152
FIRST = 1280

XZ = ("xh", "z")
XT = ("xh", "xl", "y")
T = ("xl", "y")
ALL = ("xh", "z", "c", "xl", "y")

norm_eps = 1e-06
scale_eps = 1e-06
code_limit = 448.0
smallest_normal = 0.015625
f32 = jnp.float32
bf16 = jnp.bfloat16

NN = (((1,), (0,)), ((), ()))
NT = (((1,), (1,)), ((), ()))


def dot(a, b, dims=NN):
    return lax.dot_general(a, b, dims, preferred_element_type=f32)


def busy(us, moved=0):
    return pl.CostEstimate(flops=int(us * 1.15e9), bytes_accessed=moved, transcendentals=0)


def split3(v):
    hi = v.astype(bf16)
    rest = v - hi.astype(f32)
    mid = rest.astype(bf16)
    low = (rest - mid.astype(f32)).astype(bf16)
    return hi, mid, low


def float_code(v):
    big = v * 1048577.0
    fine = big - (big - v)
    coarse = (v + 24576.0) - 24576.0
    return jnp.where(jnp.abs(v) < smallest_normal, coarse, fine)


def quant_block(tile):
    top = jnp.max(jnp.abs(tile), axis=0, keepdims=True).astype(f32)
    top = jnp.max(top, axis=1, keepdims=True) + scale_eps
    tile = tile.astype(f32)
    scale = top / code_limit
    return (float_code(tile * (1.0 / scale)) * scale).astype(bf16)


def quant_gate_up(src, out_ref, group):
    for m in range(2):
        for q in range(3):
            for h in range(2):
                cols = slice(h * QB, (h + 1) * QB)
                back = quant_block(src[m, q * QB : (q + 1) * QB, cols])
                for g in range(2):
                    unit = q * 2 + g
                    j, part = unit // 3, unit % 3
                    if m == 0:
                        to = part * 64
                    elif part < 2:
                        to = 256 + part * 64
                    else:
                        to = 192
                    to = group * 768 + j * 384 + to
                    out_ref[to : to + 64, cols] = back[g * 64 : g * 64 + 64]


def quant_down(src, out_ref, at, blocks):
    for q in range(blocks):
        for h in range(2):
            cols = slice(h * QB, (h + 1) * QB)
            back = quant_block(src[q * QB : (q + 1) * QB, cols])
            out_ref[at + q * QB : at + (q + 1) * QB, cols] = back


def quant_far_kernel(ids_ref, w_ref, near_ref, diag_ref, buf, sem):
    core, half = ids_ref[0], 1 - ids_ref[3]
    copies = []
    for p in range(2):
        for g in range(2):
            expert = core if p == 0 else 1 - core
            at = pl.multiple_of(half * UNIT_HALF + g * 384, 128)
            src = w_ref.at[expert, pl.ds(0, 2), pl.ds(at, 384), :]
            copies.append(pltpu.make_async_copy(src, buf.at[p * 2 + g], sem.at[p * 2 + g]))
    for copy in copies:
        copy.start()
    for p in range(2):
        for g in range(2):
            copies[p * 2 + g].wait()
            quant_gate_up(buf.at[p * 2 + g], diag_ref if p else near_ref, g)


def quantize_far(ids, w):
    out = jax.ShapeDtypeStruct((2 * UNIT_HALF, HALF), bf16)
    return pl.pallas_call(
        quant_far_kernel,
        in_specs=[
            pl.BlockSpec(memory_space=pltpu.SMEM),
            pl.BlockSpec(memory_space=pltpu.HBM),
        ],
        out_shape=[out, out],
        scratch_shapes=[pltpu.VMEM((4, 2, 384, HALF), bf16), pltpu.SemaphoreType.DMA((4,))],
        compiler_params=pltpu.CompilerParams(vmem_limit_bytes=60 << 20),
        name="quantize_far",
    )(ids, w)


def quant_rest_kernel(
    ids_ref, w_ref, pair_ref, near_ref, diag_ref, buf, sem, down_buf, down_sem
):
    core, half = ids_ref[0], ids_ref[3]
    copies = []
    for p in range(2):
        expert = core if p == 0 else 1 - core
        for g in range(2):
            at = pl.multiple_of(half * UNIT_HALF + g * 384, 128)
            src = w_ref.at[expert, :, pl.ds(at, 384), :]
            copies.append(pltpu.make_async_copy(src, buf.at[p * 2 + g], sem.at[p * 2 + g]))
    down_copies = []
    for p in range(2):
        expert = core if p == 0 else 1 - core
        at = pl.multiple_of((1 - half) * UNIT_HALF, 128)
        src = w_ref.at[expert, 2, pl.ds(at, UNIT_HALF), :]
        down_copies.append(pltpu.make_async_copy(src, down_buf.at[p], down_sem.at[p]))
    for copy in copies + down_copies:
        copy.start()
    for p in range(2):
        out_ref = pair_ref.at[1 - core if p else core]
        for g in range(2):
            copies[p * 2 + g].wait()
            quant_gate_up(buf.at[p * 2 + g], out_ref, g)
            quant_down(buf.at[p * 2 + g, 2], out_ref, 2 * UNIT_HALF + g * 384, 3)
    for p in range(2):
        down_copies[p].wait()
        quant_down(down_buf.at[p], diag_ref if p else near_ref, 0, 6)


def keep_kernel(mixed_ref, out_ref):
    out_ref[...] = mixed_ref[...]


def hold(mixed):
    return pl.pallas_call(
        keep_kernel,
        out_shape=jax.ShapeDtypeStruct(mixed.shape, bf16),
        compiler_params=pltpu.CompilerParams(vmem_limit_bytes=12 << 20),
        name="hold",
    )(mixed)


def quantize_rest(ids, w):
    whole = jax.ShapeDtypeStruct((2, 3 * UNIT_HALF, HALF), bf16)
    third = jax.ShapeDtypeStruct((UNIT_HALF, HALF), bf16)
    return pl.pallas_call(
        quant_rest_kernel,
        in_specs=[
            pl.BlockSpec(memory_space=pltpu.SMEM),
            pl.BlockSpec(memory_space=pltpu.HBM),
        ],
        out_shape=[whole, third, third],
        scratch_shapes=[
            pltpu.VMEM((4, 3, 384, HALF), bf16),
            pltpu.SemaphoreType.DMA((4,)),
            pltpu.VMEM((2, UNIT_HALF, HALF), bf16),
            pltpu.SemaphoreType.DMA((2,)),
        ],
        compiler_params=pltpu.CompilerParams(vmem_limit_bytes=16 << 20),
        name="quantize_rest",
    )(ids, w)


def first_kernel(*refs):
    sources, (out_ref, table), held, sem = refs[:3], refs[3:5], refs[5:8], refs[8]
    copies = [pltpu.make_async_copy(a, b, sem.at[i]) for i, (a, b) in enumerate(zip(sources, held))]
    for copy in copies:
        copy.start()
    for copy in copies:
        copy.wait()
    hidden_ref, routing_ref, gates_ref = held
    hidden = hidden_ref[...].astype(f32)
    mean = jnp.sum(hidden * hidden, axis=1, keepdims=True) * (1.0 / D)
    hi, mid, low = split3(lax.rsqrt(mean + norm_eps))
    lane = lax.broadcasted_iota(jnp.int32, (ROWS_DEV, 128), 1)
    rs = jnp.where(
        lane == 0,
        hi.astype(f32),
        jnp.where(lane == 1, mid.astype(f32), jnp.where(lane == 2, low.astype(f32), 0.0)),
    ).astype(bf16)
    table[...] = jnp.zeros((128, 128), f32)
    table[0:32, :ROWS_DEV] = routing_ref[...].astype(f32)
    for i, part in enumerate(split3(gates_ref[...])):
        table[32 + 32 * i : 64 + 32 * i, :ROWS_DEV] = part.astype(f32)
    named = table[...].T[:ROWS_DEV].astype(bf16)
    for z in range(4):
        for half in range(2):
            at = half * 2048 + z * 512
            out_ref[z, :, half * 512 : half * 512 + 512] = hidden_ref[:, at : at + 512]
        out_ref[z, :, WIDTH : WIDTH + 128] = named
        out_ref[z, :, WIDTH + 128 :] = rs


def first_rows(hidden, routing, gates):
    return pl.pallas_call(
        first_kernel,
        in_specs=[pl.BlockSpec(memory_space=pltpu.HBM)] * 3,
        out_shape=jax.ShapeDtypeStruct((4, ROWS_DEV, FIRST), bf16),
        scratch_shapes=[
            pltpu.VMEM((128, 128), f32),
            pltpu.VMEM((ROWS_DEV, D), bf16),
            pltpu.VMEM((STEPS * TOPK, ROWS_DEV), jnp.int32),
            pltpu.VMEM((STEPS * TOPK, ROWS_DEV), f32),
            pltpu.SemaphoreType.DMA((3,)),
        ],
        compiler_params=pltpu.CompilerParams(vmem_limit_bytes=60 << 20),
        name="first_rows",
    )(hidden, routing, gates)


def spread_kernel(ids_ref, own_ref, far_ref, *out_refs):
    half, z = ids_ref[3], ids_ref[4]
    for d in range(4):
        at = (z + d) % 4
        out_refs[d][half] = own_ref[at]
        out_refs[d][1 - half] = far_ref[at]


def spread(ids, own, far):
    return pl.pallas_call(
        spread_kernel,
        in_specs=[pl.BlockSpec(memory_space=pltpu.SMEM)] + [pl.BlockSpec()] * 2,
        out_shape=[jax.ShapeDtypeStruct((2, ROWS_DEV, FIRST), bf16)] * 4,
        compiler_params=pltpu.CompilerParams(vmem_limit_bytes=4 << 20),
        name="spread",
    )(ids, own, far)


def prepare_kernel(ids_ref, own_ref, other_ref, gain_ref, x_ref, stream_ref, tab_ref, rows, tab):
    core, tp, expert, half, z = [ids_ref[i] for i in range(5)]
    for d in range(4):
        for far in range(2):
            at = (far * 4 + (z - d + 4) % 4) * 16
            rows[pl.ds(pl.multiple_of(core * 128 + at, 16), 16), :] = own_ref[d, far]
            rows[pl.ds(pl.multiple_of((1 - core) * 128 + at, 16), 16), :] = other_ref[d, far]
    named = rows[:, WIDTH : WIDTH + 128].astype(f32)
    gates = pltpu.roll(named, 96, 1) + pltpu.roll(named, 64, 1) + pltpu.roll(named, 32, 1)
    lane = lax.broadcasted_iota(jnp.int32, (ROWS, 128), 1)
    match = jnp.where((named == expert.astype(f32)) & (lane < 32), 1.0, 0.0)
    weighted = match * gates
    group = lane // TOPK
    mask = jnp.zeros((ROWS, 128), f32)
    weight = jnp.zeros((ROWS, 128), f32)
    for s in range(STEPS):
        here = jnp.sum(jnp.where(group == s, match, 0.0), axis=1, keepdims=True)
        gate = jnp.sum(jnp.where(group == s, weighted, 0.0), axis=1, keepdims=True)
        mask = jnp.where(lane == s, here, mask)
        weight = jnp.where(lane == s, gate, weight)
    r0 = lax.broadcasted_iota(jnp.int32, (ROWS, ROWS), 0)
    r1 = lax.broadcasted_iota(jnp.int32, (ROWS, ROWS), 1)
    before = jnp.where(r1 < r0, 1.0, 0.0).astype(bf16)
    place = jnp.where(mask > 0.0, dot(before, mask.astype(bf16)), -1.0)
    tab[...] = jnp.where(lane < 64, weight, pltpu.roll(place, 64, 1))
    for c in range(2):
        for far in range(2):
            for u in range(4):
                at = pl.multiple_of(c * 128 + far * 64 + ((u - z + 4) % 4) * 16, 16)
                to = slice(c * 128 + far * 64 + u * 16, c * 128 + far * 64 + u * 16 + 16)
                block = rows[pl.ds(at, 16), :].astype(f32)
                rs = jnp.sum(block[:, WIDTH + 128 :], axis=1, keepdims=True)
                x_ref[to, :] = (block[:, :WIDTH] * rs * gain_ref[...]).astype(bf16)
                tab_ref[to, :] = tab[pl.ds(at, 16), :]
    at = core * 128 + half * 64 + ((tp // 2 - z + 4) % 4) * 16
    mine = rows[pl.ds(pl.multiple_of(at, 16), 16), :WIDTH].astype(f32)
    stream_ref[...] = jnp.where(tp % 2 == 0, mine[:8], mine[8:])


def prepare(ids, own, other, gain):
    return pl.pallas_call(
        prepare_kernel,
        in_specs=[pl.BlockSpec(memory_space=pltpu.SMEM)] + [pl.BlockSpec()] * 3,
        out_shape=[
            jax.ShapeDtypeStruct((ROWS, WIDTH), bf16),
            jax.ShapeDtypeStruct((8, WIDTH), f32),
            jax.ShapeDtypeStruct((ROWS, 128), f32),
        ],
        scratch_shapes=[pltpu.VMEM((ROWS, FIRST), bf16), pltpu.VMEM((ROWS, 128), f32)],
        compiler_params=pltpu.CompilerParams(vmem_limit_bytes=8 << 20),
        name="prepare",
    )(ids, own, other, gain)


def one_hot(tab_ref, step):
    slot = lax.broadcasted_iota(jnp.int32, (ROWS, ROWS), 1).astype(f32)
    return jnp.where(slot == tab_ref[:, 64 + step : 65 + step], 1.0, 0.0)


def block_at(ids_ref):
    core, half = ids_ref[0], ids_ref[3]
    far = 1 - half
    return [half * 2 + core, half * 2 + 1 - core, far * 2 + core, far * 2 + 1 - core]


def gate_up_kernel(step, ids_ref, *refs):
    core, z = ids_ref[0], ids_ref[4]
    first = step == 0
    if first:
        x_ref, *refs = refs
    else:
        own_ref, other_ref, *refs = refs
    tab_ref, *refs = refs
    w_refs, p_refs, xs = refs[:3], refs[3:7], refs[7]
    w_refs = [w_refs[0].at[core], w_refs[0].at[1 - core], *w_refs[1:]]
    if not first:
        x_ref = refs[8]
        x_ref[pl.ds(pl.multiple_of(core * 128, 128), 128), :] = own_ref[...]
        x_ref[pl.ds(pl.multiple_of((1 - core) * 128, 128), 128), :] = other_ref[...]
    hot = one_hot(tab_ref, step)
    picked = dot(hot.T[:SLOTS].astype(bf16), x_ref[:, :WIDTH]).astype(bf16)
    for b in range(4):
        xs[b] = picked[:, b * HALF : (b + 1) * HALF]
    if first:
        tail = jnp.zeros((PAY - SLOTS, 384), bf16)
    else:
        squares = jnp.sum(x_ref[:, WIDTH:].astype(f32), axis=1, keepdims=True)
        line = jnp.sum(hot * squares, axis=0, keepdims=True)
        line = jnp.concatenate([line, jnp.zeros((1, 128), f32)], axis=1)
        hi, mid, low = split3(line)
        at = lax.broadcasted_iota(jnp.int32, (PAY - SLOTS, 384), 0)
        tail = jnp.where(
            at == 0,
            hi.astype(f32),
            jnp.where(at == 1, mid.astype(f32), jnp.where(at == 2, low.astype(f32), 0.0)),
        ).astype(bf16)
    ours = [xs[at] for at in block_at(ids_ref)]
    for d in range(4):
        at = pl.multiple_of(((z + d) % 4) * 384, 128)
        part = dot(ours[0], w_refs[0][pl.ds(at, 384), :], NT)
        for b in range(1, 4):
            part = part + dot(ours[b], w_refs[b][pl.ds(at, 384), :], NT)
        p_refs[d][:SLOTS, :] = part.astype(bf16)
        p_refs[d][SLOTS:, :] = tail


def gate_up(step, ids, x, tab, weights):
    scratch = [pltpu.VMEM((4, SLOTS, HALF), bf16)]
    if step > 0:
        scratch.append(pltpu.VMEM((ROWS, EXT), bf16))
    return pl.pallas_call(
        lambda *refs: gate_up_kernel(step, *refs),
        in_specs=[pl.BlockSpec(memory_space=pltpu.SMEM)] + [pl.BlockSpec()] * (len(x) + 4),
        out_shape=[jax.ShapeDtypeStruct((PAY, 384), bf16)] * 4,
        scratch_shapes=scratch,
        compiler_params=pltpu.CompilerParams(vmem_limit_bytes=10 << 20),
        cost_estimate=busy(2.2, 4600000),
        name="gate_up",
    )(ids, *x, tab, *weights)


def act_kernel(first, *refs):
    out_ref = refs[4]
    total = refs[0][...].astype(f32)
    for j in range(1, 4):
        total = total + refs[j][...].astype(f32)
    sums = total[:SLOTS]
    if not first:
        line = jnp.sum(total[SLOTS : SLOTS + 8, :HALF], axis=0, keepdims=True)
        rs_line = lax.rsqrt(line * (1.0 / D) + norm_eps)
        r0 = lax.broadcasted_iota(jnp.int32, (SLOTS, HALF), 0)
        r1 = lax.broadcasted_iota(jnp.int32, (SLOTS, HALF), 1)
        rs = jnp.sum(jnp.where(r0 == r1, rs_line, 0.0), axis=1, keepdims=True)
        sums = sums * rs
    t0, t1, t2 = sums[:, :128], sums[:, 128:256], sums[:, 256:]
    a0 = jax.nn.silu(t0) * t2
    a1 = jax.nn.silu(t1) * pltpu.roll(t1, 64, 1)
    half = SLOTS // 2
    lane = lax.broadcasted_iota(jnp.int32, (half, 128), 1)
    middle = jnp.where(lane < 64, a1[:half], pltpu.roll(a1[half:], 64, 1))
    out_ref[...] = jnp.concatenate([a0[:half], middle, a0[half:]], axis=1).astype(bf16)


def activate(first, p):
    return pl.pallas_call(
        lambda *refs: act_kernel(first, *refs),
        out_shape=jax.ShapeDtypeStruct((SLOTS // 2, 384), bf16),
        compiler_params=pltpu.CompilerParams(vmem_limit_bytes=8 << 20),
        cost_estimate=busy(0.3),
        name="activate",
    )(*p)


def down_kernel(step, ids_ref, *refs):
    core, z = ids_ref[0], ids_ref[4]
    a_refs, tab_ref, w_refs = refs[:4], refs[4], refs[5:8]
    w_refs = [w_refs[0].at[core], w_refs[0].at[1 - core], *w_refs[1:]]
    send_ref, keep_ref, ys = refs[8:]
    half = SLOTS // 2
    lane = lax.broadcasted_iota(jnp.int32, (half, 128), 1)
    sums = [jnp.zeros((SLOTS, HALF), f32)] * 4
    for d in range(4):
        block = a_refs[d][...].astype(f32)
        middle = block[:, 128:256]
        low = jnp.concatenate([block[:, :128], jnp.where(lane < 64, middle, 0.0)], axis=1)
        high = jnp.concatenate([block[:, 256:], jnp.where(lane < 64, 0.0, middle)], axis=1)
        act = jnp.concatenate([low, high], axis=0).astype(bf16)
        for b in range(4):
            start = 2 * UNIT_HALF if b < 2 else 0
            at = pl.multiple_of(((z - d + 4) % 4) * UNITS + start, 64)
            after = pl.multiple_of(((z - d + 4) % 4) * UNITS + start + 128, 64)
            w = jnp.concatenate([w_refs[b][pl.ds(at, UNITS), :], w_refs[b][pl.ds(after, 64), :]], axis=0)
            sums[b] = sums[b] + dot(act, w)
    for b, at in enumerate(block_at(ids_ref)):
        ys[at] = sums[b].astype(bf16)
    slot = lax.broadcasted_iota(jnp.int32, (128, HALF), 1).astype(f32)
    for ref, part in ((send_ref, 1 - core), (keep_ref, core)):
        tab = tab_ref[pl.ds(pl.multiple_of(part * 128, 128), 128), :]
        hot = jnp.where(slot == tab[:, 64 + step : 65 + step], 1.0, 0.0)[:, :SLOTS].astype(bf16)
        for b in range(4):
            rows = dot(hot, ys[b]) * tab[:, step : step + 1]
            ref[:, b * HALF : (b + 1) * HALF] = rows.astype(ref.dtype)


def down(step, ids, acts, tab, weights):
    return pl.pallas_call(
        lambda *refs: down_kernel(step, *refs),
        in_specs=[pl.BlockSpec(memory_space=pltpu.SMEM)] + [pl.BlockSpec()] * 8,
        out_shape=[
            jax.ShapeDtypeStruct((128, WIDTH), bf16),
            jax.ShapeDtypeStruct((128, WIDTH), f32),
        ],
        scratch_shapes=[pltpu.VMEM((4, SLOTS, HALF), bf16)],
        compiler_params=pltpu.CompilerParams(vmem_limit_bytes=10 << 20),
        cost_estimate=busy(1.9, 3000000),
        name="down",
    )(ids, *acts, tab, *weights)


def pair_kernel(keep_ref, other_ref, out_ref):
    out_ref[...] = (keep_ref[...] + other_ref[...].astype(f32)).astype(bf16)


def pair(keep, other):
    return pl.pallas_call(
        pair_kernel,
        out_shape=jax.ShapeDtypeStruct((128, WIDTH), bf16),
        compiler_params=pltpu.CompilerParams(vmem_limit_bytes=4 << 20),
        name="pair",
    )(keep, other)


def residual_kernel(p_ref, stream_ref, gain_ref, new_ref, x_ref):
    total = p_ref[0].astype(f32)
    for j in range(1, 16):
        total = total + p_ref[j].astype(f32)
    stream = stream_ref[...] + total
    new_ref[...] = stream
    hi, mid, low = split3(jnp.sum(stream * stream, axis=1, keepdims=True))
    lane = lax.broadcasted_iota(jnp.int32, (8, 128), 1)
    parts = jnp.where(
        lane == 0,
        hi.astype(f32),
        jnp.where(lane == 1, mid.astype(f32), jnp.where(lane == 2, low.astype(f32), 0.0)),
    )
    row = jnp.concatenate([stream * gain_ref[...], parts], axis=1).astype(bf16)
    for j in range(16):
        x_ref[j] = row


def residual(p, stream, gain):
    return pl.pallas_call(
        residual_kernel,
        out_shape=[
            jax.ShapeDtypeStruct((8, WIDTH), f32),
            jax.ShapeDtypeStruct((16, 8, EXT), bf16),
        ],
        compiler_params=pltpu.CompilerParams(vmem_limit_bytes=4 << 20),
        name="residual",
    )(p, stream, gain)


def last_kernel(p_ref, stream_ref, before_ref, change_ref):
    total = p_ref[0].astype(f32)
    for j in range(1, 16):
        total = total + p_ref[j].astype(f32)
    change_ref[...] = (stream_ref[...] - before_ref[...] + total).astype(bf16)


def last(p, stream, before):
    return pl.pallas_call(
        last_kernel,
        out_shape=jax.ShapeDtypeStruct((8, WIDTH), bf16),
        compiler_params=pltpu.CompilerParams(vmem_limit_bytes=4 << 20),
        name="last",
    )(p, stream, before)


def place_kernel(ids_ref, whole_ref, hidden_ref, out_ref):
    z = ids_ref[4]
    for a in range(4):
        for h in range(2):
            block = whole_ref[((a + z) % 4) * 2 + h].astype(f32)
            for far in range(2):
                to = far * 2048 + a * 512
                rows = hidden_ref[:, to : to + 512].astype(f32)[h * 8 : h * 8 + 8]
                out_ref[h * 8 : h * 8 + 8, to : to + 512] = (
                    rows + block[:, far * 512 : far * 512 + 512]
                )


def place_rows(ids, whole, hidden):
    return pl.pallas_call(
        place_kernel,
        in_specs=[pl.BlockSpec(memory_space=pltpu.SMEM), pl.BlockSpec(), pl.BlockSpec()],
        out_shape=jax.ShapeDtypeStruct((ROWS_DEV, D), f32),
        compiler_params=pltpu.CompilerParams(vmem_limit_bytes=4 << 20),
        name="place_rows",
    )(ids, whole, hidden)


def exchange(x, axes):
    return lax.all_to_all(x, axes, split_axis=0, concat_axis=0, tiled=True)


def swap(x):
    return lax.ppermute(x, "c", [(0, 1), (1, 0)])


def around(x, d):
    return lax.ppermute(x, "z", [(i, (i + d) % 4) for i in range(4)])


def body(trainer_weights, hidden_in, norm_gain, routing, gate_weights):
    core, far, z = lax.axis_index("c"), lax.axis_index("xh"), lax.axis_index("z")
    tp = lax.axis_index(T)
    ids = jnp.stack([core, tp, 2 * tp + core, far, z, far * 8 + tp]).astype(jnp.int32)
    gain = lax.dynamic_index_in_dim(norm_gain.reshape(2, 4, 512), z, 1, keepdims=False)
    gain = gain.reshape(1, WIDTH)

    lines = lambda v: jnp.transpose(v, (0, 2, 1)).reshape(STEPS * TOPK, ROWS_DEV)
    pieces = first_rows(hidden_in, lines(routing), lines(gate_weights))
    pieces_far = lax.ppermute(pieces, "xh", [(0, 1), (1, 0)])

    near_out, diag_out = quantize_far(ids, trainer_weights)
    near_out, diag_out, pieces_far = lax.optimization_barrier((near_out, diag_out, pieces_far))
    gu_near = lax.ppermute(near_out, "xh", [(0, 1), (1, 0)])
    gu_diag = lax.ppermute(diag_out, ("xh", "c"), [(0, 3), (3, 0), (1, 2), (2, 1)])
    rows = spread(ids, pieces, pieces_far)
    rows = jnp.stack([rows[0]] + [around(rows[d], d) for d in (1, 2, 3)])
    mixed, near_out, diag_out = quantize_rest(ids, trainer_weights)
    here, rows_other = lax.optimization_barrier((hold(exchange(mixed, "c")), swap(rows)))
    x, stream, tab = prepare(ids, rows, rows_other, gain)

    near_out, diag_out, gu_near, x, stream, tab = lax.optimization_barrier(
        (near_out, diag_out, gu_near, x, stream, tab)
    )
    down_near = lax.ppermute(near_out, "xh", [(0, 1), (1, 0)])
    down_diag = lax.ppermute(diag_out, ("xh", "c"), [(0, 3), (3, 0), (1, 2), (2, 1)])

    x, before = [x], stream
    for step in range(STEPS):
        part = gate_up(step, ids, x, tab, [here, gu_near, gu_diag])
        if step == 0:
            gu_near, gu_diag, *part = lax.optimization_barrier((gu_near, gu_diag, *part))
            gu_near, gu_diag = hold(gu_near), hold(gu_diag)
        part = [part[0]] + [around(part[d], d) for d in (1, 2, 3)]
        act = activate(step == 0, part)
        acts = [act] + [around(act, d) for d in (1, 2, 3)]
        send, keep = down(step, ids, acts, tab, [here, down_near, down_diag])
        sums = exchange(pair(keep, swap(send)).reshape(16, 8, WIDTH), XT)
        if step < STEPS - 1:
            stream, rows = residual(sums, stream, gain)
            rows = exchange(rows, XT).reshape(128, EXT)
            x = [rows, swap(rows)]
        else:
            change = last(sums, stream, before)

    turn = [(a * 8 + t, ((t // 2 - a) % 4) * 8 + t) for a in range(4) for t in range(8)]
    mine = lax.ppermute(change, ("z", "xl", "y"), turn)
    whole = exchange(jnp.broadcast_to(mine[None], (8, 8, WIDTH)), T)
    return place_rows(ids, whole, hidden_in)


def solution(mesh):
    fine = Mesh(mesh.devices.reshape(2, 4, 2, 2, 4), ALL)
    fsdp, tp = ("xh", "z", "c"), ("xl", "y")
    in_specs = (
        P(tp, None, None, fsdp),
        P(fsdp, None),
        P(),
        P(None, fsdp, None),
        P(None, fsdp, None),
    )
    return jax.shard_map(
        body, mesh=fine, in_specs=in_specs, out_specs=P(fsdp, None), check_vma=False
    )
```

```python
import jax
import jax.numpy as jnp
from jax import lax
from jax.experimental import pallas as pl
from jax.experimental.pallas import tpu as pltpu
from jax.sharding import Mesh, PartitionSpec as P

D = 4096
FF = 1536
TOPK = 8
EXPERTS = 16
QB = 128
STEPS = 4
CAP = 11
ROWS_DEV = 16
ROWS = 256
SLOTS = 16 * CAP
UNIT_HALF = 768
WIDTH = 1024
HALF = 256
UNITS = 192
PAY = 184
EXT = 1152
FIRST = 1280

XZ = ("xh", "z")
XT = ("xh", "xl", "y")
T = ("xl", "y")
ALL = ("xh", "z", "c", "xl", "y")

norm_eps = 1e-06
scale_eps = 1e-06
code_limit = 448.0
smallest_normal = 0.015625
f32 = jnp.float32
bf16 = jnp.bfloat16

NN = (((1,), (0,)), ((), ()))
NT = (((1,), (1,)), ((), ()))


def dot(a, b, dims=NN):
    return lax.dot_general(a, b, dims, preferred_element_type=f32)


def busy(us, moved=0):
    return pl.CostEstimate(flops=int(us * 1.15e9), bytes_accessed=moved, transcendentals=0)


def split3(v):
    hi = v.astype(bf16)
    rest = v - hi.astype(f32)
    mid = rest.astype(bf16)
    low = (rest - mid.astype(f32)).astype(bf16)
    return hi, mid, low


def float_code(v):
    big = v * 1048577.0
    fine = big - (big - v)
    coarse = (v + 24576.0) - 24576.0
    return jnp.where(jnp.abs(v) < smallest_normal, coarse, fine)


def quant_block(tile):
    top = jnp.max(jnp.abs(tile), axis=0, keepdims=True).astype(f32)
    top = jnp.max(top, axis=1, keepdims=True) + scale_eps
    tile = tile.astype(f32)
    scale = top / code_limit
    return (float_code(tile * (1.0 / scale)) * scale).astype(bf16)


def quant_gate_up(src, out_ref, group):
    for m in range(2):
        for q in range(3):
            for h in range(2):
                cols = slice(h * QB, (h + 1) * QB)
                back = quant_block(src[m, q * QB : (q + 1) * QB, cols])
                for g in range(2):
                    unit = q * 2 + g
                    j, part = unit // 3, unit % 3
                    if m == 0:
                        to = part * 64
                    elif part < 2:
                        to = 256 + part * 64
                    else:
                        to = 192
                    to = group * 768 + j * 384 + to
                    out_ref[to : to + 64, cols] = back[g * 64 : g * 64 + 64]


def quant_down(src, out_ref, at, blocks):
    for q in range(blocks):
        for h in range(2):
            cols = slice(h * QB, (h + 1) * QB)
            back = quant_block(src[q * QB : (q + 1) * QB, cols])
            out_ref[at + q * QB : at + (q + 1) * QB, cols] = back


def quant_far_kernel(w_ref, near_ref, diag_ref, buf, sem):
    core, half = lax.axis_index("c"), 1 - lax.axis_index("xh")
    copies = []
    for p in range(2):
        for g in range(2):
            expert = core if p == 0 else 1 - core
            at = pl.multiple_of(half * UNIT_HALF + g * 384, 128)
            src = w_ref.at[expert, pl.ds(0, 2), pl.ds(at, 384), :]
            copies.append(pltpu.make_async_copy(src, buf.at[p * 2 + g], sem.at[p * 2 + g]))
    for copy in copies:
        copy.start()
    for p in range(2):
        for g in range(2):
            copies[p * 2 + g].wait()
            quant_gate_up(buf.at[p * 2 + g], diag_ref if p else near_ref, g)


def quantize_far(w):
    out = jax.ShapeDtypeStruct((2 * UNIT_HALF, HALF), bf16)
    return pl.pallas_call(
        quant_far_kernel,
        in_specs=[pl.BlockSpec(memory_space=pltpu.HBM)],
        out_shape=[out, out],
        scratch_shapes=[pltpu.VMEM((4, 2, 384, HALF), bf16), pltpu.SemaphoreType.DMA((4,))],
        compiler_params=pltpu.CompilerParams(vmem_limit_bytes=60 << 20),
        name="quantize_far",
    )(w)


def quant_rest_kernel(
    ids_ref, w_ref, pair_ref, near_ref, diag_ref, buf, sem, down_buf, down_sem
):
    core, half = ids_ref[0], ids_ref[3]
    copies = []
    for p in range(2):
        expert = core if p == 0 else 1 - core
        for g in range(2):
            at = pl.multiple_of(half * UNIT_HALF + g * 384, 128)
            src = w_ref.at[expert, :, pl.ds(at, 384), :]
            copies.append(pltpu.make_async_copy(src, buf.at[p * 2 + g], sem.at[p * 2 + g]))
    down_copies = []
    for p in range(2):
        expert = core if p == 0 else 1 - core
        at = pl.multiple_of((1 - half) * UNIT_HALF, 128)
        src = w_ref.at[expert, 2, pl.ds(at, UNIT_HALF), :]
        down_copies.append(pltpu.make_async_copy(src, down_buf.at[p], down_sem.at[p]))
    for copy in copies + down_copies:
        copy.start()
    for p in range(2):
        out_ref = pair_ref.at[1 - core if p else core]
        for g in range(2):
            copies[p * 2 + g].wait()
            quant_gate_up(buf.at[p * 2 + g], out_ref, g)
            quant_down(buf.at[p * 2 + g, 2], out_ref, 2 * UNIT_HALF + g * 384, 3)
    for p in range(2):
        down_copies[p].wait()
        quant_down(down_buf.at[p], diag_ref if p else near_ref, 0, 6)


def keep_kernel(mixed_ref, out_ref):
    out_ref[...] = mixed_ref[...]


def hold(mixed):
    return pl.pallas_call(
        keep_kernel,
        out_shape=jax.ShapeDtypeStruct(mixed.shape, bf16),
        compiler_params=pltpu.CompilerParams(vmem_limit_bytes=12 << 20),
        name="hold",
    )(mixed)


def quantize_rest(ids, w):
    whole = jax.ShapeDtypeStruct((2, 3 * UNIT_HALF, HALF), bf16)
    third = jax.ShapeDtypeStruct((UNIT_HALF, HALF), bf16)
    return pl.pallas_call(
        quant_rest_kernel,
        in_specs=[
            pl.BlockSpec(memory_space=pltpu.SMEM),
            pl.BlockSpec(memory_space=pltpu.HBM),
        ],
        out_shape=[whole, third, third],
        scratch_shapes=[
            pltpu.VMEM((4, 3, 384, HALF), bf16),
            pltpu.SemaphoreType.DMA((4,)),
            pltpu.VMEM((2, UNIT_HALF, HALF), bf16),
            pltpu.SemaphoreType.DMA((2,)),
        ],
        compiler_params=pltpu.CompilerParams(vmem_limit_bytes=16 << 20),
        name="quantize_rest",
    )(ids, w)


def side_by_side(refs, ids_ref, out_ref, put):
    core, half = ids_ref[0], ids_ref[3]
    far = 1 - half
    at = [half * 2 + core, half * 2 + 1 - core, far * 2 + core, far * 2 + 1 - core]
    for ref, b in zip(refs, at):
        put(ref, out_ref, pl.ds(pl.multiple_of(b * HALF, HALF), HALF))


def gate_up_side_kernel(ids_ref, here_ref, near_ref, diag_ref, out_ref):
    core = ids_ref[0]

    def put(ref, out_ref, cols):
        out_ref[:, cols] = ref[: 2 * UNIT_HALF, :]

    refs = [here_ref.at[core], here_ref.at[1 - core], near_ref, diag_ref]
    side_by_side(refs, ids_ref, out_ref, put)


def gate_up_side(ids, here, near, diag):
    return pl.pallas_call(
        gate_up_side_kernel,
        in_specs=[pl.BlockSpec(memory_space=pltpu.SMEM)] + [pl.BlockSpec()] * 3,
        out_shape=jax.ShapeDtypeStruct((2 * UNIT_HALF, WIDTH), bf16),
        compiler_params=pltpu.CompilerParams(vmem_limit_bytes=12 << 20),
        name="gate_up_side",
    )(ids, here, near, diag)


def down_side_kernel(ids_ref, here_ref, near_ref, diag_ref, out_ref):
    core = ids_ref[0]

    def put(ref, out_ref, cols):
        for j in range(4):
            out_ref[j * HALF : j * HALF + UNITS, cols] = ref[j * UNITS : (j + 1) * UNITS, :]
            out_ref[j * HALF + UNITS : (j + 1) * HALF, cols] = ref[
                j * UNITS + 128 : (j + 1) * UNITS, :
            ]

    rows = pl.ds(2 * UNIT_HALF, UNIT_HALF)
    refs = [here_ref.at[core, rows], here_ref.at[1 - core, rows], near_ref, diag_ref]
    side_by_side(refs, ids_ref, out_ref, put)


def down_side(ids, here, near, diag):
    return pl.pallas_call(
        down_side_kernel,
        in_specs=[pl.BlockSpec(memory_space=pltpu.SMEM)] + [pl.BlockSpec()] * 3,
        out_shape=jax.ShapeDtypeStruct((4 * HALF, WIDTH), bf16),
        compiler_params=pltpu.CompilerParams(vmem_limit_bytes=12 << 20),
        name="down_side",
    )(ids, here, near, diag)


def first_kernel(*refs):
    sources, (out_ref, table), held, sem = refs[:3], refs[3:5], refs[5:8], refs[8]
    copies = [pltpu.make_async_copy(a, b, sem.at[i]) for i, (a, b) in enumerate(zip(sources, held))]
    for copy in copies:
        copy.start()
    for copy in copies:
        copy.wait()
    hidden_ref, routing_ref, gates_ref = held
    hidden = hidden_ref[...].astype(f32)
    mean = jnp.sum(hidden * hidden, axis=1, keepdims=True) * (1.0 / D)
    hi, mid, low = split3(lax.rsqrt(mean + norm_eps))
    lane = lax.broadcasted_iota(jnp.int32, (ROWS_DEV, 128), 1)
    rs = jnp.where(
        lane == 0,
        hi.astype(f32),
        jnp.where(lane == 1, mid.astype(f32), jnp.where(lane == 2, low.astype(f32), 0.0)),
    ).astype(bf16)
    table[...] = jnp.zeros((128, 128), f32)
    table[0:32, :ROWS_DEV] = routing_ref[...].astype(f32)
    for i, part in enumerate(split3(gates_ref[...])):
        table[32 + 32 * i : 64 + 32 * i, :ROWS_DEV] = part.astype(f32)
    named = table[...].T[:ROWS_DEV].astype(bf16)
    for z in range(4):
        for half in range(2):
            at = half * 2048 + z * 512
            out_ref[z, :, half * 512 : half * 512 + 512] = hidden_ref[:, at : at + 512]
        out_ref[z, :, WIDTH : WIDTH + 128] = named
        out_ref[z, :, WIDTH + 128 :] = rs


def first_rows(hidden, routing, gates):
    return pl.pallas_call(
        first_kernel,
        in_specs=[pl.BlockSpec(memory_space=pltpu.HBM)] * 3,
        out_shape=jax.ShapeDtypeStruct((4, ROWS_DEV, FIRST), bf16),
        scratch_shapes=[
            pltpu.VMEM((128, 128), f32),
            pltpu.VMEM((ROWS_DEV, D), bf16),
            pltpu.VMEM((STEPS * TOPK, ROWS_DEV), jnp.int32),
            pltpu.VMEM((STEPS * TOPK, ROWS_DEV), f32),
            pltpu.SemaphoreType.DMA((3,)),
        ],
        compiler_params=pltpu.CompilerParams(vmem_limit_bytes=60 << 20),
        name="first_rows",
    )(hidden, routing, gates)


def spread_kernel(ids_ref, own_ref, far_ref, *out_refs):
    half, z = ids_ref[3], ids_ref[4]
    for d in range(4):
        at = (z + d) % 4
        out_refs[d][half] = own_ref[at]
        out_refs[d][1 - half] = far_ref[at]


def spread(ids, own, far):
    return pl.pallas_call(
        spread_kernel,
        in_specs=[pl.BlockSpec(memory_space=pltpu.SMEM)] + [pl.BlockSpec()] * 2,
        out_shape=[jax.ShapeDtypeStruct((2, ROWS_DEV, FIRST), bf16)] * 4,
        compiler_params=pltpu.CompilerParams(vmem_limit_bytes=4 << 20),
        name="spread",
    )(ids, own, far)


def prepare_kernel(ids_ref, own_ref, other_ref, gain_ref, x_ref, stream_ref, tab_ref, rows, tab):
    core, tp, expert, half, z = [ids_ref[i] for i in range(5)]
    for d in range(4):
        for far in range(2):
            at = (far * 4 + (z - d + 4) % 4) * 16
            rows[pl.ds(pl.multiple_of(core * 128 + at, 16), 16), :] = own_ref[d, far]
            rows[pl.ds(pl.multiple_of((1 - core) * 128 + at, 16), 16), :] = other_ref[d, far]
    named = rows[:, WIDTH : WIDTH + 128].astype(f32)
    gates = pltpu.roll(named, 96, 1) + pltpu.roll(named, 64, 1) + pltpu.roll(named, 32, 1)
    lane = lax.broadcasted_iota(jnp.int32, (ROWS, 128), 1)
    match = jnp.where((named == expert.astype(f32)) & (lane < 32), 1.0, 0.0)
    weighted = match * gates
    group = lane // TOPK
    mask = jnp.zeros((ROWS, 128), f32)
    weight = jnp.zeros((ROWS, 128), f32)
    for s in range(STEPS):
        here = jnp.sum(jnp.where(group == s, match, 0.0), axis=1, keepdims=True)
        gate = jnp.sum(jnp.where(group == s, weighted, 0.0), axis=1, keepdims=True)
        mask = jnp.where(lane == s, here, mask)
        weight = jnp.where(lane == s, gate, weight)
    r0 = lax.broadcasted_iota(jnp.int32, (ROWS, ROWS), 0)
    r1 = lax.broadcasted_iota(jnp.int32, (ROWS, ROWS), 1)
    before = jnp.where(r1 < r0, 1.0, 0.0).astype(bf16)
    place = jnp.where(mask > 0.0, dot(before, mask.astype(bf16)), -1.0)
    tab[...] = jnp.where(lane < 64, weight, pltpu.roll(place, 64, 1))
    for c in range(2):
        for far in range(2):
            for u in range(4):
                at = pl.multiple_of(c * 128 + far * 64 + ((u - z + 4) % 4) * 16, 16)
                to = slice(c * 128 + far * 64 + u * 16, c * 128 + far * 64 + u * 16 + 16)
                block = rows[pl.ds(at, 16), :].astype(f32)
                rs = jnp.sum(block[:, WIDTH + 128 :], axis=1, keepdims=True)
                x_ref[to, :] = (block[:, :WIDTH] * rs * gain_ref[...]).astype(bf16)
                tab_ref[to, :] = tab[pl.ds(at, 16), :]
    at = core * 128 + half * 64 + ((tp // 2 - z + 4) % 4) * 16
    mine = rows[pl.ds(pl.multiple_of(at, 16), 16), :WIDTH].astype(f32)
    stream_ref[...] = jnp.where(tp % 2 == 0, mine[:8], mine[8:])


def prepare(ids, own, other, gain):
    return pl.pallas_call(
        prepare_kernel,
        in_specs=[pl.BlockSpec(memory_space=pltpu.SMEM)] + [pl.BlockSpec()] * 3,
        out_shape=[
            jax.ShapeDtypeStruct((ROWS, WIDTH), bf16),
            jax.ShapeDtypeStruct((8, WIDTH), f32),
            jax.ShapeDtypeStruct((ROWS, 128), f32),
        ],
        scratch_shapes=[pltpu.VMEM((ROWS, FIRST), bf16), pltpu.VMEM((ROWS, 128), f32)],
        compiler_params=pltpu.CompilerParams(vmem_limit_bytes=8 << 20),
        name="prepare",
    )(ids, own, other, gain)


def one_hot(tab_ref, step):
    slot = lax.broadcasted_iota(jnp.int32, (ROWS, ROWS), 1).astype(f32)
    return jnp.where(slot == tab_ref[:, 64 + step : 65 + step], 1.0, 0.0)


def block_at(ids_ref):
    core, half = ids_ref[0], ids_ref[3]
    far = 1 - half
    return [half * 2 + core, half * 2 + 1 - core, far * 2 + core, far * 2 + 1 - core]


def gate_up_kernel(step, ids_ref, *refs):
    core, z = ids_ref[0], ids_ref[4]
    first = step == 0
    if first:
        x_ref, *refs = refs
    else:
        own_ref, other_ref, *refs = refs
    tab_ref, *refs = refs
    if first:
        w_refs, p_refs, xs = refs[:3], refs[3:7], refs[7]
        w_refs = [w_refs[0].at[core], w_refs[0].at[1 - core], *w_refs[1:]]
    else:
        w_ref, p_refs, x_ref = refs[0], refs[1:5], refs[5]
        x_ref[pl.ds(pl.multiple_of(core * 128, 128), 128), :] = own_ref[...]
        x_ref[pl.ds(pl.multiple_of((1 - core) * 128, 128), 128), :] = other_ref[...]
    hot = one_hot(tab_ref, step)
    picked = dot(hot.T[:SLOTS].astype(bf16), x_ref[:, :WIDTH]).astype(bf16)
    if first:
        for b in range(4):
            xs[b] = picked[:, b * HALF : (b + 1) * HALF]
        tail = jnp.zeros((PAY - SLOTS, 384), bf16)
    else:
        squares = jnp.sum(x_ref[:, WIDTH:].astype(f32), axis=1, keepdims=True)
        line = jnp.sum(hot * squares, axis=0, keepdims=True)
        line = jnp.concatenate([line, jnp.zeros((1, 128), f32)], axis=1)
        hi, mid, low = split3(line)
        at = lax.broadcasted_iota(jnp.int32, (PAY - SLOTS, 384), 0)
        tail = jnp.where(
            at == 0,
            hi.astype(f32),
            jnp.where(at == 1, mid.astype(f32), jnp.where(at == 2, low.astype(f32), 0.0)),
        ).astype(bf16)
    ours = [xs[at] for at in block_at(ids_ref)] if first else None
    for d in range(4):
        at = pl.multiple_of(((z + d) % 4) * 384, 128)
        if first:
            part = dot(ours[0], w_refs[0][pl.ds(at, 384), :], NT)
            for b in range(1, 4):
                part = part + dot(ours[b], w_refs[b][pl.ds(at, 384), :], NT)
        else:
            part = dot(picked, w_ref[pl.ds(at, 384), :], NT)
        p_refs[d][:SLOTS, :] = part.astype(bf16)
        p_refs[d][SLOTS:, :] = tail


def gate_up(step, ids, x, tab, weights):
    first = step == 0
    scratch = pltpu.VMEM((4, SLOTS, HALF) if first else (ROWS, EXT), bf16)
    return pl.pallas_call(
        lambda *refs: gate_up_kernel(step, *refs),
        in_specs=[pl.BlockSpec(memory_space=pltpu.SMEM)] + [pl.BlockSpec()] * (len(x) + 1 + len(weights)),
        out_shape=[jax.ShapeDtypeStruct((PAY, 384), bf16)] * 4,
        scratch_shapes=[scratch],
        compiler_params=pltpu.CompilerParams(vmem_limit_bytes=10 << 20),
        cost_estimate=busy(2.2, 4600000),
        name="gate_up",
    )(ids, *x, tab, *weights)


def act_kernel(first, *refs):
    out_ref = refs[4]
    total = refs[0][...].astype(f32)
    for j in range(1, 4):
        total = total + refs[j][...].astype(f32)
    sums = total[:SLOTS]
    if not first:
        line = jnp.sum(total[SLOTS : SLOTS + 8, :HALF], axis=0, keepdims=True)
        rs_line = lax.rsqrt(line * (1.0 / D) + norm_eps)
        r0 = lax.broadcasted_iota(jnp.int32, (SLOTS, HALF), 0)
        r1 = lax.broadcasted_iota(jnp.int32, (SLOTS, HALF), 1)
        rs = jnp.sum(jnp.where(r0 == r1, rs_line, 0.0), axis=1, keepdims=True)
        sums = sums * rs
    t0, t1, t2 = sums[:, :128], sums[:, 128:256], sums[:, 256:]
    a0 = jax.nn.silu(t0) * t2
    a1 = jax.nn.silu(t1) * pltpu.roll(t1, 64, 1)
    half = SLOTS // 2
    lane = lax.broadcasted_iota(jnp.int32, (half, 128), 1)
    middle = jnp.where(lane < 64, a1[:half], pltpu.roll(a1[half:], 64, 1))
    out_ref[...] = jnp.concatenate([a0[:half], middle, a0[half:]], axis=1).astype(bf16)


def activate(first, p):
    return pl.pallas_call(
        lambda *refs: act_kernel(first, *refs),
        out_shape=jax.ShapeDtypeStruct((SLOTS // 2, 384), bf16),
        compiler_params=pltpu.CompilerParams(vmem_limit_bytes=8 << 20),
        cost_estimate=busy(0.3),
        name="activate",
    )(*p)


def down_kernel(step, ids_ref, *refs):
    core, z = ids_ref[0], ids_ref[4]
    first = step == 0
    a_refs, tab_ref, refs = refs[:4], refs[4], refs[5:]
    if first:
        w_refs = [refs[0].at[core], refs[0].at[1 - core], *refs[1:3]]
        send_ref, ys = refs[3:]
        sums = [jnp.zeros((SLOTS, HALF), f32)] * 4
    else:
        w_ref, send_ref, ys, acts = refs
    half = SLOTS // 2
    lane = lax.broadcasted_iota(jnp.int32, (half, 128), 1)
    for d in range(4):
        block = a_refs[d][...].astype(f32)
        middle = block[:, 128:256]
        low = jnp.concatenate([block[:, :128], jnp.where(lane < 64, middle, 0.0)], axis=1)
        high = jnp.concatenate([block[:, 256:], jnp.where(lane < 64, 0.0, middle)], axis=1)
        act = jnp.concatenate([low, high], axis=0).astype(bf16)
        source = (z - d + 4) % 4
        if not first:
            acts[:, pl.ds(pl.multiple_of(source * HALF, HALF), HALF)] = act
            continue
        for b in range(4):
            start = 2 * UNIT_HALF if b < 2 else 0
            at = pl.multiple_of(source * UNITS + start, 64)
            after = pl.multiple_of(source * UNITS + start + 128, 64)
            w = jnp.concatenate([w_refs[b][pl.ds(at, UNITS), :], w_refs[b][pl.ds(after, 64), :]], axis=0)
            sums[b] = sums[b] + dot(act, w)
    if first:
        for b, at in enumerate(block_at(ids_ref)):
            ys[at] = sums[b].astype(bf16)
        result = [ys[b] for b in range(4)]
    else:
        total = [dot(acts[...], w_ref[:, b * HALF : (b + 1) * HALF]) for b in range(4)]
        result = [t.astype(bf16) for t in total]
        for b in range(4):
            ys[b] = result[b]
    place_part(step, 1 - core, tab_ref, result, send_ref)


def place_part(step, part, tab_ref, result, out_ref):
    slot = lax.broadcasted_iota(jnp.int32, (128, HALF), 1).astype(f32)
    tab = tab_ref[pl.ds(pl.multiple_of(part * 128, 128), 128), :]
    hot = jnp.where(slot == tab[:, 64 + step : 65 + step], 1.0, 0.0)[:, :SLOTS].astype(bf16)
    for b in range(4):
        rows = dot(hot, result[b]) * tab[:, step : step + 1]
        out_ref[:, b * HALF : (b + 1) * HALF] = rows.astype(out_ref.dtype)


def kept_kernel(step, ids_ref, ys_ref, tab_ref, out_ref):
    place_part(step, ids_ref[0], tab_ref, [ys_ref[b] for b in range(4)], out_ref)


def kept(step, ids, ys, tab):
    return pl.pallas_call(
        lambda *refs: kept_kernel(step, *refs),
        in_specs=[pl.BlockSpec(memory_space=pltpu.SMEM)] + [pl.BlockSpec()] * 2,
        out_shape=jax.ShapeDtypeStruct((128, WIDTH), f32),
        compiler_params=pltpu.CompilerParams(vmem_limit_bytes=6 << 20),
        cost_estimate=busy(0.4),
        name="kept",
    )(ids, ys, tab)


def down(step, ids, acts, tab, weights):
    return pl.pallas_call(
        lambda *refs: down_kernel(step, *refs),
        in_specs=[pl.BlockSpec(memory_space=pltpu.SMEM)] + [pl.BlockSpec()] * (5 + len(weights)),
        out_shape=[
            jax.ShapeDtypeStruct((128, WIDTH), bf16),
            jax.ShapeDtypeStruct((4, SLOTS, HALF), bf16),
        ],
        scratch_shapes=[] if step == 0 else [pltpu.VMEM((SLOTS, WIDTH), bf16)],
        compiler_params=pltpu.CompilerParams(vmem_limit_bytes=10 << 20),
        cost_estimate=busy(1.9, 3000000),
        name="down",
    )(ids, *acts, tab, *weights)


def pair_kernel(keep_ref, other_ref, out_ref):
    out_ref[...] = (keep_ref[...] + other_ref[...].astype(f32)).astype(bf16)


def pair(keep, other):
    return pl.pallas_call(
        pair_kernel,
        out_shape=jax.ShapeDtypeStruct((128, WIDTH), bf16),
        compiler_params=pltpu.CompilerParams(vmem_limit_bytes=4 << 20),
        name="pair",
    )(keep, other)


def residual_kernel(p_ref, stream_ref, gain_ref, new_ref, x_ref):
    total = p_ref[0].astype(f32)
    for j in range(1, 16):
        total = total + p_ref[j].astype(f32)
    stream = stream_ref[...] + total
    new_ref[...] = stream
    hi, mid, low = split3(jnp.sum(stream * stream, axis=1, keepdims=True))
    lane = lax.broadcasted_iota(jnp.int32, (8, 128), 1)
    parts = jnp.where(
        lane == 0,
        hi.astype(f32),
        jnp.where(lane == 1, mid.astype(f32), jnp.where(lane == 2, low.astype(f32), 0.0)),
    )
    row = jnp.concatenate([stream * gain_ref[...], parts], axis=1).astype(bf16)
    for j in range(16):
        x_ref[j] = row


def residual(p, stream, gain):
    return pl.pallas_call(
        residual_kernel,
        out_shape=[
            jax.ShapeDtypeStruct((8, WIDTH), f32),
            jax.ShapeDtypeStruct((16, 8, EXT), bf16),
        ],
        compiler_params=pltpu.CompilerParams(vmem_limit_bytes=4 << 20),
        name="residual",
    )(p, stream, gain)


def last_kernel(p_ref, stream_ref, before_ref, change_ref):
    total = p_ref[0].astype(f32)
    for j in range(1, 16):
        total = total + p_ref[j].astype(f32)
    change_ref[...] = (stream_ref[...] - before_ref[...] + total).astype(bf16)


def last(p, stream, before):
    return pl.pallas_call(
        last_kernel,
        out_shape=jax.ShapeDtypeStruct((8, WIDTH), bf16),
        compiler_params=pltpu.CompilerParams(vmem_limit_bytes=4 << 20),
        name="last",
    )(p, stream, before)


def place_kernel(ids_ref, whole_ref, hidden_ref, out_ref):
    z = ids_ref[4]
    for a in range(4):
        for h in range(2):
            block = whole_ref[((a + z) % 4) * 2 + h].astype(f32)
            for far in range(2):
                to = far * 2048 + a * 512
                rows = hidden_ref[:, to : to + 512].astype(f32)[h * 8 : h * 8 + 8]
                out_ref[h * 8 : h * 8 + 8, to : to + 512] = (
                    rows + block[:, far * 512 : far * 512 + 512]
                )


def place_rows(ids, whole, hidden):
    return pl.pallas_call(
        place_kernel,
        in_specs=[pl.BlockSpec(memory_space=pltpu.SMEM), pl.BlockSpec(), pl.BlockSpec()],
        out_shape=jax.ShapeDtypeStruct((ROWS_DEV, D), f32),
        compiler_params=pltpu.CompilerParams(vmem_limit_bytes=4 << 20),
        name="place_rows",
    )(ids, whole, hidden)


def exchange(x, axes):
    return lax.all_to_all(x, axes, split_axis=0, concat_axis=0, tiled=True)


def swap(x):
    return lax.ppermute(x, "c", [(0, 1), (1, 0)])


def around(x, d):
    return lax.ppermute(x, "z", [(i, (i + d) % 4) for i in range(4)])


def body(trainer_weights, hidden_in, norm_gain, routing, gate_weights):
    core, far, z = lax.axis_index("c"), lax.axis_index("xh"), lax.axis_index("z")
    tp = lax.axis_index(T)
    ids = jnp.stack([core, tp, 2 * tp + core, far, z, far * 8 + tp]).astype(jnp.int32)
    gain = lax.dynamic_index_in_dim(norm_gain.reshape(2, 4, 512), z, 1, keepdims=False)
    gain = gain.reshape(1, WIDTH)

    lines = lambda v: jnp.transpose(v, (0, 2, 1)).reshape(STEPS * TOPK, ROWS_DEV)
    pieces = first_rows(hidden_in, lines(routing), lines(gate_weights))
    pieces_far = lax.ppermute(pieces, "xh", [(0, 1), (1, 0)])

    near_out, diag_out = quantize_far(trainer_weights)
    near_out, diag_out, pieces_far = lax.optimization_barrier((near_out, diag_out, pieces_far))
    gu_near = lax.ppermute(near_out, "xh", [(0, 1), (1, 0)])
    gu_diag = lax.ppermute(diag_out, ("xh", "c"), [(0, 3), (3, 0), (1, 2), (2, 1)])
    rows = spread(ids, pieces, pieces_far)
    rows = jnp.stack([rows[0]] + [around(rows[d], d) for d in (1, 2, 3)])
    mixed, near_out, diag_out = quantize_rest(ids, trainer_weights)
    here, rows_other = lax.optimization_barrier((hold(exchange(mixed, "c")), swap(rows)))
    x, stream, tab = prepare(ids, rows, rows_other, gain)

    near_out, diag_out, gu_near, x, stream, tab = lax.optimization_barrier(
        (near_out, diag_out, gu_near, x, stream, tab)
    )
    down_near = lax.ppermute(near_out, "xh", [(0, 1), (1, 0)])
    down_diag = lax.ppermute(diag_out, ("xh", "c"), [(0, 3), (3, 0), (1, 2), (2, 1)])

    x, before = [x], stream
    gu_weights, down_weights = [here, gu_near, gu_diag], [here, down_near, down_diag]
    for step in range(STEPS):
        part = gate_up(step, ids, x, tab, gu_weights)
        if step == 0:
            gu_near, gu_diag, *part = lax.optimization_barrier((gu_near, gu_diag, *part))
            gu_weights = [gate_up_side(ids, here, gu_near, gu_diag)]
        part = [part[0]] + [around(part[d], d) for d in (1, 2, 3)]
        act = activate(step == 0, part)
        acts = [act] + [around(act, d) for d in (1, 2, 3)]
        send, ys = down(step, ids, acts, tab, down_weights)
        if step == 0:
            send, down_near, down_diag = lax.optimization_barrier((send, down_near, down_diag))
            down_weights = [down_side(ids, here, down_near, down_diag)]
        sums = exchange(pair(kept(step, ids, ys, tab), swap(send)).reshape(16, 8, WIDTH), XT)
        if step < STEPS - 1:
            stream, rows = residual(sums, stream, gain)
            rows = exchange(rows, XT).reshape(128, EXT)
            x = [rows, swap(rows)]
        else:
            change = last(sums, stream, before)

    turn = [(a * 8 + t, ((t // 2 - a) % 4) * 8 + t) for a in range(4) for t in range(8)]
    mine = lax.ppermute(change, ("z", "xl", "y"), turn)
    whole = exchange(jnp.broadcast_to(mine[None], (8, 8, WIDTH)), T)
    return place_rows(ids, whole, hidden_in)


def solution(mesh):
    fine = Mesh(mesh.devices.reshape(2, 4, 2, 2, 4), ALL)
    fsdp, tp = ("xh", "z", "c"), ("xl", "y")
    in_specs = (
        P(tp, None, None, fsdp),
        P(fsdp, None),
        P(),
        P(None, fsdp, None),
        P(None, fsdp, None),
    )
    return jax.shard_map(
        body, mesh=fine, in_specs=in_specs, out_specs=P(fsdp, None), check_vma=False
    )
```

```python
import jax
import jax.numpy as jnp
from jax import lax
from jax.experimental import pallas as pl
from jax.experimental.pallas import tpu as pltpu
from jax.sharding import Mesh, PartitionSpec as P

D = 4096
FF = 1536
TOPK = 8
EXPERTS = 16
QB = 128
STEPS = 4
CAP = 11
ROWS_DEV = 16
ROWS = 256
SLOTS = 16 * CAP
UNIT_HALF = 768
WIDTH = 1024
HALF = 256
UNITS = 192
PAY = 184
EXT = 1152
FIRST = 1280

XZ = ("xh", "z")
XT = ("xh", "xl", "y")
T = ("xl", "y")
ALL = ("xh", "z", "c", "xl", "y")

norm_eps = 1e-06
scale_eps = 1e-06
code_limit = 448.0
smallest_normal = 0.015625
f32 = jnp.float32
bf16 = jnp.bfloat16

NN = (((1,), (0,)), ((), ()))
NT = (((1,), (1,)), ((), ()))


def dot(a, b, dims=NN):
    return lax.dot_general(a, b, dims, preferred_element_type=f32)


def busy(us, moved=0):
    return pl.CostEstimate(flops=int(us * 1.15e9), bytes_accessed=moved, transcendentals=0)


def split3(v):
    hi = v.astype(bf16)
    rest = v - hi.astype(f32)
    mid = rest.astype(bf16)
    low = (rest - mid.astype(f32)).astype(bf16)
    return hi, mid, low


def float_code(v):
    big = v * 1048577.0
    fine = big - (big - v)
    coarse = (v + 24576.0) - 24576.0
    return jnp.where(jnp.abs(v) < smallest_normal, coarse, fine)


def quant_block(tile):
    top = jnp.max(jnp.abs(tile), axis=0, keepdims=True).astype(f32)
    top = jnp.max(top, axis=1, keepdims=True) + scale_eps
    tile = tile.astype(f32)
    scale = top / code_limit
    return (float_code(tile * (1.0 / scale)) * scale).astype(bf16)


def quant_gate_up(src, out_ref, group):
    for m in range(2):
        for q in range(3):
            for h in range(2):
                cols = slice(h * QB, (h + 1) * QB)
                back = quant_block(src[m, q * QB : (q + 1) * QB, cols])
                for g in range(2):
                    unit = q * 2 + g
                    j, part = unit // 3, unit % 3
                    if m == 0:
                        to = part * 64
                    elif part < 2:
                        to = 256 + part * 64
                    else:
                        to = 192
                    to = group * 768 + j * 384 + to
                    out_ref[to : to + 64, cols] = back[g * 64 : g * 64 + 64]


def quant_down(src, out_ref, at, blocks):
    for q in range(blocks):
        for h in range(2):
            cols = slice(h * QB, (h + 1) * QB)
            back = quant_block(src[q * QB : (q + 1) * QB, cols])
            out_ref[at + q * QB : at + (q + 1) * QB, cols] = back


def quant_far_kernel(w_ref, near_ref, diag_ref, buf, sem):
    core, half = lax.axis_index("c"), 1 - lax.axis_index("xh")
    copies = []
    for p in range(2):
        for g in range(2):
            expert = core if p == 0 else 1 - core
            at = pl.multiple_of(half * UNIT_HALF + g * 384, 128)
            src = w_ref.at[expert, pl.ds(0, 2), pl.ds(at, 384), :]
            copies.append(pltpu.make_async_copy(src, buf.at[p * 2 + g], sem.at[p * 2 + g]))
    for copy in copies:
        copy.start()
    for p in range(2):
        for g in range(2):
            copies[p * 2 + g].wait()
            quant_gate_up(buf.at[p * 2 + g], diag_ref if p else near_ref, g)


def quantize_far(w):
    out = jax.ShapeDtypeStruct((2 * UNIT_HALF, HALF), bf16)
    return pl.pallas_call(
        quant_far_kernel,
        in_specs=[pl.BlockSpec(memory_space=pltpu.HBM)],
        out_shape=[out, out],
        scratch_shapes=[pltpu.VMEM((4, 2, 384, HALF), bf16), pltpu.SemaphoreType.DMA((4,))],
        compiler_params=pltpu.CompilerParams(vmem_limit_bytes=60 << 20),
        name="quantize_far",
    )(w)


def quant_rest_kernel(
    ids_ref, w_ref, pair_ref, near_ref, diag_ref, buf, sem, down_buf, down_sem
):
    core, half = ids_ref[0], ids_ref[3]
    copies = []
    for p in range(2):
        expert = core if p == 0 else 1 - core
        for g in range(2):
            at = pl.multiple_of(half * UNIT_HALF + g * 384, 128)
            src = w_ref.at[expert, :, pl.ds(at, 384), :]
            copies.append(pltpu.make_async_copy(src, buf.at[p * 2 + g], sem.at[p * 2 + g]))
    down_copies = []
    for p in range(2):
        expert = core if p == 0 else 1 - core
        at = pl.multiple_of((1 - half) * UNIT_HALF, 128)
        src = w_ref.at[expert, 2, pl.ds(at, UNIT_HALF), :]
        down_copies.append(pltpu.make_async_copy(src, down_buf.at[p], down_sem.at[p]))
    for copy in copies + down_copies:
        copy.start()
    for p in range(2):
        out_ref = pair_ref.at[1 - core if p else core]
        for g in range(2):
            copies[p * 2 + g].wait()
            quant_gate_up(buf.at[p * 2 + g], out_ref, g)
            quant_down(buf.at[p * 2 + g, 2], out_ref, 2 * UNIT_HALF + g * 384, 3)
    for p in range(2):
        down_copies[p].wait()
        quant_down(down_buf.at[p], diag_ref if p else near_ref, 0, 6)


def keep_kernel(mixed_ref, out_ref):
    out_ref[...] = mixed_ref[...]


def hold(mixed):
    return pl.pallas_call(
        keep_kernel,
        out_shape=jax.ShapeDtypeStruct(mixed.shape, bf16),
        compiler_params=pltpu.CompilerParams(vmem_limit_bytes=12 << 20),
        name="hold",
    )(mixed)


def quantize_rest(ids, w):
    whole = jax.ShapeDtypeStruct((2, 3 * UNIT_HALF, HALF), bf16)
    third = jax.ShapeDtypeStruct((UNIT_HALF, HALF), bf16)
    return pl.pallas_call(
        quant_rest_kernel,
        in_specs=[
            pl.BlockSpec(memory_space=pltpu.SMEM),
            pl.BlockSpec(memory_space=pltpu.HBM),
        ],
        out_shape=[whole, third, third],
        scratch_shapes=[
            pltpu.VMEM((4, 3, 384, HALF), bf16),
            pltpu.SemaphoreType.DMA((4,)),
            pltpu.VMEM((2, UNIT_HALF, HALF), bf16),
            pltpu.SemaphoreType.DMA((2,)),
        ],
        compiler_params=pltpu.CompilerParams(vmem_limit_bytes=16 << 20),
        name="quantize_rest",
    )(ids, w)


def side_by_side(refs, ids_ref, out_ref, put):
    core, half = ids_ref[0], ids_ref[3]
    far = 1 - half
    at = [half * 2 + core, half * 2 + 1 - core, far * 2 + core, far * 2 + 1 - core]
    for ref, b in zip(refs, at):
        put(ref, out_ref, pl.ds(pl.multiple_of(b * HALF, HALF), HALF))


def gate_up_side_kernel(ids_ref, here_ref, near_ref, diag_ref, out_ref):
    core = ids_ref[0]

    def put(ref, out_ref, cols):
        out_ref[:, cols] = ref[: 2 * UNIT_HALF, :]

    refs = [here_ref.at[core], here_ref.at[1 - core], near_ref, diag_ref]
    side_by_side(refs, ids_ref, out_ref, put)


def gate_up_side(ids, here, near, diag):
    return pl.pallas_call(
        gate_up_side_kernel,
        in_specs=[pl.BlockSpec(memory_space=pltpu.SMEM)] + [pl.BlockSpec()] * 3,
        out_shape=jax.ShapeDtypeStruct((2 * UNIT_HALF, WIDTH), bf16),
        compiler_params=pltpu.CompilerParams(vmem_limit_bytes=12 << 20),
        name="gate_up_side",
    )(ids, here, near, diag)


def down_side_kernel(ids_ref, here_ref, near_ref, diag_ref, out_ref):
    core = ids_ref[0]

    def put(ref, out_ref, cols):
        for j in range(4):
            out_ref[j * HALF : j * HALF + UNITS, cols] = ref[j * UNITS : (j + 1) * UNITS, :]
            out_ref[j * HALF + UNITS : (j + 1) * HALF, cols] = ref[
                j * UNITS + 128 : (j + 1) * UNITS, :
            ]

    rows = pl.ds(2 * UNIT_HALF, UNIT_HALF)
    refs = [here_ref.at[core, rows], here_ref.at[1 - core, rows], near_ref, diag_ref]
    side_by_side(refs, ids_ref, out_ref, put)


def down_side(ids, here, near, diag):
    return pl.pallas_call(
        down_side_kernel,
        in_specs=[pl.BlockSpec(memory_space=pltpu.SMEM)] + [pl.BlockSpec()] * 3,
        out_shape=jax.ShapeDtypeStruct((4 * HALF, WIDTH), bf16),
        compiler_params=pltpu.CompilerParams(vmem_limit_bytes=12 << 20),
        name="down_side",
    )(ids, here, near, diag)


def first_kernel(*refs):
    sources, (out_ref, table), held, sem = refs[:3], refs[3:5], refs[5:8], refs[8]
    copies = [pltpu.make_async_copy(a, b, sem.at[i]) for i, (a, b) in enumerate(zip(sources, held))]
    for copy in copies:
        copy.start()
    for copy in copies:
        copy.wait()
    hidden_ref, routing_ref, gates_ref = held
    hidden = hidden_ref[...].astype(f32)
    mean = jnp.sum(hidden * hidden, axis=1, keepdims=True) * (1.0 / D)
    hi, mid, low = split3(lax.rsqrt(mean + norm_eps))
    lane = lax.broadcasted_iota(jnp.int32, (ROWS_DEV, 128), 1)
    rs = jnp.where(
        lane == 0,
        hi.astype(f32),
        jnp.where(lane == 1, mid.astype(f32), jnp.where(lane == 2, low.astype(f32), 0.0)),
    ).astype(bf16)
    table[...] = jnp.zeros((128, 128), f32)
    table[0:32, :ROWS_DEV] = routing_ref[...].astype(f32)
    for i, part in enumerate(split3(gates_ref[...])):
        table[32 + 32 * i : 64 + 32 * i, :ROWS_DEV] = part.astype(f32)
    named = table[...].T[:ROWS_DEV].astype(bf16)
    for z in range(4):
        for half in range(2):
            at = half * 2048 + z * 512
            out_ref[z, :, half * 512 : half * 512 + 512] = hidden_ref[:, at : at + 512]
        out_ref[z, :, WIDTH : WIDTH + 128] = named
        out_ref[z, :, WIDTH + 128 :] = rs


def first_rows(hidden, routing, gates):
    return pl.pallas_call(
        first_kernel,
        in_specs=[pl.BlockSpec(memory_space=pltpu.HBM)] * 3,
        out_shape=jax.ShapeDtypeStruct((4, ROWS_DEV, FIRST), bf16),
        scratch_shapes=[
            pltpu.VMEM((128, 128), f32),
            pltpu.VMEM((ROWS_DEV, D), bf16),
            pltpu.VMEM((STEPS * TOPK, ROWS_DEV), jnp.int32),
            pltpu.VMEM((STEPS * TOPK, ROWS_DEV), f32),
            pltpu.SemaphoreType.DMA((3,)),
        ],
        compiler_params=pltpu.CompilerParams(vmem_limit_bytes=60 << 20),
        name="first_rows",
    )(hidden, routing, gates)


def spread_kernel(ids_ref, own_ref, far_ref, *out_refs):
    half, z = ids_ref[3], ids_ref[4]
    for d in range(4):
        at = (z + d) % 4
        out_refs[d][half] = own_ref[at]
        out_refs[d][1 - half] = far_ref[at]


def spread(ids, own, far):
    return pl.pallas_call(
        spread_kernel,
        in_specs=[pl.BlockSpec(memory_space=pltpu.SMEM)] + [pl.BlockSpec()] * 2,
        out_shape=[jax.ShapeDtypeStruct((2, ROWS_DEV, FIRST), bf16)] * 4,
        compiler_params=pltpu.CompilerParams(vmem_limit_bytes=4 << 20),
        name="spread",
    )(ids, own, far)


def prepare_kernel(ids_ref, own_ref, other_ref, gain_ref, x_ref, stream_ref, tab_ref, rows, tab):
    core, tp, expert, half, z = [ids_ref[i] for i in range(5)]
    for d in range(4):
        for far in range(2):
            at = (far * 4 + (z - d + 4) % 4) * 16
            rows[pl.ds(pl.multiple_of(core * 128 + at, 16), 16), :] = own_ref[d, far]
            rows[pl.ds(pl.multiple_of((1 - core) * 128 + at, 16), 16), :] = other_ref[d, far]
    named = rows[:, WIDTH : WIDTH + 128].astype(f32)
    gates = pltpu.roll(named, 96, 1) + pltpu.roll(named, 64, 1) + pltpu.roll(named, 32, 1)
    lane = lax.broadcasted_iota(jnp.int32, (ROWS, 128), 1)
    match = jnp.where((named == expert.astype(f32)) & (lane < 32), 1.0, 0.0)
    weighted = match * gates
    group = lane // TOPK
    mask = jnp.zeros((ROWS, 128), f32)
    weight = jnp.zeros((ROWS, 128), f32)
    for s in range(STEPS):
        here = jnp.sum(jnp.where(group == s, match, 0.0), axis=1, keepdims=True)
        gate = jnp.sum(jnp.where(group == s, weighted, 0.0), axis=1, keepdims=True)
        mask = jnp.where(lane == s, here, mask)
        weight = jnp.where(lane == s, gate, weight)
    r0 = lax.broadcasted_iota(jnp.int32, (ROWS, ROWS), 0)
    r1 = lax.broadcasted_iota(jnp.int32, (ROWS, ROWS), 1)
    before = jnp.where(r1 < r0, 1.0, 0.0).astype(bf16)
    place = jnp.where(mask > 0.0, dot(before, mask.astype(bf16)), -1.0)
    tab[...] = jnp.where(lane < 64, weight, pltpu.roll(place, 64, 1))
    for c in range(2):
        for far in range(2):
            for u in range(4):
                at = pl.multiple_of(c * 128 + far * 64 + ((u - z + 4) % 4) * 16, 16)
                to = slice(c * 128 + far * 64 + u * 16, c * 128 + far * 64 + u * 16 + 16)
                block = rows[pl.ds(at, 16), :].astype(f32)
                rs = jnp.sum(block[:, WIDTH + 128 :], axis=1, keepdims=True)
                x_ref[to, :] = (block[:, :WIDTH] * rs * gain_ref[...]).astype(bf16)
                tab_ref[to, :] = tab[pl.ds(at, 16), :]
    at = core * 128 + half * 64 + ((tp // 2 - z + 4) % 4) * 16
    mine = rows[pl.ds(pl.multiple_of(at, 16), 16), :WIDTH].astype(f32)
    stream_ref[...] = jnp.where(tp % 2 == 0, mine[:8], mine[8:])


def prepare(ids, own, other, gain):
    return pl.pallas_call(
        prepare_kernel,
        in_specs=[pl.BlockSpec(memory_space=pltpu.SMEM)] + [pl.BlockSpec()] * 3,
        out_shape=[
            jax.ShapeDtypeStruct((ROWS, WIDTH), bf16),
            jax.ShapeDtypeStruct((8, WIDTH), f32),
            jax.ShapeDtypeStruct((ROWS, 128), f32),
        ],
        scratch_shapes=[pltpu.VMEM((ROWS, FIRST), bf16), pltpu.VMEM((ROWS, 128), f32)],
        compiler_params=pltpu.CompilerParams(vmem_limit_bytes=8 << 20),
        name="prepare",
    )(ids, own, other, gain)


def one_hot(tab_ref, step):
    slot = lax.broadcasted_iota(jnp.int32, (ROWS, ROWS), 1).astype(f32)
    return jnp.where(slot == tab_ref[:, 64 + step : 65 + step], 1.0, 0.0)


def block_at(ids_ref):
    core, half = ids_ref[0], ids_ref[3]
    far = 1 - half
    return [half * 2 + core, half * 2 + 1 - core, far * 2 + core, far * 2 + 1 - core]


def gate_up_kernel(step, ids_ref, *refs):
    core, z = ids_ref[0], ids_ref[4]
    first = step == 0
    if first:
        x_ref, *refs = refs
    else:
        own_ref, other_ref, *refs = refs
    tab_ref, *refs = refs
    if first:
        w_refs, p_refs, xs = refs[:3], refs[3:7], refs[7]
        w_refs = [w_refs[0].at[core], w_refs[0].at[1 - core], *w_refs[1:]]
    else:
        w_ref, p_refs, x_ref = refs[0], refs[1:5], refs[5]
        x_ref[pl.ds(pl.multiple_of(core * 128, 128), 128), :] = own_ref[...]
        x_ref[pl.ds(pl.multiple_of((1 - core) * 128, 128), 128), :] = other_ref[...]
    hot = one_hot(tab_ref, step)
    picked = dot(hot.T[:SLOTS].astype(bf16), x_ref[:, :WIDTH]).astype(bf16)
    if first:
        for b in range(4):
            xs[b] = picked[:, b * HALF : (b + 1) * HALF]
        tail = jnp.zeros((PAY - SLOTS, 384), bf16)
    else:
        squares = jnp.sum(x_ref[:, WIDTH:].astype(f32), axis=1, keepdims=True)
        line = jnp.sum(hot * squares, axis=0, keepdims=True)
        line = jnp.concatenate([line, jnp.zeros((1, 128), f32)], axis=1)
        hi, mid, low = split3(line)
        at = lax.broadcasted_iota(jnp.int32, (PAY - SLOTS, 384), 0)
        tail = jnp.where(
            at == 0,
            hi.astype(f32),
            jnp.where(at == 1, mid.astype(f32), jnp.where(at == 2, low.astype(f32), 0.0)),
        ).astype(bf16)
    ours = [xs[at] for at in block_at(ids_ref)] if first else None
    for d in range(4):
        at = pl.multiple_of(((z + d) % 4) * 384, 128)
        if first:
            part = dot(ours[0], w_refs[0][pl.ds(at, 384), :], NT)
            for b in range(1, 4):
                part = part + dot(ours[b], w_refs[b][pl.ds(at, 384), :], NT)
        else:
            part = dot(picked, w_ref[pl.ds(at, 384), :], NT)
        p_refs[d][:SLOTS, :] = part.astype(bf16)
        p_refs[d][SLOTS:, :] = tail


def gate_up(step, ids, x, tab, weights):
    first = step == 0
    scratch = pltpu.VMEM((4, SLOTS, HALF) if first else (ROWS, EXT), bf16)
    return pl.pallas_call(
        lambda *refs: gate_up_kernel(step, *refs),
        in_specs=[pl.BlockSpec(memory_space=pltpu.SMEM)] + [pl.BlockSpec()] * (len(x) + 1 + len(weights)),
        out_shape=[jax.ShapeDtypeStruct((PAY, 384), bf16)] * 4,
        scratch_shapes=[scratch],
        compiler_params=pltpu.CompilerParams(vmem_limit_bytes=10 << 20),
        cost_estimate=busy(2.2, 4600000),
        name="gate_up",
    )(ids, *x, tab, *weights)


def act_kernel(first, *refs):
    out_ref = refs[4]
    total = refs[0][...].astype(f32)
    for j in range(1, 4):
        total = total + refs[j][...].astype(f32)
    sums = total[:SLOTS]
    if not first:
        line = jnp.sum(total[SLOTS : SLOTS + 8, :HALF], axis=0, keepdims=True)
        rs_line = lax.rsqrt(line * (1.0 / D) + norm_eps)
        r0 = lax.broadcasted_iota(jnp.int32, (SLOTS, HALF), 0)
        r1 = lax.broadcasted_iota(jnp.int32, (SLOTS, HALF), 1)
        rs = jnp.sum(jnp.where(r0 == r1, rs_line, 0.0), axis=1, keepdims=True)
        sums = sums * rs
    t0, t1, t2 = sums[:, :128], sums[:, 128:256], sums[:, 256:]
    a0 = jax.nn.silu(t0) * t2
    a1 = jax.nn.silu(t1) * pltpu.roll(t1, 64, 1)
    half = SLOTS // 2
    lane = lax.broadcasted_iota(jnp.int32, (half, 128), 1)
    middle = jnp.where(lane < 64, a1[:half], pltpu.roll(a1[half:], 64, 1))
    out_ref[...] = jnp.concatenate([a0[:half], middle, a0[half:]], axis=1).astype(bf16)


def activate(first, p):
    return pl.pallas_call(
        lambda *refs: act_kernel(first, *refs),
        out_shape=jax.ShapeDtypeStruct((SLOTS // 2, 384), bf16),
        compiler_params=pltpu.CompilerParams(vmem_limit_bytes=8 << 20),
        cost_estimate=busy(0.3),
        name="activate",
    )(*p)


def down_kernel(step, ids_ref, *refs):
    core, z = ids_ref[0], ids_ref[4]
    first = step == 0
    a_refs, tab_ref, refs = refs[:4], refs[4], refs[5:]
    if first:
        w_refs = [refs[0].at[core], refs[0].at[1 - core], *refs[1:3]]
        send_ref, ys = refs[3:]
        sums = [jnp.zeros((SLOTS, HALF), f32)] * 4
    else:
        w_ref, send_ref, ys, acts = refs
    half = SLOTS // 2
    lane = lax.broadcasted_iota(jnp.int32, (half, 128), 1)
    for d in range(4):
        block = a_refs[d][...].astype(f32)
        middle = block[:, 128:256]
        low = jnp.concatenate([block[:, :128], jnp.where(lane < 64, middle, 0.0)], axis=1)
        high = jnp.concatenate([block[:, 256:], jnp.where(lane < 64, 0.0, middle)], axis=1)
        act = jnp.concatenate([low, high], axis=0).astype(bf16)
        source = (z - d + 4) % 4
        if not first:
            acts[:, pl.ds(pl.multiple_of(source * HALF, HALF), HALF)] = act
            continue
        for b in range(4):
            start = 2 * UNIT_HALF if b < 2 else 0
            at = pl.multiple_of(source * UNITS + start, 64)
            after = pl.multiple_of(source * UNITS + start + 128, 64)
            w = jnp.concatenate([w_refs[b][pl.ds(at, UNITS), :], w_refs[b][pl.ds(after, 64), :]], axis=0)
            sums[b] = sums[b] + dot(act, w)
    if first:
        for b, at in enumerate(block_at(ids_ref)):
            ys[at] = sums[b].astype(bf16)
        result = [ys[b] for b in range(4)]
    else:
        total = [dot(acts[...], w_ref[:, b * HALF : (b + 1) * HALF]) for b in range(4)]
        result = [t.astype(bf16) for t in total]
        for b in range(4):
            ys[b] = result[b]
    place_part(step, 1 - core, tab_ref, result, send_ref)


def place_part(step, part, tab_ref, result, out_ref):
    slot = lax.broadcasted_iota(jnp.int32, (128, HALF), 1).astype(f32)
    tab = tab_ref[pl.ds(pl.multiple_of(part * 128, 128), 128), :]
    hot = jnp.where(slot == tab[:, 64 + step : 65 + step], 1.0, 0.0)[:, :SLOTS].astype(bf16)
    for b in range(4):
        rows = dot(hot, result[b]) * tab[:, step : step + 1]
        out_ref[:, b * HALF : (b + 1) * HALF] = rows.astype(out_ref.dtype)


def kept_kernel(step, ids_ref, ys_ref, tab_ref, out_ref):
    place_part(step, ids_ref[0], tab_ref, [ys_ref[b] for b in range(4)], out_ref)


def kept(step, ids, ys, tab):
    return pl.pallas_call(
        lambda *refs: kept_kernel(step, *refs),
        in_specs=[pl.BlockSpec(memory_space=pltpu.SMEM)] + [pl.BlockSpec()] * 2,
        out_shape=jax.ShapeDtypeStruct((128, WIDTH), f32),
        compiler_params=pltpu.CompilerParams(vmem_limit_bytes=6 << 20),
        cost_estimate=busy(0.4),
        name="kept",
    )(ids, ys, tab)


def down(step, ids, acts, tab, weights):
    return pl.pallas_call(
        lambda *refs: down_kernel(step, *refs),
        in_specs=[pl.BlockSpec(memory_space=pltpu.SMEM)] + [pl.BlockSpec()] * (5 + len(weights)),
        out_shape=[
            jax.ShapeDtypeStruct((128, WIDTH), bf16),
            jax.ShapeDtypeStruct((4, SLOTS, HALF), bf16),
        ],
        scratch_shapes=[] if step == 0 else [pltpu.VMEM((SLOTS, WIDTH), bf16)],
        compiler_params=pltpu.CompilerParams(vmem_limit_bytes=10 << 20),
        cost_estimate=busy(1.9, 3000000),
        name="down",
    )(ids, *acts, tab, *weights)


def pair_kernel(keep_ref, other_ref, out_ref):
    out_ref[...] = (keep_ref[...] + other_ref[...].astype(f32)).astype(bf16)


def pair(keep, other):
    return pl.pallas_call(
        pair_kernel,
        out_shape=jax.ShapeDtypeStruct((128, WIDTH), bf16),
        compiler_params=pltpu.CompilerParams(vmem_limit_bytes=4 << 20),
        name="pair",
    )(keep, other)


def residual_kernel(p_ref, stream_ref, gain_ref, new_ref, x_ref):
    total = p_ref[0].astype(f32)
    for j in range(1, 16):
        total = total + p_ref[j].astype(f32)
    stream = stream_ref[...] + total
    new_ref[...] = stream
    hi, mid, low = split3(jnp.sum(stream * stream, axis=1, keepdims=True))
    lane = lax.broadcasted_iota(jnp.int32, (8, 128), 1)
    parts = jnp.where(
        lane == 0,
        hi.astype(f32),
        jnp.where(lane == 1, mid.astype(f32), jnp.where(lane == 2, low.astype(f32), 0.0)),
    )
    row = jnp.concatenate([stream * gain_ref[...], parts], axis=1).astype(bf16)
    for j in range(16):
        x_ref[j] = row


def residual(p, stream, gain):
    return pl.pallas_call(
        residual_kernel,
        out_shape=[
            jax.ShapeDtypeStruct((8, WIDTH), f32),
            jax.ShapeDtypeStruct((16, 8, EXT), bf16),
        ],
        compiler_params=pltpu.CompilerParams(vmem_limit_bytes=4 << 20),
        name="residual",
    )(p, stream, gain)


def last_kernel(p_ref, stream_ref, before_ref, change_ref):
    total = p_ref[0].astype(f32)
    for j in range(1, 16):
        total = total + p_ref[j].astype(f32)
    change_ref[...] = (stream_ref[...] - before_ref[...] + total).astype(bf16)


def last(p, stream, before):
    return pl.pallas_call(
        last_kernel,
        out_shape=jax.ShapeDtypeStruct((8, WIDTH), bf16),
        compiler_params=pltpu.CompilerParams(vmem_limit_bytes=4 << 20),
        name="last",
    )(p, stream, before)


def place_kernel(ids_ref, whole_ref, hidden_ref, out_ref):
    z = ids_ref[4]
    for a in range(4):
        for h in range(2):
            block = whole_ref[((a + z) % 4) * 2 + h].astype(f32)
            for far in range(2):
                to = far * 2048 + a * 512
                rows = hidden_ref[:, to : to + 512].astype(f32)[h * 8 : h * 8 + 8]
                out_ref[h * 8 : h * 8 + 8, to : to + 512] = (
                    rows + block[:, far * 512 : far * 512 + 512]
                )


def place_rows(ids, whole, hidden):
    return pl.pallas_call(
        place_kernel,
        in_specs=[pl.BlockSpec(memory_space=pltpu.SMEM), pl.BlockSpec(), pl.BlockSpec()],
        out_shape=jax.ShapeDtypeStruct((ROWS_DEV, D), f32),
        compiler_params=pltpu.CompilerParams(vmem_limit_bytes=4 << 20),
        name="place_rows",
    )(ids, whole, hidden)


def exchange(x, axes):
    return lax.all_to_all(x, axes, split_axis=0, concat_axis=0, tiled=True)


def swap(x):
    return lax.ppermute(x, "c", [(0, 1), (1, 0)])


def around(x, d):
    return lax.ppermute(x, "z", [(i, (i + d) % 4) for i in range(4)])


def body(trainer_weights, hidden_in, norm_gain, routing, gate_weights):
    core, far, z = lax.axis_index("c"), lax.axis_index("xh"), lax.axis_index("z")
    tp = lax.axis_index(T)
    ids = jnp.stack([core, tp, 2 * tp + core, far, z, far * 8 + tp]).astype(jnp.int32)
    gain = lax.dynamic_index_in_dim(norm_gain.reshape(2, 4, 512), z, 1, keepdims=False)
    gain = gain.reshape(1, WIDTH)

    lines = lambda v: jnp.transpose(v, (0, 2, 1)).reshape(STEPS * TOPK, ROWS_DEV)
    pieces = first_rows(hidden_in, lines(routing), lines(gate_weights))
    pieces_far = lax.ppermute(pieces, "xh", [(0, 1), (1, 0)])

    near_out, diag_out = quantize_far(trainer_weights)
    gu_near = lax.ppermute(near_out, "xh", [(0, 1), (1, 0)])
    gu_diag = lax.ppermute(diag_out, ("xh", "c"), [(0, 3), (3, 0), (1, 2), (2, 1)])
    rows = spread(ids, pieces, pieces_far)
    rows = jnp.stack([rows[0]] + [around(rows[d], d) for d in (1, 2, 3)])
    mixed, near_out, diag_out = quantize_rest(ids, trainer_weights)
    here, rows_other = lax.optimization_barrier((hold(exchange(mixed, "c")), swap(rows)))
    x, stream, tab = prepare(ids, rows, rows_other, gain)

    near_out, diag_out, gu_near, x, stream, tab = lax.optimization_barrier(
        (near_out, diag_out, gu_near, x, stream, tab)
    )
    down_near = lax.ppermute(near_out, "xh", [(0, 1), (1, 0)])
    down_diag = lax.ppermute(diag_out, ("xh", "c"), [(0, 3), (3, 0), (1, 2), (2, 1)])

    x, before = [x], stream
    gu_weights, down_weights = [here, gu_near, gu_diag], [here, down_near, down_diag]
    for step in range(STEPS):
        part = gate_up(step, ids, x, tab, gu_weights)
        if step == 0:
            gu_near, gu_diag, *part = lax.optimization_barrier((gu_near, gu_diag, *part))
            gu_weights = [gate_up_side(ids, here, gu_near, gu_diag)]
        part = [part[0]] + [around(part[d], d) for d in (1, 2, 3)]
        act = activate(step == 0, part)
        acts = [act] + [around(act, d) for d in (1, 2, 3)]
        send, ys = down(step, ids, acts, tab, down_weights)
        if step == 0:
            send, down_near, down_diag = lax.optimization_barrier((send, down_near, down_diag))
            down_weights = [down_side(ids, here, down_near, down_diag)]
        sums = exchange(pair(kept(step, ids, ys, tab), swap(send)).reshape(16, 8, WIDTH), XT)
        if step < STEPS - 1:
            stream, rows = residual(sums, stream, gain)
            rows = exchange(rows, XT).reshape(128, EXT)
            x = [rows, swap(rows)]
        else:
            change = last(sums, stream, before)

    turn = [(a * 8 + t, ((t // 2 - a) % 4) * 8 + t) for a in range(4) for t in range(8)]
    mine = lax.ppermute(change, ("z", "xl", "y"), turn)
    whole = exchange(jnp.broadcast_to(mine[None], (8, 8, WIDTH)), T)
    return place_rows(ids, whole, hidden_in)


def solution(mesh):
    fine = Mesh(mesh.devices.reshape(2, 4, 2, 2, 4), ALL)
    fsdp, tp = ("xh", "z", "c"), ("xl", "y")
    in_specs = (
        P(tp, None, None, fsdp),
        P(fsdp, None),
        P(),
        P(None, fsdp, None),
        P(None, fsdp, None),
    )
    return jax.shard_map(
        body, mesh=fine, in_specs=in_specs, out_specs=P(fsdp, None), check_vma=False
    )
```

```python
import jax
import jax.numpy as jnp
from jax import lax
from jax.experimental import pallas as pl
from jax.experimental.pallas import tpu as pltpu
from jax.sharding import Mesh, PartitionSpec as P

D = 4096
FF = 1536
TOPK = 8
EXPERTS = 16
QB = 128
STEPS = 4
CAP = 11
ROWS_DEV = 16
ROWS = 256
SLOTS = 16 * CAP
UNIT_HALF = 768
WIDTH = 1024
HALF = 256
UNITS = 192
PAY = 184
EXT = 1152
FIRST = 1280

XZ = ("xh", "z")
XT = ("xh", "xl", "y")
T = ("xl", "y")
ALL = ("xh", "z", "c", "xl", "y")

norm_eps = 1e-06
scale_eps = 1e-06
code_limit = 448.0
smallest_normal = 0.015625
f32 = jnp.float32
bf16 = jnp.bfloat16

NN = (((1,), (0,)), ((), ()))
NT = (((1,), (1,)), ((), ()))


def dot(a, b, dims=NN):
    return lax.dot_general(a, b, dims, preferred_element_type=f32)


def busy(us, moved=0):
    return pl.CostEstimate(flops=int(us * 1.15e9), bytes_accessed=moved, transcendentals=0)


def split3(v):
    hi = v.astype(bf16)
    rest = v - hi.astype(f32)
    mid = rest.astype(bf16)
    low = (rest - mid.astype(f32)).astype(bf16)
    return hi, mid, low


def float_code(v):
    big = v * 1048577.0
    fine = big - (big - v)
    coarse = (v + 24576.0) - 24576.0
    return jnp.where(jnp.abs(v) < smallest_normal, coarse, fine)


def quant_block(tile):
    top = jnp.max(jnp.abs(tile), axis=0, keepdims=True).astype(f32)
    top = jnp.max(top, axis=1, keepdims=True) + scale_eps
    tile = tile.astype(f32)
    scale = top / code_limit
    return (float_code(tile * (1.0 / scale)) * scale).astype(bf16)


def quant_gate_up(src, out_ref, group):
    for m in range(2):
        for q in range(3):
            for h in range(2):
                cols = slice(h * QB, (h + 1) * QB)
                back = quant_block(src[m, q * QB : (q + 1) * QB, cols])
                for g in range(2):
                    unit = q * 2 + g
                    j, part = unit // 3, unit % 3
                    if m == 0:
                        to = part * 64
                    elif part < 2:
                        to = 256 + part * 64
                    else:
                        to = 192
                    to = group * 768 + j * 384 + to
                    out_ref[to : to + 64, cols] = back[g * 64 : g * 64 + 64]


def quant_down(src, out_ref, at, blocks):
    for q in range(blocks):
        for h in range(2):
            cols = slice(h * QB, (h + 1) * QB)
            back = quant_block(src[q * QB : (q + 1) * QB, cols])
            out_ref[at + q * QB : at + (q + 1) * QB, cols] = back


def quant_far_kernel(w_ref, near_ref, diag_ref, buf, sem):
    core, half = lax.axis_index("c"), 1 - lax.axis_index("xh")
    copies = []
    for p in range(2):
        for g in range(2):
            expert = core if p == 0 else 1 - core
            at = pl.multiple_of(half * UNIT_HALF + g * 384, 128)
            src = w_ref.at[expert, pl.ds(0, 2), pl.ds(at, 384), :]
            copies.append(pltpu.make_async_copy(src, buf.at[p * 2 + g], sem.at[p * 2 + g]))
    for copy in copies:
        copy.start()
    for p in range(2):
        for g in range(2):
            copies[p * 2 + g].wait()
            quant_gate_up(buf.at[p * 2 + g], diag_ref if p else near_ref, g)


def quantize_far(w):
    out = jax.ShapeDtypeStruct((2 * UNIT_HALF, HALF), bf16)
    return pl.pallas_call(
        quant_far_kernel,
        in_specs=[pl.BlockSpec(memory_space=pltpu.HBM)],
        out_shape=[out, out],
        scratch_shapes=[pltpu.VMEM((4, 2, 384, HALF), bf16), pltpu.SemaphoreType.DMA((4,))],
        compiler_params=pltpu.CompilerParams(vmem_limit_bytes=60 << 20),
        name="quantize_far",
    )(w)


def quant_rest_kernel(
    ids_ref, w_ref, pair_ref, near_ref, diag_ref, buf, sem, down_buf, down_sem
):
    core, half = ids_ref[0], ids_ref[3]
    copies = []
    for p in range(2):
        expert = core if p == 0 else 1 - core
        for g in range(2):
            at = pl.multiple_of(half * UNIT_HALF + g * 384, 128)
            src = w_ref.at[expert, :, pl.ds(at, 384), :]
            copies.append(pltpu.make_async_copy(src, buf.at[p * 2 + g], sem.at[p * 2 + g]))
    down_copies = []
    for p in range(2):
        expert = core if p == 0 else 1 - core
        at = pl.multiple_of((1 - half) * UNIT_HALF, 128)
        src = w_ref.at[expert, 2, pl.ds(at, UNIT_HALF), :]
        down_copies.append(pltpu.make_async_copy(src, down_buf.at[p], down_sem.at[p]))
    for copy in copies + down_copies:
        copy.start()
    for p in range(2):
        out_ref = pair_ref.at[1 - core if p else core]
        for g in range(2):
            copies[p * 2 + g].wait()
            quant_gate_up(buf.at[p * 2 + g], out_ref, g)
            quant_down(buf.at[p * 2 + g, 2], out_ref, 2 * UNIT_HALF + g * 384, 3)
    for p in range(2):
        down_copies[p].wait()
        quant_down(down_buf.at[p], diag_ref if p else near_ref, 0, 6)


def keep_kernel(mixed_ref, out_ref):
    out_ref[...] = mixed_ref[...]


def hold(mixed):
    return pl.pallas_call(
        keep_kernel,
        out_shape=jax.ShapeDtypeStruct(mixed.shape, bf16),
        compiler_params=pltpu.CompilerParams(vmem_limit_bytes=12 << 20),
        name="hold",
    )(mixed)


def quantize_rest(ids, w):
    whole = jax.ShapeDtypeStruct((2, 3 * UNIT_HALF, HALF), bf16)
    third = jax.ShapeDtypeStruct((UNIT_HALF, HALF), bf16)
    return pl.pallas_call(
        quant_rest_kernel,
        in_specs=[
            pl.BlockSpec(memory_space=pltpu.SMEM),
            pl.BlockSpec(memory_space=pltpu.HBM),
        ],
        out_shape=[whole, third, third],
        scratch_shapes=[
            pltpu.VMEM((4, 3, 384, HALF), bf16),
            pltpu.SemaphoreType.DMA((4,)),
            pltpu.VMEM((2, UNIT_HALF, HALF), bf16),
            pltpu.SemaphoreType.DMA((2,)),
        ],
        compiler_params=pltpu.CompilerParams(vmem_limit_bytes=60 << 20),
        name="quantize_rest",
    )(ids, w)


def side_by_side(refs, ids_ref, out_ref, put):
    core, half = ids_ref[0], ids_ref[3]
    far = 1 - half
    at = [half * 2 + core, half * 2 + 1 - core, far * 2 + core, far * 2 + 1 - core]
    for ref, b in zip(refs, at):
        put(ref, out_ref, pl.ds(pl.multiple_of(b * HALF, HALF), HALF))


def gate_up_side_kernel(ids_ref, here_ref, near_ref, diag_ref, out_ref):
    core = ids_ref[0]

    def put(ref, out_ref, cols):
        out_ref[:, cols] = ref[: 2 * UNIT_HALF, :]

    refs = [here_ref.at[core], here_ref.at[1 - core], near_ref, diag_ref]
    side_by_side(refs, ids_ref, out_ref, put)


def gate_up_side(ids, here, near, diag):
    return pl.pallas_call(
        gate_up_side_kernel,
        in_specs=[pl.BlockSpec(memory_space=pltpu.SMEM)] + [pl.BlockSpec()] * 3,
        out_shape=jax.ShapeDtypeStruct((2 * UNIT_HALF, WIDTH), bf16),
        compiler_params=pltpu.CompilerParams(vmem_limit_bytes=12 << 20),
        name="gate_up_side",
    )(ids, here, near, diag)


def down_side_kernel(ids_ref, here_ref, near_ref, diag_ref, out_ref):
    core = ids_ref[0]

    def put(ref, out_ref, cols):
        for j in range(4):
            out_ref[j * HALF : j * HALF + UNITS, cols] = ref[j * UNITS : (j + 1) * UNITS, :]
            out_ref[j * HALF + UNITS : (j + 1) * HALF, cols] = ref[
                j * UNITS + 128 : (j + 1) * UNITS, :
            ]

    rows = pl.ds(2 * UNIT_HALF, UNIT_HALF)
    refs = [here_ref.at[core, rows], here_ref.at[1 - core, rows], near_ref, diag_ref]
    side_by_side(refs, ids_ref, out_ref, put)


def down_side(ids, here, near, diag):
    return pl.pallas_call(
        down_side_kernel,
        in_specs=[pl.BlockSpec(memory_space=pltpu.SMEM)] + [pl.BlockSpec()] * 3,
        out_shape=jax.ShapeDtypeStruct((4 * HALF, WIDTH), bf16),
        compiler_params=pltpu.CompilerParams(vmem_limit_bytes=12 << 20),
        name="down_side",
    )(ids, here, near, diag)


def first_kernel(*refs):
    sources, (out_ref, table), held, sem = refs[:3], refs[3:5], refs[5:8], refs[8]
    copies = [pltpu.make_async_copy(a, b, sem.at[i]) for i, (a, b) in enumerate(zip(sources, held))]
    for copy in copies:
        copy.start()
    for copy in copies:
        copy.wait()
    hidden_ref, routing_ref, gates_ref = held
    hidden = hidden_ref[...].astype(f32)
    mean = jnp.sum(hidden * hidden, axis=1, keepdims=True) * (1.0 / D)
    hi, mid, low = split3(lax.rsqrt(mean + norm_eps))
    lane = lax.broadcasted_iota(jnp.int32, (ROWS_DEV, 128), 1)
    rs = jnp.where(
        lane == 0,
        hi.astype(f32),
        jnp.where(lane == 1, mid.astype(f32), jnp.where(lane == 2, low.astype(f32), 0.0)),
    ).astype(bf16)
    table[...] = jnp.zeros((128, 128), f32)
    table[0:32, :ROWS_DEV] = routing_ref[...].astype(f32)
    for i, part in enumerate(split3(gates_ref[...])):
        table[32 + 32 * i : 64 + 32 * i, :ROWS_DEV] = part.astype(f32)
    named = table[...].T[:ROWS_DEV].astype(bf16)
    for z in range(4):
        for half in range(2):
            at = half * 2048 + z * 512
            out_ref[z, :, half * 512 : half * 512 + 512] = hidden_ref[:, at : at + 512]
        out_ref[z, :, WIDTH : WIDTH + 128] = named
        out_ref[z, :, WIDTH + 128 :] = rs


def first_rows(hidden, routing, gates):
    return pl.pallas_call(
        first_kernel,
        in_specs=[pl.BlockSpec(memory_space=pltpu.HBM)] * 3,
        out_shape=jax.ShapeDtypeStruct((4, ROWS_DEV, FIRST), bf16),
        scratch_shapes=[
            pltpu.VMEM((128, 128), f32),
            pltpu.VMEM((ROWS_DEV, D), bf16),
            pltpu.VMEM((STEPS * TOPK, ROWS_DEV), jnp.int32),
            pltpu.VMEM((STEPS * TOPK, ROWS_DEV), f32),
            pltpu.SemaphoreType.DMA((3,)),
        ],
        compiler_params=pltpu.CompilerParams(vmem_limit_bytes=60 << 20),
        name="first_rows",
    )(hidden, routing, gates)


def spread_kernel(ids_ref, own_ref, far_ref, *out_refs):
    half, z = ids_ref[3], ids_ref[4]
    for d in range(4):
        at = (z + d) % 4
        out_refs[d][half] = own_ref[at]
        out_refs[d][1 - half] = far_ref[at]


def spread(ids, own, far):
    return pl.pallas_call(
        spread_kernel,
        in_specs=[pl.BlockSpec(memory_space=pltpu.SMEM)] + [pl.BlockSpec()] * 2,
        out_shape=[jax.ShapeDtypeStruct((2, ROWS_DEV, FIRST), bf16)] * 4,
        compiler_params=pltpu.CompilerParams(vmem_limit_bytes=4 << 20),
        name="spread",
    )(ids, own, far)


def prepare_kernel(ids_ref, own_ref, other_ref, gain_ref, x_ref, stream_ref, tab_ref, rows, tab):
    core, tp, expert, half, z = [ids_ref[i] for i in range(5)]
    for d in range(4):
        for far in range(2):
            at = (far * 4 + (z - d + 4) % 4) * 16
            rows[pl.ds(pl.multiple_of(core * 128 + at, 16), 16), :] = own_ref[d, far]
            rows[pl.ds(pl.multiple_of((1 - core) * 128 + at, 16), 16), :] = other_ref[d, far]
    named = rows[:, WIDTH : WIDTH + 128].astype(f32)
    gates = pltpu.roll(named, 96, 1) + pltpu.roll(named, 64, 1) + pltpu.roll(named, 32, 1)
    lane = lax.broadcasted_iota(jnp.int32, (ROWS, 128), 1)
    match = jnp.where((named == expert.astype(f32)) & (lane < 32), 1.0, 0.0)
    weighted = match * gates
    group = lane // TOPK
    mask = jnp.zeros((ROWS, 128), f32)
    weight = jnp.zeros((ROWS, 128), f32)
    for s in range(STEPS):
        here = jnp.sum(jnp.where(group == s, match, 0.0), axis=1, keepdims=True)
        gate = jnp.sum(jnp.where(group == s, weighted, 0.0), axis=1, keepdims=True)
        mask = jnp.where(lane == s, here, mask)
        weight = jnp.where(lane == s, gate, weight)
    r0 = lax.broadcasted_iota(jnp.int32, (ROWS, ROWS), 0)
    r1 = lax.broadcasted_iota(jnp.int32, (ROWS, ROWS), 1)
    before = jnp.where(r1 < r0, 1.0, 0.0).astype(bf16)
    place = jnp.where(mask > 0.0, dot(before, mask.astype(bf16)), -1.0)
    tab[...] = jnp.where(lane < 64, weight, pltpu.roll(place, 64, 1))
    for c in range(2):
        for far in range(2):
            for u in range(4):
                at = pl.multiple_of(c * 128 + far * 64 + ((u - z + 4) % 4) * 16, 16)
                to = slice(c * 128 + far * 64 + u * 16, c * 128 + far * 64 + u * 16 + 16)
                block = rows[pl.ds(at, 16), :].astype(f32)
                rs = jnp.sum(block[:, WIDTH + 128 :], axis=1, keepdims=True)
                x_ref[to, :] = (block[:, :WIDTH] * rs * gain_ref[...]).astype(bf16)
                tab_ref[to, :] = tab[pl.ds(at, 16), :]
    at = core * 128 + half * 64 + ((tp // 2 - z + 4) % 4) * 16
    mine = rows[pl.ds(pl.multiple_of(at, 16), 16), :WIDTH].astype(f32)
    stream_ref[...] = jnp.where(tp % 2 == 0, mine[:8], mine[8:])


def prepare(ids, own, other, gain):
    return pl.pallas_call(
        prepare_kernel,
        in_specs=[pl.BlockSpec(memory_space=pltpu.SMEM)] + [pl.BlockSpec()] * 3,
        out_shape=[
            jax.ShapeDtypeStruct((ROWS, WIDTH), bf16),
            jax.ShapeDtypeStruct((8, WIDTH), f32),
            jax.ShapeDtypeStruct((ROWS, 128), f32),
        ],
        scratch_shapes=[pltpu.VMEM((ROWS, FIRST), bf16), pltpu.VMEM((ROWS, 128), f32)],
        compiler_params=pltpu.CompilerParams(vmem_limit_bytes=8 << 20),
        name="prepare",
    )(ids, own, other, gain)


def one_hot(tab_ref, step):
    slot = lax.broadcasted_iota(jnp.int32, (ROWS, ROWS), 1).astype(f32)
    return jnp.where(slot == tab_ref[:, 64 + step : 65 + step], 1.0, 0.0)


def block_at(ids_ref):
    core, half = ids_ref[0], ids_ref[3]
    far = 1 - half
    return [half * 2 + core, half * 2 + 1 - core, far * 2 + core, far * 2 + 1 - core]


def gate_up_kernel(step, ids_ref, *refs):
    core, z = ids_ref[0], ids_ref[4]
    first = step == 0
    if first:
        x_ref, *refs = refs
    else:
        own_ref, other_ref, *refs = refs
    tab_ref, *refs = refs
    if first:
        w_refs, p_refs, xs = refs[:3], refs[3:7], refs[7]
        w_refs = [w_refs[0].at[core], w_refs[0].at[1 - core], *w_refs[1:]]
    else:
        w_ref, p_refs, x_ref = refs[0], refs[1:5], refs[5]
        x_ref[pl.ds(pl.multiple_of(core * 128, 128), 128), :] = own_ref[...]
        x_ref[pl.ds(pl.multiple_of((1 - core) * 128, 128), 128), :] = other_ref[...]
    hot = one_hot(tab_ref, step)
    picked = dot(hot.T[:SLOTS].astype(bf16), x_ref[:, :WIDTH]).astype(bf16)
    if first:
        for b in range(4):
            xs[b] = picked[:, b * HALF : (b + 1) * HALF]
        tail = jnp.zeros((PAY - SLOTS, 384), bf16)
    else:
        squares = jnp.sum(x_ref[:, WIDTH:].astype(f32), axis=1, keepdims=True)
        line = jnp.sum(hot * squares, axis=0, keepdims=True)
        line = jnp.concatenate([line, jnp.zeros((1, 128), f32)], axis=1)
        hi, mid, low = split3(line)
        at = lax.broadcasted_iota(jnp.int32, (PAY - SLOTS, 384), 0)
        tail = jnp.where(
            at == 0,
            hi.astype(f32),
            jnp.where(at == 1, mid.astype(f32), jnp.where(at == 2, low.astype(f32), 0.0)),
        ).astype(bf16)
    ours = [xs[at] for at in block_at(ids_ref)] if first else None
    for d in range(4):
        at = pl.multiple_of(((z + d) % 4) * 384, 128)
        if first:
            part = dot(ours[0], w_refs[0][pl.ds(at, 384), :], NT)
            for b in range(1, 4):
                part = part + dot(ours[b], w_refs[b][pl.ds(at, 384), :], NT)
        else:
            part = dot(picked, w_ref[pl.ds(at, 384), :], NT)
        p_refs[d][:SLOTS, :] = part.astype(bf16)
        p_refs[d][SLOTS:, :] = tail


def gate_up(step, ids, x, tab, weights):
    first = step == 0
    scratch = pltpu.VMEM((4, SLOTS, HALF) if first else (ROWS, EXT), bf16)
    return pl.pallas_call(
        lambda *refs: gate_up_kernel(step, *refs),
        in_specs=[pl.BlockSpec(memory_space=pltpu.SMEM)] + [pl.BlockSpec()] * (len(x) + 1 + len(weights)),
        out_shape=[jax.ShapeDtypeStruct((PAY, 384), bf16)] * 4,
        scratch_shapes=[scratch],
        compiler_params=pltpu.CompilerParams(vmem_limit_bytes=10 << 20),
        cost_estimate=busy(2.2, 4600000),
        name="gate_up",
    )(ids, *x, tab, *weights)


def act_kernel(first, *refs):
    out_ref = refs[4]
    total = refs[0][...].astype(f32)
    for j in range(1, 4):
        total = total + refs[j][...].astype(f32)
    sums = total[:SLOTS]
    if not first:
        line = jnp.sum(total[SLOTS : SLOTS + 8, :HALF], axis=0, keepdims=True)
        rs_line = lax.rsqrt(line * (1.0 / D) + norm_eps)
        r0 = lax.broadcasted_iota(jnp.int32, (SLOTS, HALF), 0)
        r1 = lax.broadcasted_iota(jnp.int32, (SLOTS, HALF), 1)
        rs = jnp.sum(jnp.where(r0 == r1, rs_line, 0.0), axis=1, keepdims=True)
        sums = sums * rs
    t0, t1, t2 = sums[:, :128], sums[:, 128:256], sums[:, 256:]
    a0 = jax.nn.silu(t0) * t2
    a1 = jax.nn.silu(t1) * pltpu.roll(t1, 64, 1)
    half = SLOTS // 2
    lane = lax.broadcasted_iota(jnp.int32, (half, 128), 1)
    middle = jnp.where(lane < 64, a1[:half], pltpu.roll(a1[half:], 64, 1))
    out_ref[...] = jnp.concatenate([a0[:half], middle, a0[half:]], axis=1).astype(bf16)


def activate(first, p):
    return pl.pallas_call(
        lambda *refs: act_kernel(first, *refs),
        out_shape=jax.ShapeDtypeStruct((SLOTS // 2, 384), bf16),
        compiler_params=pltpu.CompilerParams(vmem_limit_bytes=8 << 20),
        cost_estimate=busy(0.3),
        name="activate",
    )(*p)


def down_kernel(step, ids_ref, *refs):
    core, z = ids_ref[0], ids_ref[4]
    first = step == 0
    a_refs, tab_ref, refs = refs[:4], refs[4], refs[5:]
    if first:
        w_refs = [refs[0].at[core], refs[0].at[1 - core], *refs[1:3]]
        send_ref, ys = refs[3:]
        sums = [jnp.zeros((SLOTS, HALF), f32)] * 4
    else:
        w_ref, send_ref, ys, acts = refs
    half = SLOTS // 2
    lane = lax.broadcasted_iota(jnp.int32, (half, 128), 1)
    for d in range(4):
        block = a_refs[d][...].astype(f32)
        middle = block[:, 128:256]
        low = jnp.concatenate([block[:, :128], jnp.where(lane < 64, middle, 0.0)], axis=1)
        high = jnp.concatenate([block[:, 256:], jnp.where(lane < 64, 0.0, middle)], axis=1)
        act = jnp.concatenate([low, high], axis=0).astype(bf16)
        source = (z - d + 4) % 4
        if not first:
            acts[:, pl.ds(pl.multiple_of(source * HALF, HALF), HALF)] = act
            continue
        for b in range(4):
            start = 2 * UNIT_HALF if b < 2 else 0
            at = pl.multiple_of(source * UNITS + start, 64)
            after = pl.multiple_of(source * UNITS + start + 128, 64)
            w = jnp.concatenate([w_refs[b][pl.ds(at, UNITS), :], w_refs[b][pl.ds(after, 64), :]], axis=0)
            sums[b] = sums[b] + dot(act, w)
    if first:
        for b, at in enumerate(block_at(ids_ref)):
            ys[at] = sums[b].astype(bf16)
        result = [ys[b] for b in range(4)]
    else:
        total = [dot(acts[...], w_ref[:, b * HALF : (b + 1) * HALF]) for b in range(4)]
        result = [t.astype(bf16) for t in total]
        for b in range(4):
            ys[b] = result[b]
    place_part(step, 1 - core, tab_ref, result, send_ref)


def place_part(step, part, tab_ref, result, out_ref):
    slot = lax.broadcasted_iota(jnp.int32, (128, HALF), 1).astype(f32)
    tab = tab_ref[pl.ds(pl.multiple_of(part * 128, 128), 128), :]
    hot = jnp.where(slot == tab[:, 64 + step : 65 + step], 1.0, 0.0)[:, :SLOTS].astype(bf16)
    for b in range(4):
        rows = dot(hot, result[b]) * tab[:, step : step + 1]
        out_ref[:, b * HALF : (b + 1) * HALF] = rows.astype(out_ref.dtype)


def kept_kernel(step, ids_ref, ys_ref, tab_ref, out_ref):
    place_part(step, ids_ref[0], tab_ref, [ys_ref[b] for b in range(4)], out_ref)


def kept(step, ids, ys, tab):
    return pl.pallas_call(
        lambda *refs: kept_kernel(step, *refs),
        in_specs=[pl.BlockSpec(memory_space=pltpu.SMEM)] + [pl.BlockSpec()] * 2,
        out_shape=jax.ShapeDtypeStruct((128, WIDTH), f32),
        compiler_params=pltpu.CompilerParams(vmem_limit_bytes=6 << 20),
        cost_estimate=busy(0.4),
        name="kept",
    )(ids, ys, tab)


def down(step, ids, acts, tab, weights):
    return pl.pallas_call(
        lambda *refs: down_kernel(step, *refs),
        in_specs=[pl.BlockSpec(memory_space=pltpu.SMEM)] + [pl.BlockSpec()] * (5 + len(weights)),
        out_shape=[
            jax.ShapeDtypeStruct((128, WIDTH), bf16),
            jax.ShapeDtypeStruct((4, SLOTS, HALF), bf16),
        ],
        scratch_shapes=[] if step == 0 else [pltpu.VMEM((SLOTS, WIDTH), bf16)],
        compiler_params=pltpu.CompilerParams(vmem_limit_bytes=10 << 20),
        cost_estimate=busy(1.9, 3000000),
        name="down",
    )(ids, *acts, tab, *weights)


def pair_kernel(keep_ref, other_ref, out_ref):
    out_ref[...] = (keep_ref[...] + other_ref[...].astype(f32)).astype(bf16)


def pair(keep, other):
    return pl.pallas_call(
        pair_kernel,
        out_shape=jax.ShapeDtypeStruct((128, WIDTH), bf16),
        compiler_params=pltpu.CompilerParams(vmem_limit_bytes=4 << 20),
        name="pair",
    )(keep, other)


def residual_kernel(p_ref, stream_ref, gain_ref, new_ref, x_ref):
    total = p_ref[0].astype(f32)
    for j in range(1, 16):
        total = total + p_ref[j].astype(f32)
    stream = stream_ref[...] + total
    new_ref[...] = stream
    hi, mid, low = split3(jnp.sum(stream * stream, axis=1, keepdims=True))
    lane = lax.broadcasted_iota(jnp.int32, (8, 128), 1)
    parts = jnp.where(
        lane == 0,
        hi.astype(f32),
        jnp.where(lane == 1, mid.astype(f32), jnp.where(lane == 2, low.astype(f32), 0.0)),
    )
    row = jnp.concatenate([stream * gain_ref[...], parts], axis=1).astype(bf16)
    for j in range(16):
        x_ref[j] = row


def residual(p, stream, gain):
    return pl.pallas_call(
        residual_kernel,
        out_shape=[
            jax.ShapeDtypeStruct((8, WIDTH), f32),
            jax.ShapeDtypeStruct((16, 8, EXT), bf16),
        ],
        compiler_params=pltpu.CompilerParams(vmem_limit_bytes=4 << 20),
        name="residual",
    )(p, stream, gain)


def last_kernel(p_ref, stream_ref, before_ref, change_ref):
    total = p_ref[0].astype(f32)
    for j in range(1, 16):
        total = total + p_ref[j].astype(f32)
    change_ref[...] = (stream_ref[...] - before_ref[...] + total).astype(bf16)


def last(p, stream, before):
    return pl.pallas_call(
        last_kernel,
        out_shape=jax.ShapeDtypeStruct((8, WIDTH), bf16),
        compiler_params=pltpu.CompilerParams(vmem_limit_bytes=4 << 20),
        name="last",
    )(p, stream, before)


def place_kernel(ids_ref, whole_ref, hidden_ref, out_ref):
    z = ids_ref[4]
    for a in range(4):
        for h in range(2):
            block = whole_ref[((a + z) % 4) * 2 + h].astype(f32)
            for far in range(2):
                to = far * 2048 + a * 512
                rows = hidden_ref[:, to : to + 512].astype(f32)[h * 8 : h * 8 + 8]
                out_ref[h * 8 : h * 8 + 8, to : to + 512] = (
                    rows + block[:, far * 512 : far * 512 + 512]
                )


def place_rows(ids, whole, hidden):
    return pl.pallas_call(
        place_kernel,
        in_specs=[pl.BlockSpec(memory_space=pltpu.SMEM), pl.BlockSpec(), pl.BlockSpec()],
        out_shape=jax.ShapeDtypeStruct((ROWS_DEV, D), f32),
        compiler_params=pltpu.CompilerParams(vmem_limit_bytes=4 << 20),
        name="place_rows",
    )(ids, whole, hidden)


def exchange(x, axes):
    return lax.all_to_all(x, axes, split_axis=0, concat_axis=0, tiled=True)


def swap(x):
    return lax.ppermute(x, "c", [(0, 1), (1, 0)])


def around(x, d):
    return lax.ppermute(x, "z", [(i, (i + d) % 4) for i in range(4)])


def body(trainer_weights, hidden_in, norm_gain, routing, gate_weights):
    core, far, z = lax.axis_index("c"), lax.axis_index("xh"), lax.axis_index("z")
    tp = lax.axis_index(T)
    ids = jnp.stack([core, tp, 2 * tp + core, far, z, far * 8 + tp]).astype(jnp.int32)
    gain = lax.dynamic_index_in_dim(norm_gain.reshape(2, 4, 512), z, 1, keepdims=False)
    gain = gain.reshape(1, WIDTH)

    lines = lambda v: jnp.transpose(v, (0, 2, 1)).reshape(STEPS * TOPK, ROWS_DEV)
    pieces = first_rows(hidden_in, lines(routing), lines(gate_weights))
    pieces_far = lax.ppermute(pieces, "xh", [(0, 1), (1, 0)])

    near_out, diag_out = quantize_far(trainer_weights)
    gu_near = lax.ppermute(near_out, "xh", [(0, 1), (1, 0)])
    gu_diag = lax.ppermute(diag_out, ("xh", "c"), [(0, 3), (3, 0), (1, 2), (2, 1)])
    rows = spread(ids, pieces, pieces_far)
    rows = jnp.stack([rows[0]] + [around(rows[d], d) for d in (1, 2, 3)])
    mixed, near_out, diag_out = quantize_rest(ids, trainer_weights)
    here, rows_other = lax.optimization_barrier((hold(exchange(mixed, "c")), swap(rows)))
    x, stream, tab = prepare(ids, rows, rows_other, gain)

    near_out, diag_out, gu_near, x, stream, tab = lax.optimization_barrier(
        (near_out, diag_out, gu_near, x, stream, tab)
    )
    down_near = lax.ppermute(near_out, "xh", [(0, 1), (1, 0)])
    down_diag = lax.ppermute(diag_out, ("xh", "c"), [(0, 3), (3, 0), (1, 2), (2, 1)])

    x, before = [x], stream
    gu_weights, down_weights = [here, gu_near, gu_diag], [here, down_near, down_diag]
    for step in range(STEPS):
        part = gate_up(step, ids, x, tab, gu_weights)
        if step == 0:
            gu_near, gu_diag, *part = lax.optimization_barrier((gu_near, gu_diag, *part))
            gu_weights = [gate_up_side(ids, here, gu_near, gu_diag)]
        part = [part[0]] + [around(part[d], d) for d in (1, 2, 3)]
        act = activate(step == 0, part)
        acts = [act] + [around(act, d) for d in (1, 2, 3)]
        send, ys = down(step, ids, acts, tab, down_weights)
        if step == 0:
            send, down_near, down_diag = lax.optimization_barrier((send, down_near, down_diag))
            down_weights = [down_side(ids, here, down_near, down_diag)]
        sums = exchange(pair(kept(step, ids, ys, tab), swap(send)).reshape(16, 8, WIDTH), XT)
        if step < STEPS - 1:
            stream, rows = residual(sums, stream, gain)
            rows = exchange(rows, XT).reshape(128, EXT)
            x = [rows, swap(rows)]
        else:
            change = last(sums, stream, before)

    turn = [(a * 8 + t, ((t // 2 - a) % 4) * 8 + t) for a in range(4) for t in range(8)]
    mine = lax.ppermute(change, ("z", "xl", "y"), turn)
    whole = exchange(jnp.broadcast_to(mine[None], (8, 8, WIDTH)), T)
    return place_rows(ids, whole, hidden_in)


def solution(mesh):
    fine = Mesh(mesh.devices.reshape(2, 4, 2, 2, 4), ALL)
    fsdp, tp = ("xh", "z", "c"), ("xl", "y")
    in_specs = (
        P(tp, None, None, fsdp),
        P(fsdp, None),
        P(),
        P(None, fsdp, None),
        P(None, fsdp, None),
    )
    return jax.shard_map(
        body, mesh=fine, in_specs=in_specs, out_specs=P(fsdp, None), check_vma=False
    )
```
